32 devices in a mesh: rep: 4 (over x, core), shard: 8 (over z, y).
Axes of the slice: x: 2, y: 2, z: 4, core: 2. Of those that a mesh axis runs over, the one named last changes fastest.
Arguments:
- tokens: bfloat16 [32768, 1024], P(('rep', 'shard')), may hold values from -6 to 6
- resets: int32 [32768], P(('rep', 'shard')), may hold values 0 or 1
- norm_gain: bfloat16 [1024], P('shard'), may hold values from 0.5 to 1.5
- in_weight: bfloat16 [1024, 4384], P('shard'), may hold values from -0.1875 to 0.1875
- conv_weight: bfloat16 [4, 2304], P(None, 'shard'), may hold values from -3 to 3
- conv_bias: bfloat16 [2304], P('shard'), may hold values from -0.5 to 0.5
- step_bias: bfloat16 [32], P('shard'), may hold values from -7 to -3
- decay_log: bfloat16 [32], P('shard'), may hold values from 0 to 2.5
- skip_gain: bfloat16 [32], P('shard'), may hold values from 0.5 to 1.5
- gate_gain: bfloat16 [2048], P('shard'), may hold values from 0.5 to 1.5
- out_weight: bfloat16 [2048, 1024], P('shard'), may hold values from -0.125 to 0.125
- cotangent: bfloat16 [32768, 1024], P(('rep', 'shard')), may hold values from -6 to 6
Outputs:
- output: bfloat16 [32768, 1024], P(('rep', 'shard'))
- input_grad: bfloat16 [32768, 1024], P(('rep', 'shard'))
- norm_gain_grad: float32 [1024], P('shard')
- in_weight_grad: float32 [1024, 4384], P('shard')
- conv_weight_grad: float32 [4, 2304], P(None, 'shard')
- conv_bias_grad: float32 [2304], P('shard')
- step_bias_grad: float32 [32], P('shard')
- decay_log_grad: float32 [32], P('shard')
- skip_gain_grad: float32 [32], P('shard')
- gate_gain_grad: float32 [2048], P('shard')
- out_weight_grad: float32 [2048, 1024], P('shard')
The draws below stay inside these ranges and needn't reach their ends.
Inputs may be any that keep to these rules, and one draw needn't show every extreme that they name: resets[t] = 1 starts a new document at position t of its sequence.
All inputs are finite; a program needn't handle non-finite values. No bound on the sum of `resets` on one device may be relied on, other than what follows from the above.
Results may differ from the reference program's by a relative error of at most 0.0082.
Values may be sent and summed in bfloat16 or wider, within the bound.
No kernel may reach another device: no remote copies, remote signals or barrier semaphores. Data moves between devices by JAX's collectives and lax.ppermute only.
A program may use at most 256 MiB of HBM per device.

```python
from functools import partial
import jax
import jax.numpy as jnp
from jax import lax

D = 1024
INNER = 2048
H = 32
K = 4
SPAN = 256
SEQ_LEN = 1024
XBC = 2304
PROJ = 4384
TOKENS = 32768


def place_ends(entries, stream_key, least, largest):
    longest = entries.shape.index(max(entries.shape))
    spots = []
    for shift in (0, 1):
        where = [jax.random.randint(jax.random.fold_in(stream_key, axis), (), 0, length) for axis, length in enumerate(entries.shape)]
        where[longest] = (where[longest] + shift) % entries.shape[longest]
        spots.append(tuple(where))
    return entries.at[spots[0]].set(least).at[spots[1]].set(largest)


def shard_levels(rng, extent, cuts, low, largest):
    gain = 1.0
    for dim, blocks in cuts:
        heights = jax.random.uniform(jax.random.fold_in(jax.random.fold_in(rng, 6), dim), (blocks,), jnp.float32, low / len(cuts), largest / len(cuts))
        gain = gain * jnp.repeat(jnp.exp(heights), extent[dim] // blocks).reshape((-1,) + (1,) * (len(extent) - 1 - dim))
    return gain


def centred(rng, dims, scale, most, split=(), dtype=jnp.bfloat16):
    loudness = shard_levels(rng, dims, split, -0.22, 0.18) if split else 1.0
    entries = jax.random.normal(rng, dims, jnp.float32) * scale * loudness
    return jnp.minimum(jnp.maximum(entries, -most), most).astype(dtype)


def setup_inputs(seed: int = 0) -> dict:
    arg_keys = jax.random.split(jax.random.key(seed), 13)
    tokens = centred(arg_keys[0], (TOKENS, D), 1.0, 6.0, ((0, 32),))
    resets = place_ends((jax.random.randint(arg_keys[1], (TOKENS,), 0, SEQ_LEN) < 4).astype(jnp.int32), jax.random.fold_in(arg_keys[1], 1), 0, 1)
    norm_gain = jnp.clip(1.0 + 0.1 * jax.random.normal(arg_keys[2], (D,), jnp.float32), 0.5, 1.5).astype(jnp.bfloat16)
    in_weight = centred(arg_keys[3], (D, PROJ), D ** -0.5, 0.1875, ((0, 8),))
    conv_weight = centred(arg_keys[4], (K, XBC), K ** -0.5, 3.0, ((1, 8),))
    conv_bias = jnp.clip(jax.random.uniform(arg_keys[5], (XBC,), jnp.float32, -0.5, 0.5) * shard_levels(arg_keys[5], (XBC,), ((0, 8),), -0.4, 0.0), -0.5, 0.5).astype(jnp.bfloat16)
    step_bias = jnp.clip(-7.0 + 4.0 * jax.random.uniform(arg_keys[6], (H,), jnp.float32) ** shard_levels(arg_keys[6], (H,), ((0, 8),), -0.2, 0.2), -7.0, -3.0).astype(jnp.bfloat16)
    decay_log = jnp.clip(2.5 * jax.random.uniform(arg_keys[7], (H,), jnp.float32) ** shard_levels(arg_keys[7], (H,), ((0, 8),), -0.2, 0.2), 0.0, 2.5).astype(jnp.bfloat16)
    skip_gain = jnp.clip(0.5 + 1.0 * jax.random.uniform(arg_keys[8], (H,), jnp.float32) ** shard_levels(arg_keys[8], (H,), ((0, 8),), -0.2, 0.2), 0.5, 1.5).astype(jnp.bfloat16)
    gate_gain = jnp.clip(1.0 + 0.1 * jax.random.normal(arg_keys[9], (INNER,), jnp.float32), 0.5, 1.5).astype(jnp.bfloat16)
    out_weight = centred(arg_keys[10], (INNER, D), INNER ** -0.5, 0.125, ((0, 8),))
    cotangent = centred(arg_keys[11], (TOKENS, D), 1.0, 6.0, ((0, 32),))
    return dict(tokens=tokens, resets=resets, norm_gain=norm_gain, in_weight=in_weight, conv_weight=conv_weight, conv_bias=conv_bias, step_bias=step_bias, decay_log=decay_log, skip_gain=skip_gain, gate_gain=gate_gain, out_weight=out_weight, cotangent=cotangent)


EPS = 1e-05

@jax.custom_vjp
def low(v):
    return lax.optimization_barrier(v.astype(jnp.bfloat16)).astype(jnp.float32)

@jax.custom_vjp
def low_back(v):
    return v

def low_keep(v):
    return (low(v), None)

def low_pass(kept, grad):
    return (grad,)

def back_keep(v):
    return (v, None)

def back_low(kept, grad):
    return (low(grad),)
low.defvjp(low_keep, low_pass)
low_back.defvjp(back_keep, back_low)

def causal_conv(inputs, segment, conv_weight, conv_bias):
    taps = conv_weight.shape[0]
    length = inputs.shape[0]
    total = conv_bias[None, :] + jnp.zeros_like(inputs)
    for offset in range(taps):
        behind = taps - 1 - offset
        moved = jnp.pad(inputs, ((behind, 0), (0, 0)))[:length]
        moved_seg = jnp.pad(segment, (behind, 0), constant_values=-1)[:length]
        same_doc = (moved_seg == segment).astype(jnp.float32)
        total = total + conv_weight[offset][None, :] * moved * same_doc[:, None]
    return total

def span_step(running, pieces):
    carried_state, last_seg = running
    x_block, b_block, c_block, rate_block, step_block, seg_block = pieces
    length = seg_block.shape[0]
    cumulative = jnp.cumsum(rate_block, axis=0)
    row_index = lax.broadcasted_iota(jnp.int32, (length, length), 0)
    col_index = lax.broadcasted_iota(jnp.int32, (length, length), 1)
    linked = ((row_index >= col_index) & (seg_block[:, None] == seg_block[None, :]))[:, :, None]
    spread = cumulative[:, None, :] - cumulative[None, :, :]
    decay_mask = jnp.where(linked, jnp.exp(jnp.where(linked, spread, 0.0)), 0.0)
    intersection = jnp.dot(c_block, b_block.T, precision=lax.Precision.HIGHEST)
    weights = intersection[:, :, None] * decay_mask * step_block[None, :, :]
    inside = jnp.einsum('tsh,shp->thp', weights, x_block, precision=lax.Precision.HIGHEST)
    carried = (seg_block == last_seg).astype(jnp.float32)
    entry_scale = jnp.exp(cumulative) * carried[:, None]
    from_state = jnp.einsum('tn,hpn->thp', c_block, carried_state, precision=lax.Precision.HIGHEST) * entry_scale[:, :, None]
    closing = (seg_block == seg_block[-1]).astype(jnp.float32)
    to_end = jnp.exp(cumulative[-1][None, :] - cumulative) * closing[:, None] * step_block
    keep_all = jnp.exp(cumulative[-1]) * (seg_block[-1] == last_seg).astype(jnp.float32)
    weighted_x = x_block * to_end[:, :, None]
    added = jnp.einsum('shp,sn->hpn', weighted_x, b_block, precision=lax.Precision.HIGHEST)
    new_state = carried_state * keep_all[:, None, None] + added
    return ((new_state, seg_block[-1]), inside + from_state)

def span_scan(x_all, b_all, c_all, rate_all, step_all, segment):
    length, head_count, head_width = x_all.shape
    block_count = length // SPAN

    def blocked(values):
        return values.reshape((block_count, SPAN) + values.shape[1:])
    pieces = (blocked(x_all), blocked(b_all), blocked(c_all), blocked(rate_all), blocked(step_all), blocked(segment))
    initial = (jnp.zeros((head_count, head_width, b_all.shape[1]), jnp.float32), jnp.array(-1, jnp.int32))
    last_state, outputs = lax.scan(jax.checkpoint(span_step), initial, pieces)
    return outputs.reshape(length, head_count, head_width)

def mixer(projected, conv_weight, conv_bias, step_bias, decay_log, skip_gain, gate_gain, segment):
    inner_width = gate_gain.shape[0]
    mixed_width = conv_bias.shape[0]
    state_width = (mixed_width - inner_width) // 2
    head_count = step_bias.shape[0]
    length = projected.shape[0]
    gate_part = projected[:, :inner_width]
    conv_in = projected[:, inner_width:inner_width + mixed_width]
    step_raw = projected[:, inner_width + mixed_width:]
    convolved = jax.nn.silu(causal_conv(conv_in, segment, conv_weight, conv_bias))
    values_x = convolved[:, :inner_width].reshape(length, head_count, inner_width // head_count)
    input_b = convolved[:, inner_width:inner_width + state_width]
    output_c = convolved[:, inner_width + state_width:]
    step_size = jax.nn.softplus(step_raw + step_bias[None, :])
    rates = -jnp.exp(decay_log)[None, :] * step_size
    scanned = span_scan(values_x, input_b, output_c, rates, step_size, segment)
    scanned = scanned + skip_gain[None, :, None] * values_x
    gated = scanned.reshape(length, inner_width) * jax.nn.silu(gate_part)
    return gated * lax.rsqrt(lax.optimization_barrier(jnp.mean(gated * gated, axis=-1, keepdims=True)) + EPS) * gate_gain[None, :]

def forward(inputs, norm_gain, in_weight, conv_weight, conv_bias, step_bias, decay_log, skip_gain, gate_gain, out_weight, segment):
    inv_rms = lax.rsqrt(lax.optimization_barrier(jnp.mean(inputs * inputs, axis=-1, keepdims=True)) + EPS)
    normed = low(inputs * inv_rms * norm_gain[None, :])
    projected = low_back(jnp.dot(normed, in_weight, precision=lax.Precision.HIGHEST))
    mixed_out = low(mixer(projected, conv_weight, conv_bias, step_bias, decay_log, skip_gain, gate_gain, segment))
    return inputs + jnp.dot(mixed_out, out_weight, precision=lax.Precision.HIGHEST)

def reference(tokens, resets, norm_gain, in_weight, conv_weight, conv_bias, step_bias, decay_log, skip_gain, gate_gain, out_weight, cotangent):
    params = tuple((value.astype(jnp.float32) for value in (norm_gain, in_weight, conv_weight, conv_bias, step_bias, decay_log, skip_gain, gate_gain, out_weight)))
    seq_count = tokens.shape[0] // SEQ_LEN
    inputs_all = tokens.astype(jnp.float32).reshape(seq_count, SEQ_LEN, tokens.shape[1])
    back_all = cotangent.astype(jnp.float32).reshape(seq_count, SEQ_LEN, tokens.shape[1])
    segments = jnp.cumsum(resets.reshape(seq_count, SEQ_LEN), axis=1).astype(jnp.int32)

    def one_sequence(totals, pieces):
        inputs, segment, back = pieces
        result, pull = jax.vjp(partial(forward, segment=segment), inputs, *params)
        grads = pull(back)
        summed = tuple((left + right for left, right in zip(totals, grads[1:])))
        return (summed, (result.astype(jnp.bfloat16), grads[0].astype(jnp.bfloat16)))
    zeros = tuple((jnp.zeros_like(value) for value in params))
    totals, (results, in_grads) = lax.scan(one_sequence, zeros, (inputs_all, segments, back_all))
    output = results.reshape(tokens.shape)
    input_grad = in_grads.reshape(tokens.shape)
    return (output, input_grad, totals[0], totals[1], totals[2], totals[3], totals[4], totals[5], totals[6], totals[7], totals[8])
```

```python
from functools import partial

import jax
import jax.numpy as jnp
import numpy as np
from jax import lax
from jax.experimental import pallas as pl
from jax.experimental.pallas import tpu as pltpu
from jax.sharding import PartitionSpec as P

EPS = 1e-05
SPAN = 128
LANES = 128
WIDTH = 64
BF = jnp.bfloat16
F32 = jnp.float32
HIGH = lax.Precision.HIGHEST


def mm(a, b):
    return jnp.dot(a, b, preferred_element_type=F32)


def mm_nt(a, b):
    return lax.dot_general(a, b, (((1,), (1,)), ((), ())), preferred_element_type=F32)


def split_lanes(v):
    lane = lax.broadcasted_iota(jnp.int32, v.shape, 1)
    high = v.astype(BF).astype(F32)
    return jnp.where(lane < 32, high, v - high).astype(BF)


def halves(v):
    high = v.astype(BF)
    return high, (v - high.astype(F32)).astype(BF)


def block_diag(v):
    lane = lax.broadcasted_iota(jnp.int32, v.shape, 1)
    zero = jnp.zeros_like(v)
    return jnp.concatenate([jnp.where(lane < WIDTH, v, zero), jnp.where(lane >= WIDTH, v, zero)], axis=0)


def softplus(v):
    return jnp.maximum(v, 0.0) + jnp.log1p(jnp.exp(-jnp.abs(v)))


def head_values(raw, col, hp_ref, ee_ref, a3_ref, at_ref, dtx_ref, esx_ref, tex_ref, keepx_ref):
    span = raw.shape[0]
    shifted = raw + hp_ref[0:1, :]
    dt = softplus(shifted)
    rates = hp_ref[1:2, :] * dt
    row = lax.broadcasted_iota(jnp.int32, (span, span), 0)
    column = lax.broadcasted_iota(jnp.int32, (span, span), 1)
    tri = jnp.where(row >= column, 1.0, 0.0).astype(F32)
    total = jnp.dot(tri, rates, precision=HIGH, preferred_element_type=F32)
    at_ref[...] = total.T
    for head in range(a3_ref.shape[0]):
        a3_ref[head] = jnp.broadcast_to(total[:, head : head + 1], a3_ref.shape[1:])
    last = total[span - 1 : span, :]
    ee = ee_ref[...]
    dtx_ref[...] = mm(split_lanes(dt), ee)
    esx_ref[...] = mm(split_lanes(jnp.exp(total) * col[:, 7:8]), ee)
    tex_ref[...] = mm(split_lanes(jnp.exp(last - total) * col[:, 8:9]), ee)
    keepx_ref[...] = mm(split_lanes(jnp.broadcast_to(jnp.exp(last) * col[0:1, 9:10], (8, LANES))), ee)
    return shifted, rates


def pair_decay(pair, a3_ref, at_ref):
    column = jnp.concatenate([a3_ref[2 * pair], a3_ref[2 * pair + 1]], axis=1)
    row = jnp.concatenate([at_ref[pl.ds(2 * pair, 1), :], at_ref[pl.ds(2 * pair + 1, 1), :]], axis=1)
    return column, row


def fwd_kernel(
    inner,
    xbc_ref, col_ref, row_ref, cw_ref, hp_ref, skip_ref, ee_ref,
    y_ref, pre_ref, sin_ref,
    buf, state, a3_ref, at_ref, dtx_ref, esx_ref, tex_ref, keepx_ref, g2_ref,
):
    span = y_ref.shape[0]
    mixed = pre_ref.shape[1]
    step = pl.program_id(0)

    @pl.when(step == 0)
    def _():
        buf[0:8, :] = jnp.zeros((8, mixed), F32)
        state[...] = jnp.zeros_like(state)

    @pl.when(step > 0)
    def _():
        buf[0:8, :] = buf[span : span + 8, :]

    buf[8 : 8 + span, :] = xbc_ref[:, :mixed]
    col = col_ref[...]
    head_values(
        xbc_ref[:, mixed : mixed + LANES], col, hp_ref, ee_ref, a3_ref, at_ref, dtx_ref, esx_ref, tex_ref, keepx_ref
    )
    same = [None] + [jnp.broadcast_to(col[:, k : k + 1], (span, LANES)) for k in (1, 2, 3)]

    def conv(lanes):
        total = cw_ref[4:5, lanes] + cw_ref[3:4, lanes] * buf[8 : 8 + span, lanes]
        for k in (1, 2, 3):
            total = total + cw_ref[3 - k : 4 - k, lanes] * (buf[8 - k : 8 - k + span, lanes] * same[k])
        pre_ref[:, lanes] = total
        return total * jax.nn.sigmoid(total)

    b_f = conv(slice(inner, inner + LANES))
    c_b = conv(slice(inner + LANES, inner + 2 * LANES)).astype(BF)
    b_b = b_f.astype(BF)
    b_t = b_f.T.astype(BF)
    t_index = lax.broadcasted_iota(jnp.int32, (span, span), 0)
    s_index = lax.broadcasted_iota(jnp.int32, (span, span), 1)
    linked = (t_index >= s_index) & (col[:, 0:1] == row_ref[0:1, :])
    inter = jnp.where(linked, mm_nt(c_b, b_b), 0.0)
    g2_ref[...] = jnp.concatenate([inter, inter], axis=1)

    def pair_step(pair, carry):
        lanes = pl.ds(pl.multiple_of(pair * LANES, LANES), LANES)
        x = conv(lanes)
        xd = x * dtx_ref[:, lanes]
        column, row = pair_decay(pair, a3_ref, at_ref)
        decay = jnp.exp(jnp.minimum(column - row, 0.0))
        inside = mm((g2_ref[...] * decay).astype(BF), block_diag(xd.astype(BF)))
        held = state[:, lanes]
        held_b = held.astype(BF)
        sin_ref[:, lanes] = held_b
        y_ref[:, lanes] = inside + mm(c_b, held_b) * esx_ref[:, lanes] + skip_ref[0:1, lanes] * x
        state[:, lanes] = held * keepx_ref[0:1, lanes] + mm(b_t, (xd * tex_ref[:, lanes]).astype(BF))
        return carry

    lax.fori_loop(0, inner // LANES, pair_step, 0, unroll=2)


def bwd_kernel(
    inner,
    xbc_ref, pre_ref, y_ref, gy_ref, sin_ref, col_ref, row_ref, cw_ref, hp_ref, skip_ref, ee_ref, rt_ref,
    gp_ref, cwg_ref, hpg_ref, skg_ref,
    grad, halo, gstate, a3_ref, at_ref, dtx_ref, esx_ref, tex_ref, keepx_ref, gt2_ref, ggt_ref, gb_ref, gc_ref, acc_ref, kv_ref,
):
    span = y_ref.shape[0]
    mixed = pre_ref.shape[1]
    step = pl.program_id(0)

    @pl.when(step == 0)
    def _():
        halo[...] = jnp.zeros_like(halo)
        gstate[...] = jnp.zeros_like(gstate)
        cwg_ref[...] = jnp.zeros_like(cwg_ref)
        hpg_ref[...] = jnp.zeros_like(hpg_ref)
        skg_ref[...] = jnp.zeros_like(skg_ref)

    col = col_ref[...]
    shifted, rates = head_values(
        xbc_ref[:, mixed : mixed + LANES], col, hp_ref, ee_ref, a3_ref, at_ref, dtx_ref, esx_ref, tex_ref, keepx_ref
    )
    ahead = [None] + [jnp.broadcast_to(col[:, 3 + k : 4 + k], (span, LANES)) for k in (1, 2, 3)]

    def conv_back(lanes, g):
        grad[0:span, lanes] = g
        grad[span : span + 8, lanes] = halo[:, lanes]
        halo[:, lanes] = g[0:8, :]
        xin = xbc_ref[:, lanes]
        back = cw_ref[3:4, lanes] * g
        cwg_ref[3:4, lanes] += jnp.sum(xin * g, axis=0, keepdims=True)
        cwg_ref[4:5, lanes] += jnp.sum(g, axis=0, keepdims=True)
        for k in (1, 2, 3):
            moved = grad[k : k + span, lanes] * ahead[k]
            back = back + cw_ref[3 - k : 4 - k, lanes] * moved
            cwg_ref[3 - k : 4 - k, lanes] += jnp.sum(xin * moved, axis=0, keepdims=True)
        gp_ref[:, lanes] = back.astype(BF)

    def act(lanes):
        pre = pre_ref[:, lanes]
        sig = jax.nn.sigmoid(pre)
        return pre * sig, sig * (1.0 + pre * (1.0 - sig))

    b_lanes, c_lanes = slice(inner, inner + LANES), slice(inner + LANES, inner + 2 * LANES)
    b_f, b_slope = act(b_lanes)
    c_f, c_slope = act(c_lanes)
    b_b, c_b = b_f.astype(BF), c_f.astype(BF)
    c_t = c_f.T.astype(BF)
    s_index = lax.broadcasted_iota(jnp.int32, (span, span), 0)
    t_index = lax.broadcasted_iota(jnp.int32, (span, span), 1)
    linked = (t_index >= s_index) & (col[:, 0:1] == row_ref[0:1, :])
    inter = jnp.where(linked, mm_nt(b_b, c_b), 0.0)
    gt2_ref[...] = jnp.concatenate([inter, inter], axis=1)
    ggt_ref[...] = jnp.zeros_like(ggt_ref)
    gb_ref[...] = jnp.zeros_like(gb_ref)
    gc_ref[...] = jnp.zeros_like(gc_ref)
    acc_ref[...] = jnp.zeros_like(acc_ref)

    def pair_step(pair, carry):
        lanes = pl.ds(pl.multiple_of(pair * LANES, LANES), LANES)
        x, slope = act(lanes)
        dtx, tex = dtx_ref[:, lanes], tex_ref[:, lanes]
        xd = x * dtx
        xd_b = xd.astype(BF)
        gy_b = gy_ref[:, lanes]
        gy = gy_b.astype(F32)
        diag = block_diag(gy_b)
        column, row = pair_decay(pair, a3_ref, at_ref)
        decay = jnp.exp(jnp.minimum(row - column, 0.0))
        linked_g = mm_nt(xd_b, diag) * decay
        ggt_ref[...] += linked_g[:, :span] + linked_g[:, span:]
        gx_in = mm((gt2_ref[...] * decay).astype(BF), diag)
        gs = gstate[:, lanes]
        gs_b = gs.astype(BF)
        gx_state = tex * mm(b_b, gs_b)
        gxd = gx_in + gx_state
        from_state = xd * gx_state
        skip = skip_ref[0:1, lanes]
        drift = gy * (y_ref[:, lanes] - skip * x) - xd_b.astype(F32) * gx_in - from_state
        parts = [halves(v) for v in (drift, from_state, x * gxd)]
        stacked = jnp.concatenate([jnp.concatenate(part, axis=1) for part in parts], axis=0)
        rt = rt_ref[lanes, :]
        acc_ref[...] += mm(stacked, jnp.concatenate([rt, rt], axis=0))
        skg_ref[0:1, lanes] += jnp.sum(gy * x, axis=0, keepdims=True)
        held_b = sin_ref[:, lanes]
        keepx = keepx_ref[0:1, lanes]
        kv_ref[0:1, lanes] = keepx * jnp.sum(held_b.astype(F32) * gs, axis=0, keepdims=True)
        scaled = (esx_ref[:, lanes] * gy).astype(BF)
        gc_ref[...] += mm_nt(scaled, held_b)
        gb_ref[...] += mm_nt((xd * tex).astype(BF), gs_b)
        gstate[:, lanes] = keepx * gs + mm(c_t, scaled)
        conv_back(lanes, (dtx * gxd + skip * gy) * slope)
        return carry

    kv_ref[...] = jnp.zeros_like(kv_ref)
    lax.fori_loop(0, inner // LANES, pair_step, 0, unroll=2)
    g_inter = jnp.where(linked, ggt_ref[...], 0.0)
    conv_back(b_lanes, (gb_ref[...] + mm(g_inter.astype(BF), c_b)) * b_slope)
    conv_back(c_lanes, (gc_ref[...] + mm(g_inter.T.astype(BF), b_b)) * c_slope)
    kv_high, kv_low = halves(kv_ref[...])
    rt = rt_ref[...]
    kept = mm(kv_high, rt) + mm(kv_low, rt)
    at_end = jnp.sum(acc_ref[span : 2 * span, :], axis=0, keepdims=True) + kept[0:1, :]
    tri = jnp.where(t_index >= s_index, 1.0, 0.0).astype(F32)
    g_rate = jnp.dot(tri, acc_ref[0:span, :], precision=HIGH, preferred_element_type=F32) + at_end
    g_raw = (acc_ref[2 * span : 3 * span, :] + hp_ref[1:2, :] * g_rate) * jax.nn.sigmoid(shifted)
    gp_ref[:, mixed : mixed + LANES] = g_raw.astype(BF)
    hpg_ref[0:1, :] += jnp.sum(g_raw, axis=0, keepdims=True)
    hpg_ref[1:2, :] += jnp.sum(rates * g_rate, axis=0, keepdims=True)


def gate_kernel(y_ref, z_ref, gm_ref, gain_ref, out_ref, gy_ref, gz_ref, gg_ref):
    rows, inner = y_ref.shape

    @pl.when(pl.program_id(0) == 0)
    def _():
        gg_ref[...] = jnp.zeros_like(gg_ref)

    pieces = [slice(k, k + LANES) for k in range(0, inner, LANES)]
    square = jnp.zeros((rows, LANES), F32)
    cross = jnp.zeros((rows, LANES), F32)
    for lanes in pieces:
        z = z_ref[:, lanes]
        gated = y_ref[:, lanes] * (z * jax.nn.sigmoid(z))
        square = square + gated * gated
        cross = cross + gated * (gm_ref[:, lanes] * gain_ref[0:1, lanes])
    inv = lax.rsqrt(jnp.sum(square, axis=1, keepdims=True) / inner + EPS)
    pull = inv * inv * inv * (jnp.sum(cross, axis=1, keepdims=True) / inner)
    for lanes in pieces:
        z, y, gm = z_ref[:, lanes], y_ref[:, lanes], gm_ref[:, lanes]
        sig = jax.nn.sigmoid(z)
        silu = z * sig
        gated = y * silu
        gain = gain_ref[0:1, lanes]
        unit = gated * inv
        out_ref[:, lanes] = (unit * gain).astype(BF)
        gg_ref[0:1, lanes] += jnp.sum(gm * unit, axis=0, keepdims=True)
        g_gated = inv * (gm * gain) - gated * pull
        gy_ref[:, lanes] = (g_gated * silu).astype(BF)
        gz_ref[:, lanes] = (g_gated * y * (sig * (1.0 + z * (1.0 - sig)))).astype(BF)


def full(shape):
    return pl.BlockSpec(shape, lambda i: (0,) * len(shape))


def onehots(inner):
    heads = inner // WIDTH
    owner = np.arange(inner) // WIDTH
    spread = np.zeros((LANES, inner), np.float32)
    spread[owner, np.arange(inner)] = 1
    spread[32 + owner, np.arange(inner)] = 1
    collect = np.zeros((inner, LANES), np.float32)
    collect[np.arange(inner), owner] = 1
    return jnp.asarray(spread, BF), jnp.asarray(collect, BF)


PARAMS = pltpu.CompilerParams(dimension_semantics=("arbitrary",), vmem_limit_bytes=52 * 2**20)


def common_scratch(inner):
    heads = inner // WIDTH
    return [
        pltpu.VMEM((heads, SPAN, LANES), F32),
        pltpu.VMEM((LANES, SPAN), F32),
        pltpu.VMEM((SPAN, inner), F32),
        pltpu.VMEM((SPAN, inner), F32),
        pltpu.VMEM((SPAN, inner), F32),
        pltpu.VMEM((8, inner), F32),
        pltpu.VMEM((SPAN, 2 * SPAN), F32),
    ]


def scan_forward(xbc, col, row, cw, hp, skip):
    length, mixed, inner = xbc.shape[0], cw.shape[1], skip.shape[1]
    spread, _ = onehots(inner)
    blocks = length // SPAN
    return pl.pallas_call(
        partial(fwd_kernel, inner),
        grid=(blocks,),
        in_specs=[
            pl.BlockSpec((SPAN, mixed + LANES), lambda i: (i, 0)),
            pl.BlockSpec((SPAN, 16), lambda i: (i, 0)),
            pl.BlockSpec((8, SPAN), lambda i: (0, i)),
            full((8, mixed)), full((8, LANES)), full((8, inner)), full((LANES, inner)),
        ],
        out_specs=[
            pl.BlockSpec((SPAN, inner), lambda i: (i, 0)),
            pl.BlockSpec((SPAN, mixed), lambda i: (i, 0)),
            pl.BlockSpec((LANES, inner), lambda i: (i, 0)),
        ],
        out_shape=[
            jax.ShapeDtypeStruct((length, inner), F32),
            jax.ShapeDtypeStruct((length, mixed), F32),
            jax.ShapeDtypeStruct((blocks * LANES, inner), BF),
        ],
        scratch_shapes=[pltpu.VMEM((SPAN + 8, mixed), F32), pltpu.VMEM((LANES, inner), F32)] + common_scratch(inner),
        compiler_params=PARAMS,
        cost_estimate=pl.CostEstimate(flops=6 * 10**9, bytes_accessed=3 * 10**7, transcendentals=10**7),
        name="scan_forward",
    )(xbc, col, row, cw, hp, skip, spread)


def scan_backward(xbc, pre, y, gy, sin, col, row, cw, hp, skip):
    length, mixed, inner = xbc.shape[0], cw.shape[1], skip.shape[1]
    spread, collect = onehots(inner)
    blocks = length // SPAN
    rev = lambda i: (blocks - 1 - i, 0)
    return pl.pallas_call(
        partial(bwd_kernel, inner),
        grid=(blocks,),
        in_specs=[
            pl.BlockSpec((SPAN, mixed + LANES), rev),
            pl.BlockSpec((SPAN, mixed), rev),
            pl.BlockSpec((SPAN, inner), rev),
            pl.BlockSpec((SPAN, inner), rev),
            pl.BlockSpec((LANES, inner), rev),
            pl.BlockSpec((SPAN, 16), rev),
            pl.BlockSpec((8, SPAN), lambda i: (0, blocks - 1 - i)),
            full((8, mixed)), full((8, LANES)), full((8, inner)), full((LANES, inner)), full((inner, LANES)),
        ],
        out_specs=[
            pl.BlockSpec((SPAN, mixed + LANES), rev),
            full((8, mixed)), full((8, LANES)), full((8, inner)),
        ],
        out_shape=[
            jax.ShapeDtypeStruct((length, mixed + LANES), BF),
            jax.ShapeDtypeStruct((8, mixed), F32),
            jax.ShapeDtypeStruct((8, LANES), F32),
            jax.ShapeDtypeStruct((8, inner), F32),
        ],
        scratch_shapes=[
            pltpu.VMEM((SPAN + 8, mixed), F32), pltpu.VMEM((8, mixed), F32), pltpu.VMEM((LANES, inner), F32),
        ] + common_scratch(inner) + [
            pltpu.VMEM((SPAN, SPAN), F32), pltpu.VMEM((SPAN, LANES), F32), pltpu.VMEM((SPAN, LANES), F32),
            pltpu.VMEM((3 * SPAN, LANES), F32), pltpu.VMEM((8, inner), F32),
        ],
        compiler_params=PARAMS,
        cost_estimate=pl.CostEstimate(flops=2 * 10**10, bytes_accessed=5 * 10**7, transcendentals=10**7),
        name="scan_backward",
    )(xbc, pre, y, gy, sin, col, row, cw, hp, skip, spread, collect)


def gate(y, z, gm, gain):
    length, inner = y.shape
    rows = 128
    block = lambda: pl.BlockSpec((rows, inner), lambda i: (i, 0))
    return pl.pallas_call(
        gate_kernel,
        grid=(length // rows,),
        in_specs=[block(), block(), block(), full((8, inner))],
        out_specs=[block(), block(), block(), full((8, inner))],
        out_shape=[jax.ShapeDtypeStruct((length, inner), BF)] * 3 + [jax.ShapeDtypeStruct((8, inner), F32)],
        compiler_params=PARAMS,
        cost_estimate=pl.CostEstimate(flops=10**8, bytes_accessed=4 * 10**7, transcendentals=4 * 10**6),
        name="gate",
    )(y, z, gm, gain)


def document_info(resets):
    length = resets.shape[0]
    segment = jnp.cumsum(resets).astype(jnp.int32)
    back = [jnp.pad(segment, (k, 0), constant_values=-1)[:length] == segment for k in (1, 2, 3)]
    ahead = [jnp.pad(segment, (0, k), constant_values=-1)[k:] == segment for k in (1, 2, 3)]
    last = segment.reshape(-1, SPAN)[:, -1]
    before = jnp.concatenate([jnp.full((1,), -1, jnp.int32), last[:-1]])
    last, before = jnp.repeat(last, SPAN), jnp.repeat(before, SPAN)
    columns = [segment] + back + ahead + [segment == before, segment == last, last == before]
    columns = columns + [jnp.zeros_like(segment)] * (16 - len(columns))
    col = jnp.stack([c.astype(F32) for c in columns], axis=1)
    row = jnp.broadcast_to(segment.astype(F32)[None, :], (8, length))
    return col, row


def rows8(*rows):
    width = rows[0].shape[-1]
    rows = [r.reshape(-1, width).astype(F32) for r in rows]
    have = sum(r.shape[0] for r in rows)
    return jnp.concatenate(rows + [jnp.zeros((8 - have, width), F32)], axis=0)


def pairs(size, flip):
    return [(i, i ^ flip) for i in range(size)]


def other_core(value, reps):
    return lax.ppermute(value, "rep", pairs(reps, 1))


def swap_halves(own, core, reps, axis):
    other = other_core(own, reps)
    first = core == 0
    return jnp.stack([jnp.where(first, own, other), jnp.where(first, other, own)], axis=axis)


def half_of(value, core, axis):
    pick = lambda k: lax.dynamic_index_in_dim(value, k, axis, keepdims=False)
    return pick(core), pick(1 - core)


def sum_cores(value, core, reps):
    mine, theirs = half_of(value, core, 1)
    return (mine.astype(F32) + other_core(theirs, reps).astype(F32)).astype(BF)


def sum_reps(value, reps):
    flip = 2
    while flip < reps:
        value = (value.astype(F32) + lax.ppermute(value, "rep", pairs(reps, flip)).astype(F32)).astype(BF)
        flip *= 2
    return value


def sum_all(value, reps, shards):
    for axis, size in (("rep", reps), ("shard", shards)):
        flip = 1
        while flip < size:
            value = value + lax.ppermute(value, axis, pairs(size, flip))
            flip *= 2
    return value


def on_device(reps, shards, *args):
    (tokens, resets, norm_gain, in_weight, conv_weight, conv_bias, step_bias, decay_log, skip_gain, gate_gain,
     out_weight, cotangent) = args
    rows, proj = in_weight.shape
    width = tokens.shape[1]
    inner = shards * gate_gain.shape[0]
    mixed = shards * conv_bias.shape[0]
    heads = shards * step_bias.shape[0]
    half = rows // 2
    core = lax.axis_index("rep") % 2
    member = lax.axis_index("shard")

    small_parts = (norm_gain, conv_weight, conv_bias, step_bias, decay_log, skip_gain, gate_gain)
    small = jnp.concatenate([v.reshape(-1) for v in small_parts])
    small = jnp.pad(small, (0, half * LANES - small.shape[0])).reshape(half, LANES)
    dt_in = in_weight[:, inner + mixed :]
    x_in = jnp.concatenate([in_weight[:, inner : inner + mixed]] + [dt_in] * (LANES // heads), axis=1)
    x_own = lax.dynamic_slice_in_dim(x_in, core * half, half, 0)
    x_all = lax.all_gather(jnp.concatenate([x_own, small], axis=1), "shard", axis=0)
    x_width = mixed + LANES
    w_x = swap_halves(x_all[:, :, :x_width], core, reps, 1).reshape(width, x_width)
    small_all = x_all[:, :, x_width:].reshape(shards, -1).astype(F32)
    z_own = lax.dynamic_slice_in_dim(in_weight[:, :inner], core * half, half, 0)
    out_own = lax.dynamic_slice_in_dim(out_weight, core * 2 * half, 2 * half, 0).reshape(half, inner)
    zo_all = lax.all_gather(jnp.concatenate([z_own, out_own], axis=0), "shard", axis=0)
    zo = swap_halves(zo_all, core, reps, 1)
    w_z = zo[:, :, :half].reshape(width, inner)
    w_out = zo[:, :, half:].reshape(inner, width)

    full_small, at = [], 0
    for part in small_parts:
        piece = small_all[:, at : at + part.size]
        at += part.size
        if part.ndim == 2:
            piece = jnp.moveaxis(piece.reshape(shards, part.shape[0], part.shape[1]), 0, 1).reshape(part.shape[0], -1)
        else:
            piece = piece.reshape(-1)
        full_small.append(piece)
    gain, cw, cb, sb, dl, sk, gg = full_small
    repeat = LANES // heads
    cw8 = rows8(cw, cb)
    hp8 = rows8(jnp.tile(sb, repeat), jnp.tile(-jnp.exp(dl), repeat))
    sk8 = rows8(jnp.repeat(sk, WIDTH))
    gg8 = rows8(gg)

    col, row = document_info(resets)
    inputs = tokens.astype(F32)
    inv_rms = lax.rsqrt(jnp.mean(inputs * inputs, axis=-1, keepdims=True) + EPS)
    normed = (inputs * inv_rms * gain[None, :]).astype(BF)
    xbc = mm(normed, w_x)
    y, pre, sin = scan_forward(xbc, col, row, cw8, hp8, sk8)
    z = mm(normed, w_z)
    g_mixed = mm_nt(cotangent, w_out)
    mixed_out, gy, gz, gg_grad = gate(y, z, g_mixed, gg8)

    def grad_of(left, right):
        return lax.dot_general(left, right, (((0,), (0,)), ((), ())), preferred_element_type=F32).astype(BF)

    out_grad = grad_of(mixed_out, cotangent).reshape(shards, 2, half, inner)
    z_grad = grad_of(normed, gz).reshape(shards, 2, half, inner)
    zo_sum = sum_cores(jnp.concatenate([z_grad, out_grad], axis=2), core, reps)
    zo_own = lax.psum_scatter(zo_sum, "shard", scatter_dimension=0)
    gp, cwg, hpg, skg = scan_backward(xbc, pre, y, gy, sin, col, row, cw8, hp8, sk8)
    x_grad = grad_of(normed, gp).reshape(shards, 2, half, x_width)
    x_own = lax.psum_scatter(sum_cores(x_grad, core, reps), "shard", scatter_dimension=0)
    output = (inputs + mm(mixed_out, w_out)).astype(BF)

    g_normed = mm_nt(gz, w_z) + mm_nt(gp, w_x)
    scaled = g_normed * gain[None, :]
    unit = inputs * inv_rms
    gain_grad = jnp.sum(g_normed * unit, axis=0)
    back = cotangent.astype(F32) + inv_rms * (scaled - unit * jnp.mean(scaled * unit, axis=-1, keepdims=True))
    input_grad = back.astype(BF)

    grads = (cwg[:4], cwg[4], hpg[0, :heads], hpg[1, :heads], skg[0].reshape(heads, WIDTH).sum(axis=1), gg_grad[0])
    split = lambda v: jnp.moveaxis(v.reshape(v.shape[:-1] + (shards, -1)), -2, 0).reshape(shards, -1)
    totals = sum_all(jnp.concatenate([split(v) for v in (gain_grad,) + grads], axis=1), reps, shards)
    own = lax.dynamic_index_in_dim(totals, member, 0, keepdims=False)
    small_grads, at = [], 0
    for part in small_parts:
        small_grads.append(own[at : at + part.size].reshape(part.shape))
        at += part.size

    both = jnp.concatenate([zo_own[:half], zo_own[half:], x_own], axis=1)
    both = swap_halves(sum_reps(both, reps), core, reps, 0).astype(F32)
    z_part = both[:, :, :inner].reshape(rows, inner)
    out_part = both[:, :, inner : 2 * inner].reshape(out_weight.shape)
    x_part = both[:, :, 2 * inner : 2 * inner + mixed + heads].reshape(rows, mixed + heads)
    in_grad = jnp.concatenate([z_part, x_part], axis=1)
    return (output, input_grad, small_grads[0], in_grad, *small_grads[1:], out_part)


def solution(mesh):
    by_token, by_shard = P(("rep", "shard"), None), P("shard")
    in_specs = (
        by_token, P(("rep", "shard")), by_shard, P("shard", None), P(None, "shard"), by_shard, by_shard, by_shard,
        by_shard, by_shard, P("shard", None), by_token,
    )
    out_specs = (
        by_token, by_token, by_shard, P("shard", None), P(None, "shard"), by_shard, by_shard, by_shard, by_shard,
        by_shard, P("shard", None),
    )
    return jax.shard_map(
        partial(on_device, mesh.shape["rep"], mesh.shape["shard"]),
        mesh=mesh,
        in_specs=in_specs,
        out_specs=out_specs,
        check_vma=False,
    )
```

```python
from functools import partial

import jax
import jax.numpy as jnp
import numpy as np
from jax import lax
from jax.experimental import pallas as pl
from jax.experimental.pallas import tpu as pltpu
from jax.sharding import PartitionSpec as P

EPS = 1e-05
SPAN = 128
LANES = 128
WIDTH = 64
BF = jnp.bfloat16
F32 = jnp.float32
HIGH = lax.Precision.HIGHEST


def mm(a, b):
    return jnp.dot(a, b, preferred_element_type=F32)


def mm_nt(a, b):
    return lax.dot_general(a, b, (((1,), (1,)), ((), ())), preferred_element_type=F32)


def split_lanes(v):
    lane = lax.broadcasted_iota(jnp.int32, v.shape, 1)
    high = v.astype(BF).astype(F32)
    return jnp.where(lane < 32, high, v - high).astype(BF)


def halves(v):
    high = v.astype(BF)
    return high, (v - high.astype(F32)).astype(BF)


def block_diag(v):
    lane = lax.broadcasted_iota(jnp.int32, v.shape, 1)
    zero = jnp.zeros_like(v)
    return jnp.concatenate([jnp.where(lane < WIDTH, v, zero), jnp.where(lane >= WIDTH, v, zero)], axis=0)


def softplus(v):
    return jnp.maximum(v, 0.0) + jnp.log1p(jnp.exp(-jnp.abs(v)))


def sigmoid(v):
    return 0.5 * jnp.tanh(0.5 * v) + 0.5


def repeat_heads(raw):
    lane = lax.broadcasted_iota(jnp.int32, raw.shape, 1)
    once = jnp.where(lane < 32, raw, 0.0)
    twice = once + pltpu.roll(once, 32, 1)
    return twice + pltpu.roll(twice, 64, 1)


def head_values(raw, col, hp_ref, ee_ref, at_ref, dtx_ref, esx_ref, tex_ref, keepx_ref):
    span = raw.shape[0]
    shifted = repeat_heads(raw) + hp_ref[0:1, :]
    dt = softplus(shifted)
    rates = hp_ref[1:2, :] * dt
    row = lax.broadcasted_iota(jnp.int32, (span, span), 0)
    column = lax.broadcasted_iota(jnp.int32, (span, span), 1)
    tri = jnp.where(row >= column, 1.0, 0.0).astype(F32)
    total = jnp.dot(tri, rates, precision=HIGH, preferred_element_type=F32)
    at_ref[...] = total.T
    last = total[span - 1 : span, :]
    ee = ee_ref[...]
    dtx_ref[...] = mm(split_lanes(dt), ee)
    esx_ref[...] = mm(split_lanes(jnp.exp(total) * col[:, 7:8]), ee)
    tex_ref[...] = mm(split_lanes(jnp.exp(last - total) * col[:, 8:9]), ee)
    keepx_ref[...] = mm(split_lanes(jnp.broadcast_to(jnp.exp(last) * col[0:1, 9:10], (8, LANES))), ee)
    return shifted, rates, total


def pair_decay(pair, total, at_ref):
    span = total.shape[0]
    heads = (2 * pair, 2 * pair + 1)
    column = jnp.concatenate([jnp.broadcast_to(total[:, h : h + 1], (span, span)) for h in heads], axis=1)
    row = jnp.concatenate([at_ref[h : h + 1, :] for h in heads], axis=1)
    return column, row


def fwd_kernel(
    inner,
    xbc_ref, col_ref, row_ref, cw_ref, hp_ref, skip_ref, ee_ref,
    y_ref, pre_ref, sin_ref,
    buf, state, at_ref, dtx_ref, esx_ref, tex_ref, keepx_ref, g2_ref,
):
    span = y_ref.shape[0]
    mixed = pre_ref.shape[1]
    step = pl.program_id(0)

    @pl.when(step == 0)
    def _():
        buf[0:8, :] = jnp.zeros((8, mixed), F32)
        state[...] = jnp.zeros_like(state)

    @pl.when(step > 0)
    def _():
        buf[0:8, :] = buf[span : span + 8, :]

    buf[8 : 8 + span, :] = xbc_ref[:, :mixed]
    col = col_ref[...]
    _, _, total = head_values(
        xbc_ref[:, mixed : mixed + LANES], col, hp_ref, ee_ref, at_ref, dtx_ref, esx_ref, tex_ref, keepx_ref
    )
    same = [None] + [jnp.broadcast_to(col[:, k : k + 1], (span, LANES)) for k in (1, 2, 3)]

    def conv(lanes):
        pre = cw_ref[4:5, lanes] + cw_ref[3:4, lanes] * buf[8 : 8 + span, lanes]
        for k in (1, 2, 3):
            pre = pre + cw_ref[3 - k : 4 - k, lanes] * (buf[8 - k : 8 - k + span, lanes] * same[k])
        pre_ref[:, lanes] = pre
        return pre * sigmoid(pre)

    b_f = conv(slice(inner, inner + LANES))
    c_b = conv(slice(inner + LANES, inner + 2 * LANES)).astype(BF)
    b_b = b_f.astype(BF)
    b_t = b_f.T.astype(BF)
    t_index = lax.broadcasted_iota(jnp.int32, (span, span), 0)
    s_index = lax.broadcasted_iota(jnp.int32, (span, span), 1)
    linked = (t_index >= s_index) & (col[:, 0:1] == row_ref[0:1, :])
    inter = jnp.where(linked, mm_nt(c_b, b_b), 0.0)
    g2_ref[...] = jnp.concatenate([inter, inter], axis=1)

    def pair_step(pair):
        lanes = slice(pair * LANES, (pair + 1) * LANES)
        x = conv(lanes)
        xd = x * dtx_ref[:, lanes]
        column, row = pair_decay(pair, total, at_ref)
        decay = jnp.exp(jnp.minimum(column - row, 0.0))
        inside = mm((g2_ref[...] * decay).astype(BF), block_diag(xd.astype(BF)))
        held = state[:, lanes]
        held_b = held.astype(BF)
        sin_ref[:, lanes] = held_b
        y_ref[:, lanes] = inside + mm(c_b, held_b) * esx_ref[:, lanes] + skip_ref[0:1, lanes] * x
        state[:, lanes] = held * keepx_ref[0:1, lanes] + mm(b_t, (xd * tex_ref[:, lanes]).astype(BF))

    for pair in range(inner // LANES):
        pair_step(pair)


def bwd_kernel(
    inner,
    xbc_ref, pre_ref, y_ref, gy_ref, sin_ref, col_ref, row_ref, cw_ref, hp_ref, skip_ref, ee_ref, rt_ref,
    gp_ref, cwg_ref, hpg_ref, skg_ref,
    grad, halo, gstate, at_ref, dtx_ref, esx_ref, tex_ref, keepx_ref, gt2_ref, ggt_ref, gb_ref, gc_ref, acc_ref, kv_ref,
):
    span = y_ref.shape[0]
    mixed = pre_ref.shape[1]
    step = pl.program_id(0)

    @pl.when(step == 0)
    def _():
        halo[...] = jnp.zeros_like(halo)
        gstate[...] = jnp.zeros_like(gstate)
        cwg_ref[...] = jnp.zeros_like(cwg_ref)
        hpg_ref[...] = jnp.zeros_like(hpg_ref)
        skg_ref[...] = jnp.zeros_like(skg_ref)

    col = col_ref[...]
    shifted, rates, total = head_values(
        xbc_ref[:, mixed : mixed + LANES], col, hp_ref, ee_ref, at_ref, dtx_ref, esx_ref, tex_ref, keepx_ref
    )
    ahead = [None] + [jnp.broadcast_to(col[:, 3 + k : 4 + k], (span, LANES)) for k in (1, 2, 3)]

    def conv_back(lanes, g):
        grad[0:span, lanes] = g
        grad[span : span + 8, lanes] = halo[:, lanes]
        halo[:, lanes] = g[0:8, :]
        xin = xbc_ref[:, lanes]
        back = cw_ref[3:4, lanes] * g
        cwg_ref[3:4, lanes] += jnp.sum(xin * g, axis=0, keepdims=True)
        cwg_ref[4:5, lanes] += jnp.sum(g, axis=0, keepdims=True)
        for k in (1, 2, 3):
            moved = grad[k : k + span, lanes] * ahead[k]
            back = back + cw_ref[3 - k : 4 - k, lanes] * moved
            cwg_ref[3 - k : 4 - k, lanes] += jnp.sum(xin * moved, axis=0, keepdims=True)
        gp_ref[:, lanes] = back.astype(BF)

    def act(lanes):
        pre = pre_ref[:, lanes]
        sig = sigmoid(pre)
        return pre * sig, sig * (1.0 + pre * (1.0 - sig))

    b_lanes, c_lanes = slice(inner, inner + LANES), slice(inner + LANES, inner + 2 * LANES)
    b_f, b_slope = act(b_lanes)
    c_f, c_slope = act(c_lanes)
    b_b, c_b = b_f.astype(BF), c_f.astype(BF)
    c_t = c_f.T.astype(BF)
    s_index = lax.broadcasted_iota(jnp.int32, (span, span), 0)
    t_index = lax.broadcasted_iota(jnp.int32, (span, span), 1)
    linked = (t_index >= s_index) & (col[:, 0:1] == row_ref[0:1, :])
    inter = jnp.where(linked, mm_nt(b_b, c_b), 0.0)
    gt2_ref[...] = jnp.concatenate([inter, inter], axis=1)
    ggt_ref[...] = jnp.zeros_like(ggt_ref)
    gb_ref[...] = jnp.zeros_like(gb_ref)
    gc_ref[...] = jnp.zeros_like(gc_ref)
    acc_ref[...] = jnp.zeros_like(acc_ref)

    def pair_step(pair):
        lanes = slice(pair * LANES, (pair + 1) * LANES)
        x, slope = act(lanes)
        dtx, tex = dtx_ref[:, lanes], tex_ref[:, lanes]
        xd = x * dtx
        xd_b = xd.astype(BF)
        gy_b = gy_ref[:, lanes]
        gy = gy_b.astype(F32)
        diag = block_diag(gy_b)
        column, row = pair_decay(pair, total, at_ref)
        decay = jnp.exp(jnp.minimum(row - column, 0.0))
        linked_g = mm_nt(xd_b, diag) * decay
        ggt_ref[...] += linked_g[:, :span] + linked_g[:, span:]
        gx_in = mm((gt2_ref[...] * decay).astype(BF), diag)
        gs = gstate[:, lanes]
        gs_b = gs.astype(BF)
        gx_state = tex * mm(b_b, gs_b)
        gxd = gx_in + gx_state
        from_state = xd * gx_state
        skip = skip_ref[0:1, lanes]
        drift = gy * (y_ref[:, lanes] - skip * x) - xd_b.astype(F32) * gx_in - from_state
        parts = [halves(v) for v in (drift, from_state, x * gxd)]
        stacked = jnp.concatenate([jnp.concatenate(part, axis=1) for part in parts], axis=0)
        rt = rt_ref[lanes, :]
        acc_ref[...] += mm(stacked, jnp.concatenate([rt, rt], axis=0))
        skg_ref[0:1, lanes] += jnp.sum(gy * x, axis=0, keepdims=True)
        held_b = sin_ref[:, lanes]
        keepx = keepx_ref[0:1, lanes]
        kv_ref[0:1, lanes] = keepx * jnp.sum(held_b.astype(F32) * gs, axis=0, keepdims=True)
        scaled = (esx_ref[:, lanes] * gy).astype(BF)
        gc_ref[...] += mm_nt(scaled, held_b)
        gb_ref[...] += mm_nt((xd * tex).astype(BF), gs_b)
        gstate[:, lanes] = keepx * gs + mm(c_t, scaled)
        conv_back(lanes, (dtx * gxd + skip * gy) * slope)

    kv_ref[...] = jnp.zeros_like(kv_ref)
    for pair in range(inner // LANES):
        pair_step(pair)
    g_inter = jnp.where(linked, ggt_ref[...], 0.0)
    conv_back(b_lanes, (gb_ref[...] + mm(g_inter.astype(BF), c_b)) * b_slope)
    conv_back(c_lanes, (gc_ref[...] + mm(g_inter.T.astype(BF), b_b)) * c_slope)
    kv_high, kv_low = halves(kv_ref[...])
    rt = rt_ref[...]
    kept = mm(kv_high, rt) + mm(kv_low, rt)
    at_end = jnp.sum(acc_ref[span : 2 * span, :], axis=0, keepdims=True) + kept[0:1, :]
    tri = jnp.where(t_index >= s_index, 1.0, 0.0).astype(F32)
    g_rate = jnp.dot(tri, acc_ref[0:span, :], precision=HIGH, preferred_element_type=F32) + at_end
    g_raw = (acc_ref[2 * span : 3 * span, :] + hp_ref[1:2, :] * g_rate) * sigmoid(shifted)
    gp_ref[:, mixed : mixed + LANES] = g_raw.astype(BF)
    hpg_ref[0:1, :] += jnp.sum(g_raw, axis=0, keepdims=True)
    hpg_ref[1:2, :] += jnp.sum(rates * g_rate, axis=0, keepdims=True)


def gate_kernel(y_ref, z_ref, gm_ref, gain_ref, out_ref, gy_ref, gz_ref, gg_ref):
    rows, inner = y_ref.shape

    @pl.when(pl.program_id(0) == 0)
    def _():
        gg_ref[...] = jnp.zeros_like(gg_ref)

    pieces = [slice(k, k + LANES) for k in range(0, inner, LANES)]
    square = jnp.zeros((rows, LANES), F32)
    cross = jnp.zeros((rows, LANES), F32)
    for lanes in pieces:
        z = z_ref[:, lanes]
        gated = y_ref[:, lanes] * (z * sigmoid(z))
        square = square + gated * gated
        cross = cross + gated * (gm_ref[:, lanes] * gain_ref[0:1, lanes])
    inv = lax.rsqrt(jnp.sum(square, axis=1, keepdims=True) / inner + EPS)
    pull = inv * inv * inv * (jnp.sum(cross, axis=1, keepdims=True) / inner)
    for lanes in pieces:
        z, y, gm = z_ref[:, lanes], y_ref[:, lanes], gm_ref[:, lanes]
        sig = sigmoid(z)
        silu = z * sig
        gated = y * silu
        gain = gain_ref[0:1, lanes]
        unit = gated * inv
        out_ref[:, lanes] = (unit * gain).astype(BF)
        gg_ref[0:1, lanes] += jnp.sum(gm * unit, axis=0, keepdims=True)
        g_gated = inv * (gm * gain) - gated * pull
        gy_ref[:, lanes] = (g_gated * silu).astype(BF)
        gz_ref[:, lanes] = (g_gated * y * (sig * (1.0 + z * (1.0 - sig)))).astype(BF)


def full(shape):
    return pl.BlockSpec(shape, lambda i: (0,) * len(shape))


def onehots(inner):
    heads = inner // WIDTH
    owner = np.arange(inner) // WIDTH
    spread = np.zeros((LANES, inner), np.float32)
    spread[owner, np.arange(inner)] = 1
    spread[32 + owner, np.arange(inner)] = 1
    collect = np.zeros((inner, LANES), np.float32)
    collect[np.arange(inner), owner] = 1
    return jnp.asarray(spread, BF), jnp.asarray(collect, BF)


PARAMS = pltpu.CompilerParams(dimension_semantics=("arbitrary",), vmem_limit_bytes=52 * 2**20)


def common_scratch(inner):
    return [
        pltpu.VMEM((LANES, SPAN), F32),
        pltpu.VMEM((SPAN, inner), F32),
        pltpu.VMEM((SPAN, inner), F32),
        pltpu.VMEM((SPAN, inner), F32),
        pltpu.VMEM((8, inner), F32),
        pltpu.VMEM((SPAN, 2 * SPAN), F32),
    ]


def scan_forward(xbc, col, row, cw, hp, skip):
    length, mixed, inner = xbc.shape[0], cw.shape[1], skip.shape[1]
    spread, _ = onehots(inner)
    blocks = length // SPAN
    return pl.pallas_call(
        partial(fwd_kernel, inner),
        grid=(blocks,),
        in_specs=[
            pl.BlockSpec((SPAN, mixed + LANES), lambda i: (i, 0)),
            pl.BlockSpec((SPAN, 16), lambda i: (i, 0)),
            pl.BlockSpec((8, SPAN), lambda i: (0, i)),
            full((8, mixed)), full((8, LANES)), full((8, inner)), full((LANES, inner)),
        ],
        out_specs=[
            pl.BlockSpec((SPAN, inner), lambda i: (i, 0)),
            pl.BlockSpec((SPAN, mixed), lambda i: (i, 0)),
            pl.BlockSpec((LANES, inner), lambda i: (i, 0)),
        ],
        out_shape=[
            jax.ShapeDtypeStruct((length, inner), F32),
            jax.ShapeDtypeStruct((length, mixed), F32),
            jax.ShapeDtypeStruct((blocks * LANES, inner), BF),
        ],
        scratch_shapes=[pltpu.VMEM((SPAN + 8, mixed), F32), pltpu.VMEM((LANES, inner), F32)] + common_scratch(inner),
        compiler_params=PARAMS,
        cost_estimate=pl.CostEstimate(flops=6 * 10**9, bytes_accessed=3 * 10**7, transcendentals=10**7),
        name="scan_forward",
    )(xbc, col, row, cw, hp, skip, spread)


def scan_backward(xbc, pre, y, gy, sin, col, row, cw, hp, skip):
    length, mixed, inner = xbc.shape[0], cw.shape[1], skip.shape[1]
    spread, collect = onehots(inner)
    blocks = length // SPAN
    rev = lambda i: (blocks - 1 - i, 0)
    return pl.pallas_call(
        partial(bwd_kernel, inner),
        grid=(blocks,),
        in_specs=[
            pl.BlockSpec((SPAN, mixed + LANES), rev),
            pl.BlockSpec((SPAN, mixed), rev),
            pl.BlockSpec((SPAN, inner), rev),
            pl.BlockSpec((SPAN, inner), rev),
            pl.BlockSpec((LANES, inner), rev),
            pl.BlockSpec((SPAN, 16), rev),
            pl.BlockSpec((8, SPAN), lambda i: (0, blocks - 1 - i)),
            full((8, mixed)), full((8, LANES)), full((8, inner)), full((LANES, inner)), full((inner, LANES)),
        ],
        out_specs=[
            pl.BlockSpec((SPAN, mixed + LANES), rev),
            full((8, mixed)), full((8, LANES)), full((8, inner)),
        ],
        out_shape=[
            jax.ShapeDtypeStruct((length, mixed + LANES), BF),
            jax.ShapeDtypeStruct((8, mixed), F32),
            jax.ShapeDtypeStruct((8, LANES), F32),
            jax.ShapeDtypeStruct((8, inner), F32),
        ],
        scratch_shapes=[
            pltpu.VMEM((SPAN + 8, mixed), F32), pltpu.VMEM((8, mixed), F32), pltpu.VMEM((LANES, inner), F32),
        ] + common_scratch(inner) + [
            pltpu.VMEM((SPAN, SPAN), F32), pltpu.VMEM((SPAN, LANES), F32), pltpu.VMEM((SPAN, LANES), F32),
            pltpu.VMEM((3 * SPAN, LANES), F32), pltpu.VMEM((8, inner), F32),
        ],
        compiler_params=PARAMS,
        cost_estimate=pl.CostEstimate(flops=2 * 10**10, bytes_accessed=5 * 10**7, transcendentals=10**7),
        name="scan_backward",
    )(xbc, pre, y, gy, sin, col, row, cw, hp, skip, spread, collect)


def gate(y, z, gm, gain):
    length, inner = y.shape
    rows = 128
    block = lambda: pl.BlockSpec((rows, inner), lambda i: (i, 0))
    return pl.pallas_call(
        gate_kernel,
        grid=(length // rows,),
        in_specs=[block(), block(), block(), full((8, inner))],
        out_specs=[block(), block(), block(), full((8, inner))],
        out_shape=[jax.ShapeDtypeStruct((length, inner), BF)] * 3 + [jax.ShapeDtypeStruct((8, inner), F32)],
        compiler_params=PARAMS,
        cost_estimate=pl.CostEstimate(flops=10**8, bytes_accessed=4 * 10**7, transcendentals=4 * 10**6),
        name="gate",
    )(y, z, gm, gain)


def document_info(resets):
    length = resets.shape[0]
    segment = jnp.cumsum(resets).astype(jnp.int32)
    back = [jnp.pad(segment, (k, 0), constant_values=-1)[:length] == segment for k in (1, 2, 3)]
    ahead = [jnp.pad(segment, (0, k), constant_values=-1)[k:] == segment for k in (1, 2, 3)]
    last = segment.reshape(-1, SPAN)[:, -1]
    before = jnp.concatenate([jnp.full((1,), -1, jnp.int32), last[:-1]])
    last, before = jnp.repeat(last, SPAN), jnp.repeat(before, SPAN)
    columns = [segment] + back + ahead + [segment == before, segment == last, last == before]
    columns = columns + [jnp.zeros_like(segment)] * (16 - len(columns))
    col = jnp.stack([c.astype(F32) for c in columns], axis=1)
    row = jnp.broadcast_to(segment.astype(F32)[None, :], (8, length))
    return col, row


def rows8(*rows):
    width = rows[0].shape[-1]
    rows = [r.reshape(-1, width).astype(F32) for r in rows]
    have = sum(r.shape[0] for r in rows)
    return jnp.concatenate(rows + [jnp.zeros((8 - have, width), F32)], axis=0)


def pairs(size, flip):
    return [(i, i ^ flip) for i in range(size)]


def other_core(value, reps):
    return lax.ppermute(value, "rep", pairs(reps, 1))


def swap_halves(own, core, reps, axis):
    other = other_core(own, reps)
    first = core == 0
    return jnp.stack([jnp.where(first, own, other), jnp.where(first, other, own)], axis=axis)


def half_of(value, core, axis):
    pick = lambda k: lax.dynamic_index_in_dim(value, k, axis, keepdims=False)
    return pick(core), pick(1 - core)


def sum_cores(value, core, reps):
    mine, theirs = half_of(value, core, 1)
    return (mine.astype(F32) + other_core(theirs, reps).astype(F32)).astype(BF)


def sum_reps(value, reps):
    flip = 2
    while flip < reps:
        value = (value.astype(F32) + lax.ppermute(value, "rep", pairs(reps, flip)).astype(F32)).astype(BF)
        flip *= 2
    return value


def sum_all(value, reps, shards):
    for axis, size in (("rep", reps), ("shard", shards)):
        flip = 1
        while flip < size:
            value = value + lax.ppermute(value, axis, pairs(size, flip))
            flip *= 2
    return value


def add(*values):
    return sum(v.astype(F32) for v in values).astype(BF)


def gather_shards(value, shards):
    if shards != 8:
        return lax.all_gather(value, "shard", axis=0), value
    member = lax.axis_index("shard")
    z, y = member // 2, member % 2
    got = [(0, value)]
    for k in (1, 3, 2):
        moves = [(i, (i + 2 * k) % 8) for i in range(8)]
        got.append((k, lax.ppermute(value, "shard", moves)))
    out = jnp.zeros((4, 2) + value.shape, value.dtype)
    zero = (0,) * value.ndim
    for k, block in got:
        across = lax.ppermute(block, "shard", pairs(8, 1))
        at = (z - k) % 4
        out = lax.dynamic_update_slice(out, block[None, None], (at, y) + zero)
        out = lax.dynamic_update_slice(out, across[None, None], (at, 1 - y) + zero)
    return out.reshape((8,) + value.shape), got[1][1]


ORDER = ((3, 2, 1, 0), (3, 2, 0, 1), (0, 1, 3, 2), (0, 1, 2, 3))


def scatter_shards(value, shards):
    if shards != 8:
        return lax.psum_scatter(value, "shard", scatter_dimension=0)
    member = lax.axis_index("shard")
    z, y = member // 2, member % 2
    order = lax.dynamic_index_in_dim(jnp.asarray(ORDER, jnp.int32), z, 0, keepdims=False)

    def entry(i, side):
        return lax.dynamic_index_in_dim(value, 2 * order[i] + side, 0, keepdims=False)

    def move(block, steps):
        return lax.ppermute(block, "shard", [(2 * a + s, 2 * b + s) for a, b in steps for s in (0, 1)])

    across = [lax.ppermute(entry(i, 1 - y), "shard", pairs(8, 1)) for i in range(4)]
    line = [add(entry(i, y), across[i]) for i in range(4)]
    first = move(line[0], ((0, 1), (3, 2)))
    second = jnp.where((z == 0) | (z == 3), line[1], add(line[0], first))
    up = move(second, ((0, 1), (1, 2)))
    down = move(second, ((3, 2), (2, 1)))
    up = move(add(jnp.where(z == 1, line[1], line[2]), up), ((0, 1), (1, 2), (2, 3)))
    down = move(add(jnp.where(z == 2, line[1], line[2]), down), ((3, 2), (2, 1), (1, 0)))
    return add(line[3], up, down)


def on_device(reps, shards, *args):
    (tokens, resets, norm_gain, in_weight, conv_weight, conv_bias, step_bias, decay_log, skip_gain, gate_gain,
     out_weight, cotangent) = args
    rows = in_weight.shape[0]
    width = tokens.shape[1]
    inner = shards * gate_gain.shape[0]
    mixed = shards * conv_bias.shape[0]
    heads = shards * step_bias.shape[0]
    half = rows // 2
    core = lax.axis_index("rep") % 2
    member = lax.axis_index("shard")
    barrier = lax.optimization_barrier

    small_parts = (norm_gain, conv_weight, conv_bias, step_bias, decay_log, skip_gain, gate_gain)
    small = jnp.concatenate([v.reshape(-1) for v in small_parts])
    spare = LANES - heads
    small = jnp.pad(small, (0, half * spare - small.shape[0])).reshape(half, spare)
    small = jnp.pad(small, ((0, 0), (mixed + heads, 0)))
    own_rows = lax.dynamic_slice_in_dim(in_weight, core * half, half, 0)
    x_all, arrived = gather_shards(jnp.pad(own_rows[:, inner:], ((0, 0), (0, spare))) + small, shards)
    w_x = swap_halves(x_all, core, reps, 1).reshape(width, mixed + LANES)
    small_all = x_all[:, :, mixed + heads :].reshape(shards, -1).astype(F32)
    out_own = lax.dynamic_slice_in_dim(out_weight, core * 2 * half, 2 * half, 0)
    zo_own = jnp.concatenate([own_rows[:, :width], own_rows[:, width:inner], out_own], axis=0)
    zo_own, _ = barrier((zo_own, arrived))
    zo_all = lax.all_gather(zo_own, "shard", axis=0)

    full_small, at = [], 0
    for part in small_parts:
        piece = small_all[:, at : at + part.size]
        at += part.size
        if part.ndim == 2:
            piece = jnp.moveaxis(piece.reshape(shards, part.shape[0], part.shape[1]), 0, 1).reshape(part.shape[0], -1)
        else:
            piece = piece.reshape(-1)
        full_small.append(piece)
    gain, cw, cb, sb, dl, sk, gg = full_small
    repeat = LANES // heads
    cw8 = rows8(cw, cb)
    hp8 = rows8(jnp.tile(sb, repeat), jnp.tile(-jnp.exp(dl), repeat))
    sk8 = rows8(jnp.repeat(sk, WIDTH))
    gg8 = rows8(gg)

    col, row = document_info(resets)
    inputs = tokens.astype(F32)
    inv_rms = lax.rsqrt(jnp.mean(inputs * inputs, axis=-1, keepdims=True) + EPS)
    normed = (inputs * inv_rms * gain[None, :]).astype(BF)
    xbc = mm(normed, w_x)
    y, pre, sin = scan_forward(xbc, col, row, cw8, hp8, sk8)
    zo_all, y = barrier((zo_all, y))
    zo = swap_halves(zo_all, core, reps, 1)
    w_z = jnp.concatenate([zo[:, :, :half].reshape(width, width), zo[:, :, half : 2 * half].reshape(width, width)], axis=1)
    w_out = zo[:, :, 2 * half :].reshape(inner, width)
    z = mm(normed, w_z)
    g_mixed = mm_nt(cotangent, w_out)
    mixed_out, gy, gz, gg_grad = gate(y, z, g_mixed, gg8)

    def grad_of(left, right):
        return lax.dot_general(left, right, (((0,), (0,)), ((), ())), preferred_element_type=F32).astype(BF)

    out_grad = sum_cores(grad_of(mixed_out, cotangent).reshape(shards, 2, 2 * half, width), core, reps)
    z_grads = [
        sum_cores(grad_of(normed, gz[:, k : k + width]).reshape(shards, 2, half, width), core, reps)
        for k in (0, width)
    ]
    zo_sum, gy = barrier((jnp.concatenate(z_grads + [out_grad], axis=1), gy))
    zo_own = lax.psum_scatter(zo_sum, "shard", scatter_dimension=0)
    gp, cwg, hpg, skg = scan_backward(xbc, pre, y, gy, sin, col, row, cw8, hp8, sk8)
    x_grad = grad_of(normed, gp).reshape(shards, 2, half, mixed + LANES)
    zo_own, x_grad = barrier((zo_own, x_grad))
    x_own = scatter_shards(sum_cores(x_grad, core, reps), shards)
    output = (inputs + mm(mixed_out, w_out)).astype(BF)

    g_normed = mm_nt(gz, w_z) + mm_nt(gp, w_x)
    scaled = g_normed * gain[None, :]
    unit = inputs * inv_rms
    gain_grad = jnp.sum(g_normed * unit, axis=0)
    back = cotangent.astype(F32) + inv_rms * (scaled - unit * jnp.mean(scaled * unit, axis=-1, keepdims=True))
    input_grad = back.astype(BF)

    grads = (cwg[:4], cwg[4], hpg[0, :heads], hpg[1, :heads], skg[0].reshape(heads, WIDTH).sum(axis=1), gg_grad[0])
    split = lambda v: jnp.moveaxis(v.reshape(v.shape[:-1] + (shards, -1)), -2, 0).reshape(shards, -1)
    totals = sum_all(jnp.concatenate([split(v) for v in (gain_grad,) + grads], axis=1), reps, shards)
    own = lax.dynamic_index_in_dim(totals, member, 0, keepdims=False)
    small_grads, at = [], 0
    for part in small_parts:
        small_grads.append(own[at : at + part.size].reshape(part.shape))
        at += part.size

    zo_own = swap_halves(sum_reps(zo_own, reps), core, reps, 0).astype(F32)
    x_own = swap_halves(sum_reps(x_own, reps), core, reps, 0).astype(F32)
    out_part = zo_own[:, 2 * half :].reshape(out_weight.shape)
    in_grad = jnp.concatenate(
        [
            zo_own[:, :half].reshape(rows, width),
            zo_own[:, half : 2 * half].reshape(rows, width),
            x_own.reshape(rows, -1)[:, : mixed + heads],
        ],
        axis=1,
    )
    return (output, input_grad, small_grads[0], in_grad, *small_grads[1:], out_part)


def solution(mesh):
    by_token, by_shard = P(("rep", "shard"), None), P("shard")
    in_specs = (
        by_token, P(("rep", "shard")), by_shard, P("shard", None), P(None, "shard"), by_shard, by_shard, by_shard,
        by_shard, by_shard, P("shard", None), by_token,
    )
    out_specs = (
        by_token, by_token, by_shard, P("shard", None), P(None, "shard"), by_shard, by_shard, by_shard, by_shard,
        by_shard, P("shard", None),
    )
    return jax.shard_map(
        partial(on_device, mesh.shape["rep"], mesh.shape["shard"]),
        mesh=mesh,
        in_specs=in_specs,
        out_specs=out_specs,
        check_vma=False,
    )
```

```python
from functools import partial

import jax
import jax.numpy as jnp
import numpy as np
from jax import lax
from jax.experimental import pallas as pl
from jax.experimental.pallas import tpu as pltpu
from jax.sharding import PartitionSpec as P

EPS = 1e-05
SPAN = 128
LANES = 128
WIDTH = 64
BF = jnp.bfloat16
F32 = jnp.float32
HIGH = lax.Precision.HIGHEST


def mm(a, b):
    return jnp.dot(a, b, preferred_element_type=F32)


def mm_nt(a, b):
    return lax.dot_general(a, b, (((1,), (1,)), ((), ())), preferred_element_type=F32)


def split_lanes(v):
    lane = lax.broadcasted_iota(jnp.int32, v.shape, 1)
    high = v.astype(BF).astype(F32)
    return jnp.where(lane < 32, high, v - high).astype(BF)


def halves(v):
    high = v.astype(BF)
    return high, (v - high.astype(F32)).astype(BF)


def block_diag(v):
    lane = lax.broadcasted_iota(jnp.int32, v.shape, 1)
    zero = jnp.zeros_like(v)
    return jnp.concatenate([jnp.where(lane < WIDTH, v, zero), jnp.where(lane >= WIDTH, v, zero)], axis=0)


def softplus(v):
    return jnp.maximum(v, 0.0) + jnp.log1p(jnp.exp(-jnp.abs(v)))


def sigmoid(v):
    return 0.5 * jnp.tanh(0.5 * v) + 0.5


def repeat_heads(raw):
    lane = lax.broadcasted_iota(jnp.int32, raw.shape, 1)
    once = jnp.where(lane < 32, raw, 0.0)
    twice = once + pltpu.roll(once, 32, 1)
    return twice + pltpu.roll(twice, 64, 1)


def head_values(raw, col, hp_ref, ee_ref, at_ref, dtx_ref, esx_ref, tex_ref, keepx_ref):
    span = raw.shape[0]
    shifted = repeat_heads(raw) + hp_ref[0:1, :]
    dt = softplus(shifted)
    rates = hp_ref[1:2, :] * dt
    row = lax.broadcasted_iota(jnp.int32, (span, span), 0)
    column = lax.broadcasted_iota(jnp.int32, (span, span), 1)
    tri = jnp.where(row >= column, 1.0, 0.0).astype(F32)
    total = jnp.dot(tri, rates, precision=HIGH, preferred_element_type=F32)
    at_ref[...] = total.T
    last = total[span - 1 : span, :]
    ee = ee_ref[...]
    dtx_ref[...] = mm(split_lanes(dt), ee)
    esx_ref[...] = mm(split_lanes(jnp.exp(total) * col[:, 7:8]), ee)
    tex_ref[...] = mm(split_lanes(jnp.exp(last - total) * col[:, 8:9]), ee)
    keepx_ref[...] = mm(split_lanes(jnp.broadcast_to(jnp.exp(last) * col[0:1, 9:10], (8, LANES))), ee)
    return shifted, rates, total


def pair_decay(pair, total, at_ref):
    span = total.shape[0]
    heads = (2 * pair, 2 * pair + 1)
    column = jnp.concatenate([jnp.broadcast_to(total[:, h : h + 1], (span, span)) for h in heads], axis=1)
    row = jnp.concatenate([at_ref[h : h + 1, :] for h in heads], axis=1)
    return column, row


def fwd_kernel(
    inner,
    xbc_ref, col_ref, row_ref, cw_ref, hp_ref, skip_ref, ee_ref,
    y_ref, pre_ref, sin_ref,
    buf, state, at_ref, dtx_ref, esx_ref, tex_ref, keepx_ref, g2_ref,
):
    span = y_ref.shape[0]
    mixed = pre_ref.shape[1]
    step = pl.program_id(0)

    @pl.when(step == 0)
    def _():
        buf[0:8, :] = jnp.zeros((8, mixed), F32)
        state[...] = jnp.zeros_like(state)

    @pl.when(step > 0)
    def _():
        buf[0:8, :] = buf[span : span + 8, :]

    buf[8 : 8 + span, :] = xbc_ref[:, :mixed]
    col = col_ref[...]
    _, _, total = head_values(
        xbc_ref[:, mixed : mixed + LANES], col, hp_ref, ee_ref, at_ref, dtx_ref, esx_ref, tex_ref, keepx_ref
    )
    same = [None] + [jnp.broadcast_to(col[:, k : k + 1], (span, LANES)) for k in (1, 2, 3)]

    def conv(lanes):
        pre = cw_ref[4:5, lanes] + cw_ref[3:4, lanes] * buf[8 : 8 + span, lanes]
        for k in (1, 2, 3):
            pre = pre + cw_ref[3 - k : 4 - k, lanes] * (buf[8 - k : 8 - k + span, lanes] * same[k])
        pre_ref[:, lanes] = pre
        return pre * sigmoid(pre)

    b_f = conv(slice(inner, inner + LANES))
    c_b = conv(slice(inner + LANES, inner + 2 * LANES)).astype(BF)
    b_b = b_f.astype(BF)
    b_t = b_f.T.astype(BF)
    t_index = lax.broadcasted_iota(jnp.int32, (span, span), 0)
    s_index = lax.broadcasted_iota(jnp.int32, (span, span), 1)
    linked = (t_index >= s_index) & (col[:, 0:1] == row_ref[0:1, :])
    inter = jnp.where(linked, mm_nt(c_b, b_b), 0.0)
    g2_ref[...] = jnp.concatenate([inter, inter], axis=1)

    def pair_step(pair):
        lanes = slice(pair * LANES, (pair + 1) * LANES)
        x = conv(lanes)
        xd = x * dtx_ref[:, lanes]
        column, row = pair_decay(pair, total, at_ref)
        decay = jnp.exp(jnp.minimum(column - row, 0.0))
        inside = mm((g2_ref[...] * decay).astype(BF), block_diag(xd.astype(BF)))
        held = state[:, lanes]
        held_b = held.astype(BF)
        sin_ref[:, lanes] = held_b
        y_ref[:, lanes] = inside + mm(c_b, held_b) * esx_ref[:, lanes] + skip_ref[0:1, lanes] * x
        state[:, lanes] = held * keepx_ref[0:1, lanes] + mm(b_t, (xd * tex_ref[:, lanes]).astype(BF))

    for pair in range(inner // LANES):
        pair_step(pair)


def bwd_kernel(
    inner,
    xbc_ref, pre_ref, y_ref, gy_ref, sin_ref, col_ref, row_ref, cw_ref, hp_ref, skip_ref, ee_ref, rt_ref,
    gp_ref, cwg_ref, hpg_ref, skg_ref,
    grad, halo, gstate, at_ref, dtx_ref, esx_ref, tex_ref, keepx_ref, gt2_ref, ggt_ref, gb_ref, gc_ref, acc_ref, kv_ref,
):
    span = y_ref.shape[0]
    mixed = pre_ref.shape[1]
    step = pl.program_id(0)

    @pl.when(step == 0)
    def _():
        halo[...] = jnp.zeros_like(halo)
        gstate[...] = jnp.zeros_like(gstate)
        cwg_ref[...] = jnp.zeros_like(cwg_ref)
        hpg_ref[...] = jnp.zeros_like(hpg_ref)
        skg_ref[...] = jnp.zeros_like(skg_ref)

    col = col_ref[...]
    shifted, rates, total = head_values(
        xbc_ref[:, mixed : mixed + LANES], col, hp_ref, ee_ref, at_ref, dtx_ref, esx_ref, tex_ref, keepx_ref
    )
    ahead = [None] + [jnp.broadcast_to(col[:, 3 + k : 4 + k], (span, LANES)) for k in (1, 2, 3)]

    def conv_back(lanes, g):
        grad[0:span, lanes] = g
        grad[span : span + 8, lanes] = halo[:, lanes]
        halo[:, lanes] = g[0:8, :]
        xin = xbc_ref[:, lanes]
        back = cw_ref[3:4, lanes] * g
        cwg_ref[3:4, lanes] += jnp.sum(xin * g, axis=0, keepdims=True)
        cwg_ref[4:5, lanes] += jnp.sum(g, axis=0, keepdims=True)
        for k in (1, 2, 3):
            moved = grad[k : k + span, lanes] * ahead[k]
            back = back + cw_ref[3 - k : 4 - k, lanes] * moved
            cwg_ref[3 - k : 4 - k, lanes] += jnp.sum(xin * moved, axis=0, keepdims=True)
        gp_ref[:, lanes] = back.astype(BF)

    def act(lanes):
        pre = pre_ref[:, lanes]
        sig = sigmoid(pre)
        return pre * sig, sig * (1.0 + pre * (1.0 - sig))

    b_lanes, c_lanes = slice(inner, inner + LANES), slice(inner + LANES, inner + 2 * LANES)
    b_f, b_slope = act(b_lanes)
    c_f, c_slope = act(c_lanes)
    b_b, c_b = b_f.astype(BF), c_f.astype(BF)
    c_t = c_f.T.astype(BF)
    s_index = lax.broadcasted_iota(jnp.int32, (span, span), 0)
    t_index = lax.broadcasted_iota(jnp.int32, (span, span), 1)
    linked = (t_index >= s_index) & (col[:, 0:1] == row_ref[0:1, :])
    inter = jnp.where(linked, mm_nt(b_b, c_b), 0.0)
    gt2_ref[...] = jnp.concatenate([inter, inter], axis=1)
    ggt_ref[...] = jnp.zeros_like(ggt_ref)
    gb_ref[...] = jnp.zeros_like(gb_ref)
    gc_ref[...] = jnp.zeros_like(gc_ref)
    acc_ref[...] = jnp.zeros_like(acc_ref)

    def pair_step(pair):
        lanes = slice(pair * LANES, (pair + 1) * LANES)
        x, slope = act(lanes)
        dtx, tex = dtx_ref[:, lanes], tex_ref[:, lanes]
        xd = x * dtx
        xd_b = xd.astype(BF)
        gy_b = gy_ref[:, lanes]
        gy = gy_b.astype(F32)
        diag = block_diag(gy_b)
        column, row = pair_decay(pair, total, at_ref)
        decay = jnp.exp(jnp.minimum(row - column, 0.0))
        linked_g = mm_nt(xd_b, diag) * decay
        ggt_ref[...] += linked_g[:, :span] + linked_g[:, span:]
        gx_in = mm((gt2_ref[...] * decay).astype(BF), diag)
        gs = gstate[:, lanes]
        gs_b = gs.astype(BF)
        gx_state = tex * mm(b_b, gs_b)
        gxd = gx_in + gx_state
        from_state = xd * gx_state
        skip = skip_ref[0:1, lanes]
        drift = gy * (y_ref[:, lanes] - skip * x) - xd_b.astype(F32) * gx_in - from_state
        parts = [halves(v) for v in (drift, from_state, x * gxd)]
        stacked = jnp.concatenate([jnp.concatenate(part, axis=1) for part in parts], axis=0)
        rt = rt_ref[lanes, :]
        acc_ref[...] += mm(stacked, jnp.concatenate([rt, rt], axis=0))
        skg_ref[0:1, lanes] += jnp.sum(gy * x, axis=0, keepdims=True)
        held_b = sin_ref[:, lanes]
        keepx = keepx_ref[0:1, lanes]
        kv_ref[0:1, lanes] = keepx * jnp.sum(held_b.astype(F32) * gs, axis=0, keepdims=True)
        scaled = (esx_ref[:, lanes] * gy).astype(BF)
        gc_ref[...] += mm_nt(scaled, held_b)
        gb_ref[...] += mm_nt((xd * tex).astype(BF), gs_b)
        gstate[:, lanes] = keepx * gs + mm(c_t, scaled)
        conv_back(lanes, (dtx * gxd + skip * gy) * slope)

    kv_ref[...] = jnp.zeros_like(kv_ref)
    for pair in range(inner // LANES):
        pair_step(pair)
    g_inter = jnp.where(linked, ggt_ref[...], 0.0)
    conv_back(b_lanes, (gb_ref[...] + mm(g_inter.astype(BF), c_b)) * b_slope)
    conv_back(c_lanes, (gc_ref[...] + mm(g_inter.T.astype(BF), b_b)) * c_slope)
    kv_high, kv_low = halves(kv_ref[...])
    rt = rt_ref[...]
    kept = mm(kv_high, rt) + mm(kv_low, rt)
    at_end = jnp.sum(acc_ref[span : 2 * span, :], axis=0, keepdims=True) + kept[0:1, :]
    tri = jnp.where(t_index >= s_index, 1.0, 0.0).astype(F32)
    g_rate = jnp.dot(tri, acc_ref[0:span, :], precision=HIGH, preferred_element_type=F32) + at_end
    g_raw = (acc_ref[2 * span : 3 * span, :] + hp_ref[1:2, :] * g_rate) * sigmoid(shifted)
    gp_ref[:, mixed : mixed + LANES] = g_raw.astype(BF)
    hpg_ref[0:1, :] += jnp.sum(g_raw, axis=0, keepdims=True)
    hpg_ref[1:2, :] += jnp.sum(rates * g_rate, axis=0, keepdims=True)


def gate_kernel(y_ref, normed_ref, dy_ref, wz_ref, wo_ref, gain_ref, out_ref, gy_ref, gz_ref, gg_ref, z_ref, gm_ref):
    rows, inner = y_ref.shape

    @pl.when(pl.program_id(0) == 0)
    def _():
        gg_ref[...] = jnp.zeros_like(gg_ref)

    pieces = [slice(k, k + 2 * LANES) for k in range(0, inner, 2 * LANES)]
    square = jnp.zeros((rows, 2 * LANES), F32)
    cross = jnp.zeros((rows, 2 * LANES), F32)
    normed, dy = normed_ref[...], dy_ref[...]
    for lanes in pieces:
        z = mm(normed, wz_ref[:, lanes])
        gm = mm_nt(dy, wo_ref[lanes, :])
        z_ref[:, lanes] = z
        gm_ref[:, lanes] = gm
        gated = y_ref[:, lanes] * (z * sigmoid(z))
        square = square + gated * gated
        cross = cross + gated * (gm * gain_ref[0:1, lanes])
    inv = lax.rsqrt(jnp.sum(square, axis=1, keepdims=True) / inner + EPS)
    pull = inv * inv * inv * (jnp.sum(cross, axis=1, keepdims=True) / inner)
    for lanes in pieces:
        z, y, gm = z_ref[:, lanes], y_ref[:, lanes], gm_ref[:, lanes]
        sig = sigmoid(z)
        silu = z * sig
        gated = y * silu
        gain = gain_ref[0:1, lanes]
        unit = gated * inv
        out_ref[:, lanes] = (unit * gain).astype(BF)
        gg_ref[0:1, lanes] += jnp.sum(gm * unit, axis=0, keepdims=True)
        g_gated = inv * (gm * gain) - gated * pull
        gy_ref[:, lanes] = (g_gated * silu).astype(BF)
        gz_ref[:, lanes] = (g_gated * y * (sig + silu * (1.0 - sig))).astype(BF)


def full(shape):
    return pl.BlockSpec(shape, lambda i: (0,) * len(shape))


def onehots(inner):
    heads = inner // WIDTH
    owner = np.arange(inner) // WIDTH
    spread = np.zeros((LANES, inner), np.float32)
    spread[owner, np.arange(inner)] = 1
    spread[32 + owner, np.arange(inner)] = 1
    collect = np.zeros((inner, LANES), np.float32)
    collect[np.arange(inner), owner] = 1
    return jnp.asarray(spread, BF), jnp.asarray(collect, BF)


PARAMS = pltpu.CompilerParams(dimension_semantics=("arbitrary",), vmem_limit_bytes=52 * 2**20)


def common_scratch(inner):
    return [
        pltpu.VMEM((LANES, SPAN), F32),
        pltpu.VMEM((SPAN, inner), F32),
        pltpu.VMEM((SPAN, inner), F32),
        pltpu.VMEM((SPAN, inner), F32),
        pltpu.VMEM((8, inner), F32),
        pltpu.VMEM((SPAN, 2 * SPAN), F32),
    ]


def scan_forward(xbc, col, row, cw, hp, skip):
    length, mixed, inner = xbc.shape[0], cw.shape[1], skip.shape[1]
    spread, _ = onehots(inner)
    blocks = length // SPAN
    return pl.pallas_call(
        partial(fwd_kernel, inner),
        grid=(blocks,),
        in_specs=[
            pl.BlockSpec((SPAN, mixed + LANES), lambda i: (i, 0)),
            pl.BlockSpec((SPAN, 16), lambda i: (i, 0)),
            pl.BlockSpec((8, SPAN), lambda i: (0, i)),
            full((8, mixed)), full((8, LANES)), full((8, inner)), full((LANES, inner)),
        ],
        out_specs=[
            pl.BlockSpec((SPAN, inner), lambda i: (i, 0)),
            pl.BlockSpec((SPAN, mixed), lambda i: (i, 0)),
            pl.BlockSpec((LANES, inner), lambda i: (i, 0)),
        ],
        out_shape=[
            jax.ShapeDtypeStruct((length, inner), F32),
            jax.ShapeDtypeStruct((length, mixed), F32),
            jax.ShapeDtypeStruct((blocks * LANES, inner), BF),
        ],
        scratch_shapes=[pltpu.VMEM((SPAN + 8, mixed), F32), pltpu.VMEM((LANES, inner), F32)] + common_scratch(inner),
        compiler_params=PARAMS,
        cost_estimate=pl.CostEstimate(flops=6 * 10**9, bytes_accessed=3 * 10**7, transcendentals=10**7),
        name="scan_forward",
    )(xbc, col, row, cw, hp, skip, spread)


def scan_backward(xbc, pre, y, gy, sin, col, row, cw, hp, skip):
    length, mixed, inner = xbc.shape[0], cw.shape[1], skip.shape[1]
    spread, collect = onehots(inner)
    blocks = length // SPAN
    rev = lambda i: (blocks - 1 - i, 0)
    return pl.pallas_call(
        partial(bwd_kernel, inner),
        grid=(blocks,),
        in_specs=[
            pl.BlockSpec((SPAN, mixed + LANES), rev),
            pl.BlockSpec((SPAN, mixed), rev),
            pl.BlockSpec((SPAN, inner), rev),
            pl.BlockSpec((SPAN, inner), rev),
            pl.BlockSpec((LANES, inner), rev),
            pl.BlockSpec((SPAN, 16), rev),
            pl.BlockSpec((8, SPAN), lambda i: (0, blocks - 1 - i)),
            full((8, mixed)), full((8, LANES)), full((8, inner)), full((LANES, inner)), full((inner, LANES)),
        ],
        out_specs=[
            pl.BlockSpec((SPAN, mixed + LANES), rev),
            full((8, mixed)), full((8, LANES)), full((8, inner)),
        ],
        out_shape=[
            jax.ShapeDtypeStruct((length, mixed + LANES), BF),
            jax.ShapeDtypeStruct((8, mixed), F32),
            jax.ShapeDtypeStruct((8, LANES), F32),
            jax.ShapeDtypeStruct((8, inner), F32),
        ],
        scratch_shapes=[
            pltpu.VMEM((SPAN + 8, mixed), F32), pltpu.VMEM((8, mixed), F32), pltpu.VMEM((LANES, inner), F32),
        ] + common_scratch(inner) + [
            pltpu.VMEM((SPAN, SPAN), F32), pltpu.VMEM((SPAN, LANES), F32), pltpu.VMEM((SPAN, LANES), F32),
            pltpu.VMEM((3 * SPAN, LANES), F32), pltpu.VMEM((8, inner), F32),
        ],
        compiler_params=PARAMS,
        cost_estimate=pl.CostEstimate(flops=2 * 10**10, bytes_accessed=5 * 10**7, transcendentals=10**7),
        name="scan_backward",
    )(xbc, pre, y, gy, sin, col, row, cw, hp, skip, spread, collect)


def gate(y, normed, dy, w_z, w_out, gain):
    length, inner = y.shape
    width = normed.shape[1]
    rows = 256
    block = lambda columns: pl.BlockSpec((rows, columns), lambda i: (i, 0))
    return pl.pallas_call(
        gate_kernel,
        grid=(length // rows,),
        in_specs=[
            block(inner), block(width), block(width), full((width, inner)), full((inner, width)), full((8, inner)),
        ],
        out_specs=[block(inner), block(inner), block(inner), full((8, inner))],
        out_shape=[jax.ShapeDtypeStruct((length, inner), BF)] * 3 + [jax.ShapeDtypeStruct((8, inner), F32)],
        scratch_shapes=[pltpu.VMEM((rows, inner), F32), pltpu.VMEM((rows, inner), F32)],
        compiler_params=PARAMS,
        cost_estimate=pl.CostEstimate(flops=9 * 10**9, bytes_accessed=4 * 10**7, transcendentals=4 * 10**6),
        name="gate",
    )(y, normed, dy, w_z, w_out, gain)


def input_kernel(tokens_ref, dy_ref, gz_ref, gp_ref, wz_ref, wx_ref, gain_ref, out_ref, gg_ref):
    @pl.when(pl.program_id(0) == 0)
    def _():
        gg_ref[...] = jnp.zeros_like(gg_ref)

    g_normed = mm_nt(gz_ref[...], wz_ref[...]) + mm_nt(gp_ref[...], wx_ref[...])
    inputs = tokens_ref[...].astype(F32)
    inv = lax.rsqrt(jnp.mean(inputs * inputs, axis=1, keepdims=True) + EPS)
    unit = inputs * inv
    scaled = g_normed * gain_ref[0:1, :]
    gg_ref[0:1, :] += jnp.sum(g_normed * unit, axis=0, keepdims=True)
    pull = jnp.mean(scaled * unit, axis=1, keepdims=True)
    out_ref[...] = (dy_ref[...].astype(F32) + inv * (scaled - unit * pull)).astype(BF)


def input_gradient(tokens, dy, gz, gp, w_z, w_x, gain):
    length, width = tokens.shape
    rows = 256
    block = lambda v: pl.BlockSpec((rows, v.shape[1]), lambda i: (i, 0))
    return pl.pallas_call(
        input_kernel,
        grid=(length // rows,),
        in_specs=[block(v) for v in (tokens, dy, gz, gp)] + [full(v.shape) for v in (w_z, w_x, gain)],
        out_specs=[block(tokens), full((8, width))],
        out_shape=[jax.ShapeDtypeStruct((length, width), BF), jax.ShapeDtypeStruct((8, width), F32)],
        compiler_params=PARAMS,
        cost_estimate=pl.CostEstimate(flops=10**7, bytes_accessed=10**5, transcendentals=0),
        name="input_gradient",
    )(tokens, dy, gz, gp, w_z, w_x, gain)


def document_info(resets):
    length = resets.shape[0]
    segment = jnp.cumsum(resets).astype(jnp.int32)
    back = [jnp.pad(segment, (k, 0), constant_values=-1)[:length] == segment for k in (1, 2, 3)]
    ahead = [jnp.pad(segment, (0, k), constant_values=-1)[k:] == segment for k in (1, 2, 3)]
    last = segment.reshape(-1, SPAN)[:, -1]
    before = jnp.concatenate([jnp.full((1,), -1, jnp.int32), last[:-1]])
    last, before = jnp.repeat(last, SPAN), jnp.repeat(before, SPAN)
    columns = [segment] + back + ahead + [segment == before, segment == last, last == before]
    columns = columns + [jnp.zeros_like(segment)] * (16 - len(columns))
    col = jnp.stack([c.astype(F32) for c in columns], axis=1)
    row = jnp.broadcast_to(segment.astype(F32)[None, :], (8, length))
    return col, row


def rows8(*rows):
    width = rows[0].shape[-1]
    rows = [r.reshape(-1, width).astype(F32) for r in rows]
    have = sum(r.shape[0] for r in rows)
    return jnp.concatenate(rows + [jnp.zeros((8 - have, width), F32)], axis=0)


def pairs(size, flip):
    return [(i, i ^ flip) for i in range(size)]


def other_core(value, reps):
    return lax.ppermute(value, "rep", pairs(reps, 1))


def swap_halves(own, core, reps, axis):
    other = other_core(own, reps)
    first = core == 0
    return jnp.stack([jnp.where(first, own, other), jnp.where(first, other, own)], axis=axis)


def half_of(value, core, axis):
    pick = lambda k: lax.dynamic_index_in_dim(value, k, axis, keepdims=False)
    return pick(core), pick(1 - core)


def sum_cores(value, core, reps):
    mine, theirs = half_of(value, core, 1)
    return (mine.astype(F32) + other_core(theirs, reps).astype(F32)).astype(BF)


def sum_reps(value, reps):
    flip = 2
    while flip < reps:
        value = add(value, lax.ppermute(value, "rep", pairs(reps, flip)))
        flip *= 2
    return value


def gather_shards(value, small, shards):
    if shards != 8:
        return lax.all_gather(value, "shard", axis=0), lax.all_gather(small, "shard", axis=0), value
    member = lax.axis_index("shard")
    z, y = member // 2, member % 2

    def from_behind(block, k):
        return lax.ppermute(block, "shard", [(i, (i + 2 * k) % 8) for i in range(8)])

    got = [(0, value)] + [(k, from_behind(value, k)) for k in (1, 3, 2)]
    other = lax.ppermute(small, "shard", pairs(8, 1))
    pair = jnp.stack([jnp.where(y == 0, small, other), jnp.where(y == 0, other, small)])
    places = jnp.stack([pair] + [from_behind(pair, k) for k in (1, 2, 3)])
    small_all = jnp.take(places, (z - jnp.arange(4)) % 4, axis=0).reshape((8,) + small.shape)
    blank, arrived = lax.optimization_barrier((jnp.zeros((), value.dtype), got[1][1]))
    got[1] = (1, arrived)
    out = jnp.broadcast_to(blank, (4, 2) + value.shape)
    start = (0,) * value.ndim
    for k, block in got:
        across = lax.ppermute(block, "shard", pairs(8, 1))
        at = (z - k) % 4
        out = lax.dynamic_update_slice(out, block[None, None], (at, y) + start)
        out = lax.dynamic_update_slice(out, across[None, None], (at, 1 - y) + start)
        if k == 3:
            out, small_all = lax.optimization_barrier((out, small_all))
    return out.reshape((8,) + value.shape), small_all, arrived


def along_z(value, z):
    own = lax.dynamic_index_in_dim(value, z, 0, keepdims=False)
    got = []
    for k in (1, 3, 2):
        entry = lax.dynamic_index_in_dim(value, (z + k) % 4, 0, keepdims=False)
        got.append(lax.ppermute(entry, "shard", [(i, (i + 2 * k) % 8) for i in range(8)]))
    return [own] + got


def along_y(value, y, axis):
    mine, theirs = half_of(value, y, axis)
    return [mine, lax.ppermute(theirs, "shard", pairs(8, 1))]


def add(*values):
    return sum(v.astype(F32) for v in values).astype(values[0].dtype)


def scatter_shards(first, second, shards, during):
    if shards != 8:
        first, second = during(0, (first, second))
        return during(1, tuple(lax.psum_scatter(v, "shard", scatter_dimension=0) for v in (first, second)))
    member = lax.axis_index("shard")
    z, y = member // 2, member % 2
    first = along_y(first.reshape((4, 2) + first.shape[1:]), y, 1)
    second = along_z(second.reshape((4, 2) + second.shape[1:]), z)
    first, second = during(0, (first, second))
    first = along_z(add(*first), z)
    second = along_y(add(*second), y, 0)
    first, second = during(1, (first, second))
    return add(*first), add(*second)


def on_device(reps, shards, *args):
    (tokens, resets, norm_gain, in_weight, conv_weight, conv_bias, step_bias, decay_log, skip_gain, gate_gain,
     out_weight, cotangent) = args
    rows = in_weight.shape[0]
    width = tokens.shape[1]
    inner = shards * gate_gain.shape[0]
    mixed = shards * conv_bias.shape[0]
    heads = shards * step_bias.shape[0]
    half = rows // 2
    core = lax.axis_index("rep") % 2
    barrier = lax.optimization_barrier

    small_parts = (norm_gain, conv_weight, conv_bias, step_bias, decay_log, skip_gain, gate_gain)
    small = jnp.concatenate([v.reshape(-1) for v in small_parts])
    small = jnp.pad(small, (0, -small.shape[0] % 1024)).reshape(-1, 1024)
    own_rows = lax.dynamic_slice_in_dim(in_weight, core * half, half, 0)
    x_all, small_all, arrived = gather_shards(jnp.pad(own_rows[:, inner:], ((0, 0), (0, LANES - heads))), small, shards)
    w_x = swap_halves(x_all, core, reps, 1).reshape(width, mixed + LANES)
    small_all = small_all.reshape(shards, -1).astype(F32)
    out_own = lax.dynamic_slice_in_dim(out_weight, core * 2 * half, 2 * half, 0)
    zo_own = jnp.concatenate([own_rows[:, :width], own_rows[:, width:inner], out_own], axis=0)
    zo_own, _ = barrier((zo_own, arrived))
    zo_all = lax.all_gather(zo_own, "shard", axis=0)

    full_small, at = [], 0
    for part in small_parts:
        piece = small_all[:, at : at + part.size]
        at += part.size
        if part.ndim == 2:
            piece = jnp.moveaxis(piece.reshape(shards, part.shape[0], part.shape[1]), 0, 1).reshape(part.shape[0], -1)
        else:
            piece = piece.reshape(-1)
        full_small.append(piece)
    gain, cw, cb, sb, dl, sk, gg = full_small
    repeat = LANES // heads
    cw8 = rows8(cw, cb)
    hp8 = rows8(jnp.tile(sb, repeat), jnp.tile(-jnp.exp(dl), repeat))
    sk8 = rows8(jnp.repeat(sk, WIDTH))
    gg8 = rows8(gg)

    col, row = document_info(resets)
    inputs = tokens.astype(F32)
    inv_rms = lax.rsqrt(jnp.mean(inputs * inputs, axis=-1, keepdims=True) + EPS)
    normed = (inputs * inv_rms * gain[None, :]).astype(BF)
    xbc = mm(normed, w_x)
    y, pre, sin = scan_forward(xbc, col, row, cw8, hp8, sk8)
    zo_all, y = barrier((zo_all, y))
    zo = swap_halves(zo_all, core, reps, 1)
    w_z = jnp.concatenate([zo[:, :, :half].reshape(width, width), zo[:, :, half : 2 * half].reshape(width, width)], axis=1)
    w_out = zo[:, :, 2 * half :].reshape(inner, width)
    mixed_out, gy, gz, gg_grad = gate(y, normed, cotangent, w_z, w_out, gg8)

    def grad_of(left, right):
        return lax.dot_general(left, right, (((0,), (0,)), ((), ())), preferred_element_type=F32).astype(BF)

    out_grad = sum_cores(grad_of(mixed_out, cotangent).reshape(shards, 2, 2 * half, width), core, reps)
    z_grads = [
        sum_cores(grad_of(normed, gz[:, k : k + width]).reshape(shards, 2, half, width), core, reps)
        for k in (0, width)
    ]
    zo_sum, gy = barrier((jnp.concatenate(z_grads + [out_grad], axis=1), gy))
    zo_own = lax.psum_scatter(zo_sum, "shard", scatter_dimension=0)
    gp, cwg, hpg, skg = scan_backward(xbc, pre, y, gy, sin, col, row, cw8, hp8, sk8)
    cut = (mixed + LANES) // (3 * LANES) * 2 * LANES
    x_grad = grad_of(normed, gp).reshape(shards, 2, half, mixed + LANES)
    x_mine, x_theirs = half_of(x_grad, core, 1)
    x_theirs = other_core(x_theirs, reps)
    output = (inputs + mm(mixed_out, w_out)).astype(BF)
    x_theirs, output = barrier((x_theirs, output))
    x_sums = [add(x_mine[:, :, s], x_theirs[:, :, s]) for s in (slice(0, cut), slice(cut, mixed + LANES))]
    x_sums, gp = barrier((x_sums, gp))
    input_grad, gain_grad = input_gradient(tokens, cotangent, gz, gp, w_z, w_x, rows8(gain))

    def during(stage, value):
        nonlocal input_grad, gain_grad, zo_own
        if stage == 0:
            value, input_grad, gain_grad, zo_own = barrier((value, input_grad, gain_grad, zo_own))
        return value

    x_parts = scatter_shards(*x_sums, shards, during)
    gain_grad = gain_grad[0]

    grads = (cwg[:4], cwg[4], hpg[0, :heads], hpg[1, :heads], skg[0].reshape(heads, WIDTH).sum(axis=1), gg_grad[0])
    split = lambda v: jnp.moveaxis(v.reshape(v.shape[:-1] + (shards, -1)), -2, 0).reshape(shards, -1)
    own = jnp.concatenate([split(v) for v in (gain_grad,) + grads], axis=1)
    own = own + other_core(own, reps)
    own, _ = scatter_shards(own, own[:, :LANES], shards, lambda stage, value: value)
    own = sum_reps(own, reps)
    small_grads, at = [], 0
    for part in small_parts:
        small_grads.append(own[at : at + part.size].reshape(part.shape))
        at += part.size

    zo_own = swap_halves(sum_reps(zo_own, reps), core, reps, 0).astype(F32)
    x_own = swap_halves(sum_reps(jnp.concatenate(x_parts, axis=1), reps), core, reps, 0).astype(F32)
    out_part = zo_own[:, 2 * half :].reshape(out_weight.shape)
    in_grad = jnp.concatenate(
        [
            zo_own[:, :half].reshape(rows, width),
            zo_own[:, half : 2 * half].reshape(rows, width),
            x_own.reshape(rows, -1)[:, : mixed + heads],
        ],
        axis=1,
    )
    return (output, input_grad, small_grads[0], in_grad, *small_grads[1:], out_part)


def solution(mesh):
    by_token, by_shard = P(("rep", "shard"), None), P("shard")
    in_specs = (
        by_token, P(("rep", "shard")), by_shard, P("shard", None), P(None, "shard"), by_shard, by_shard, by_shard,
        by_shard, by_shard, P("shard", None), by_token,
    )
    out_specs = (
        by_token, by_token, by_shard, P("shard", None), P(None, "shard"), by_shard, by_shard, by_shard, by_shard,
        by_shard, P("shard", None),
    )
    return jax.shard_map(
        partial(on_device, mesh.shape["rep"], mesh.shape["shard"]),
        mesh=mesh,
        in_specs=in_specs,
        out_specs=out_specs,
        check_vma=False,
    )
```

```python
from functools import partial

import jax
import jax.numpy as jnp
import numpy as np
from jax import lax
from jax.experimental import pallas as pl
from jax.experimental.pallas import tpu as pltpu
from jax.sharding import PartitionSpec as P

EPS = 1e-05
SPAN = 128
LANES = 128
WIDTH = 64
BF = jnp.bfloat16
F32 = jnp.float32
HIGH = lax.Precision.HIGHEST


def mm(a, b):
    return jnp.dot(a, b, preferred_element_type=F32)


def mm_nt(a, b):
    return lax.dot_general(a, b, (((1,), (1,)), ((), ())), preferred_element_type=F32)


def split_lanes(v):
    lane = lax.broadcasted_iota(jnp.int32, v.shape, 1)
    high = v.astype(BF).astype(F32)
    return jnp.where(lane < 32, high, v - high).astype(BF)


def halves(v):
    high = v.astype(BF)
    return high, (v - high.astype(F32)).astype(BF)


def block_diag(v):
    lane = lax.broadcasted_iota(jnp.int32, v.shape, 1)
    zero = jnp.zeros_like(v)
    return jnp.concatenate([jnp.where(lane < WIDTH, v, zero), jnp.where(lane >= WIDTH, v, zero)], axis=0)


def softplus(v):
    return jnp.maximum(v, 0.0) + jnp.log1p(jnp.exp(-jnp.abs(v)))


def sigmoid(v):
    return 0.5 * jnp.tanh(0.5 * v) + 0.5


def repeat_heads(raw):
    lane = lax.broadcasted_iota(jnp.int32, raw.shape, 1)
    once = jnp.where(lane < 32, raw, 0.0)
    twice = once + pltpu.roll(once, 32, 1)
    return twice + pltpu.roll(twice, 64, 1)


def head_values(raw, col, hp_ref, ee_ref, at_ref, dtx_ref, esx_ref, tex_ref, keepx_ref):
    span = raw.shape[0]
    shifted = repeat_heads(raw) + hp_ref[0:1, :]
    dt = softplus(shifted)
    rates = hp_ref[1:2, :] * dt
    row = lax.broadcasted_iota(jnp.int32, (span, span), 0)
    column = lax.broadcasted_iota(jnp.int32, (span, span), 1)
    tri = jnp.where(row >= column, 1.0, 0.0).astype(F32)
    total = jnp.dot(tri, rates, precision=HIGH, preferred_element_type=F32)
    at_ref[...] = total.T
    last = total[span - 1 : span, :]
    ee = ee_ref[...]
    dtx_ref[...] = mm(split_lanes(dt), ee)
    esx_ref[...] = mm(split_lanes(jnp.exp(total) * col[:, 7:8]), ee)
    tex_ref[...] = mm(split_lanes(jnp.exp(last - total) * col[:, 8:9]), ee)
    keepx_ref[...] = mm(split_lanes(jnp.broadcast_to(jnp.exp(last) * col[0:1, 9:10], (8, LANES))), ee)
    return shifted, rates, total


def pair_decay(pair, total, at_ref):
    span = total.shape[0]
    heads = (2 * pair, 2 * pair + 1)
    column = jnp.concatenate([jnp.broadcast_to(total[:, h : h + 1], (span, span)) for h in heads], axis=1)
    row = jnp.concatenate([at_ref[h : h + 1, :] for h in heads], axis=1)
    return column, row


def fwd_kernel(
    inner,
    xbc_ref, col_ref, row_ref, cw_ref, hp_ref, skip_ref, ee_ref,
    y_ref, pre_ref, sin_ref,
    buf, state, at_ref, dtx_ref, esx_ref, tex_ref, keepx_ref, g2_ref,
):
    span = y_ref.shape[0]
    mixed = pre_ref.shape[1]
    step = pl.program_id(0)

    @pl.when(step == 0)
    def _():
        buf[0:8, :] = jnp.zeros((8, mixed), F32)
        state[...] = jnp.zeros_like(state)

    @pl.when(step > 0)
    def _():
        buf[0:8, :] = buf[span : span + 8, :]

    buf[8 : 8 + span, :] = xbc_ref[:, :mixed]
    col = col_ref[...]
    _, _, total = head_values(
        xbc_ref[:, mixed : mixed + LANES], col, hp_ref, ee_ref, at_ref, dtx_ref, esx_ref, tex_ref, keepx_ref
    )
    same = [None] + [jnp.broadcast_to(col[:, k : k + 1], (span, LANES)) for k in (1, 2, 3)]

    def conv(lanes):
        pre = cw_ref[4:5, lanes] + cw_ref[3:4, lanes] * buf[8 : 8 + span, lanes]
        for k in (1, 2, 3):
            pre = pre + cw_ref[3 - k : 4 - k, lanes] * (buf[8 - k : 8 - k + span, lanes] * same[k])
        pre_ref[:, lanes] = pre
        return pre * sigmoid(pre)

    b_f = conv(slice(inner, inner + LANES))
    c_b = conv(slice(inner + LANES, inner + 2 * LANES)).astype(BF)
    b_b = b_f.astype(BF)
    b_t = b_f.T.astype(BF)
    t_index = lax.broadcasted_iota(jnp.int32, (span, span), 0)
    s_index = lax.broadcasted_iota(jnp.int32, (span, span), 1)
    linked = (t_index >= s_index) & (col[:, 0:1] == row_ref[0:1, :])
    inter = jnp.where(linked, mm_nt(c_b, b_b), 0.0)
    g2_ref[...] = jnp.concatenate([inter, inter], axis=1)

    def pair_step(pair):
        lanes = slice(pair * LANES, (pair + 1) * LANES)
        x = conv(lanes)
        xd = x * dtx_ref[:, lanes]
        column, row = pair_decay(pair, total, at_ref)
        decay = jnp.exp(jnp.minimum(column - row, 0.0))
        inside = mm((g2_ref[...] * decay).astype(BF), block_diag(xd.astype(BF)))
        held = state[:, lanes]
        held_b = held.astype(BF)
        sin_ref[:, lanes] = held_b
        y_ref[:, lanes] = inside + mm(c_b, held_b) * esx_ref[:, lanes] + skip_ref[0:1, lanes] * x
        state[:, lanes] = held * keepx_ref[0:1, lanes] + mm(b_t, (xd * tex_ref[:, lanes]).astype(BF))

    for pair in range(inner // LANES):
        pair_step(pair)


def bwd_kernel(
    inner,
    xbc_ref, pre_ref, y_ref, gy_ref, sin_ref, col_ref, row_ref, cw_ref, hp_ref, skip_ref, ee_ref, rt_ref,
    gp_ref, cwg_ref, hpg_ref, skg_ref,
    grad, halo, gstate, at_ref, dtx_ref, esx_ref, tex_ref, keepx_ref, gt2_ref, ggt_ref, gb_ref, gc_ref, acc_ref, kv_ref,
):
    span = y_ref.shape[0]
    mixed = pre_ref.shape[1]
    step = pl.program_id(0)

    @pl.when(step == 0)
    def _():
        halo[...] = jnp.zeros_like(halo)
        gstate[...] = jnp.zeros_like(gstate)
        cwg_ref[...] = jnp.zeros_like(cwg_ref)
        hpg_ref[...] = jnp.zeros_like(hpg_ref)
        skg_ref[...] = jnp.zeros_like(skg_ref)

    col = col_ref[...]
    shifted, rates, total = head_values(
        xbc_ref[:, mixed : mixed + LANES], col, hp_ref, ee_ref, at_ref, dtx_ref, esx_ref, tex_ref, keepx_ref
    )
    ahead = [None] + [jnp.broadcast_to(col[:, 3 + k : 4 + k], (span, LANES)) for k in (1, 2, 3)]

    def conv_back(lanes, g):
        grad[0:span, lanes] = g
        grad[span : span + 8, lanes] = halo[:, lanes]
        halo[:, lanes] = g[0:8, :]
        xin = xbc_ref[:, lanes]
        back = cw_ref[3:4, lanes] * g
        cwg_ref[3:4, lanes] += jnp.sum(xin * g, axis=0, keepdims=True)
        cwg_ref[4:5, lanes] += jnp.sum(g, axis=0, keepdims=True)
        for k in (1, 2, 3):
            moved = grad[k : k + span, lanes] * ahead[k]
            back = back + cw_ref[3 - k : 4 - k, lanes] * moved
            cwg_ref[3 - k : 4 - k, lanes] += jnp.sum(xin * moved, axis=0, keepdims=True)
        gp_ref[:, lanes] = back.astype(BF)

    def act(lanes):
        pre = pre_ref[:, lanes]
        sig = sigmoid(pre)
        return pre * sig, sig * (1.0 + pre * (1.0 - sig))

    b_lanes, c_lanes = slice(inner, inner + LANES), slice(inner + LANES, inner + 2 * LANES)
    b_f, b_slope = act(b_lanes)
    c_f, c_slope = act(c_lanes)
    b_b, c_b = b_f.astype(BF), c_f.astype(BF)
    c_t = c_f.T.astype(BF)
    s_index = lax.broadcasted_iota(jnp.int32, (span, span), 0)
    t_index = lax.broadcasted_iota(jnp.int32, (span, span), 1)
    linked = (t_index >= s_index) & (col[:, 0:1] == row_ref[0:1, :])
    inter = jnp.where(linked, mm_nt(b_b, c_b), 0.0)
    gt2_ref[...] = jnp.concatenate([inter, inter], axis=1)
    ggt_ref[...] = jnp.zeros_like(ggt_ref)
    gb_ref[...] = jnp.zeros_like(gb_ref)
    gc_ref[...] = jnp.zeros_like(gc_ref)
    acc_ref[...] = jnp.zeros_like(acc_ref)

    def pair_step(pair):
        lanes = slice(pair * LANES, (pair + 1) * LANES)
        x, slope = act(lanes)
        dtx, tex = dtx_ref[:, lanes], tex_ref[:, lanes]
        xd = x * dtx
        xd_b = xd.astype(BF)
        gy_b = gy_ref[:, lanes]
        gy = gy_b.astype(F32)
        diag = block_diag(gy_b)
        column, row = pair_decay(pair, total, at_ref)
        decay = jnp.exp(jnp.minimum(row - column, 0.0))
        linked_g = mm_nt(xd_b, diag) * decay
        ggt_ref[...] += linked_g[:, :span] + linked_g[:, span:]
        gx_in = mm((gt2_ref[...] * decay).astype(BF), diag)
        gs = gstate[:, lanes]
        gs_b = gs.astype(BF)
        gx_state = tex * mm(b_b, gs_b)
        gxd = gx_in + gx_state
        from_state = xd * gx_state
        skip = skip_ref[0:1, lanes]
        drift = gy * (y_ref[:, lanes] - skip * x) - xd_b.astype(F32) * gx_in - from_state
        parts = [halves(v) for v in (drift, from_state, x * gxd)]
        stacked = jnp.concatenate([jnp.concatenate(part, axis=1) for part in parts], axis=0)
        rt = rt_ref[lanes, :]
        acc_ref[...] += mm(stacked, jnp.concatenate([rt, rt], axis=0))
        skg_ref[0:1, lanes] += jnp.sum(gy * x, axis=0, keepdims=True)
        held_b = sin_ref[:, lanes]
        keepx = keepx_ref[0:1, lanes]
        kv_ref[0:1, lanes] = keepx * jnp.sum(held_b.astype(F32) * gs, axis=0, keepdims=True)
        scaled = (esx_ref[:, lanes] * gy).astype(BF)
        gc_ref[...] += mm_nt(scaled, held_b)
        gb_ref[...] += mm_nt((xd * tex).astype(BF), gs_b)
        gstate[:, lanes] = keepx * gs + mm(c_t, scaled)
        conv_back(lanes, (dtx * gxd + skip * gy) * slope)

    kv_ref[...] = jnp.zeros_like(kv_ref)
    for pair in range(inner // LANES):
        pair_step(pair)
    g_inter = jnp.where(linked, ggt_ref[...], 0.0)
    conv_back(b_lanes, (gb_ref[...] + mm(g_inter.astype(BF), c_b)) * b_slope)
    conv_back(c_lanes, (gc_ref[...] + mm(g_inter.T.astype(BF), b_b)) * c_slope)
    kv_high, kv_low = halves(kv_ref[...])
    rt = rt_ref[...]
    kept = mm(kv_high, rt) + mm(kv_low, rt)
    at_end = jnp.sum(acc_ref[span : 2 * span, :], axis=0, keepdims=True) + kept[0:1, :]
    tri = jnp.where(t_index >= s_index, 1.0, 0.0).astype(F32)
    g_rate = jnp.dot(tri, acc_ref[0:span, :], precision=HIGH, preferred_element_type=F32) + at_end
    g_raw = (acc_ref[2 * span : 3 * span, :] + hp_ref[1:2, :] * g_rate) * sigmoid(shifted)
    gp_ref[:, mixed : mixed + LANES] = g_raw.astype(BF)
    hpg_ref[0:1, :] += jnp.sum(g_raw, axis=0, keepdims=True)
    hpg_ref[1:2, :] += jnp.sum(rates * g_rate, axis=0, keepdims=True)


def z_weight(zo_refs, lanes):
    shards, rows, width = zo_refs[0].shape
    half, side = rows // 4, lanes.start // width
    columns = slice(lanes.start - side * width, lanes.stop - side * width)
    parts = [ref[:, side * half : (side + 1) * half, columns] for ref in zo_refs]
    return jnp.stack(parts, axis=1).reshape(2 * shards * half, columns.stop - columns.start)


def out_weight_rows(zo_refs, lanes):
    shards, rows, width = zo_refs[0].shape
    parts = [ref[lanes.start // rows : lanes.stop // rows, rows // 2 :, :] for ref in zo_refs]
    return jnp.stack(parts, axis=1).reshape(lanes.stop - lanes.start, width)


def gate_kernel(y_ref, normed_ref, dy_ref, zo0_ref, zo1_ref, gain_ref, out_ref, gy_ref, gz_ref, gg_ref, z_ref, gm_ref):
    rows, inner = y_ref.shape

    @pl.when(pl.program_id(0) == 0)
    def _():
        gg_ref[...] = jnp.zeros_like(gg_ref)

    pieces = [slice(k, k + 2 * LANES) for k in range(0, inner, 2 * LANES)]
    square = jnp.zeros((rows, 2 * LANES), F32)
    cross = jnp.zeros((rows, 2 * LANES), F32)
    normed, dy = normed_ref[...], dy_ref[...]
    for lanes in pieces:
        z = mm(normed, z_weight((zo0_ref, zo1_ref), lanes))
        gm = mm_nt(dy, out_weight_rows((zo0_ref, zo1_ref), lanes))
        z_ref[:, lanes] = z
        gm_ref[:, lanes] = gm
        gated = y_ref[:, lanes] * (z * sigmoid(z))
        square = square + gated * gated
        cross = cross + gated * (gm * gain_ref[0:1, lanes])
    inv = lax.rsqrt(jnp.sum(square, axis=1, keepdims=True) / inner + EPS)
    pull = inv * inv * inv * (jnp.sum(cross, axis=1, keepdims=True) / inner)
    for lanes in pieces:
        z, y, gm = z_ref[:, lanes], y_ref[:, lanes], gm_ref[:, lanes]
        sig = sigmoid(z)
        silu = z * sig
        gated = y * silu
        gain = gain_ref[0:1, lanes]
        unit = gated * inv
        out_ref[:, lanes] = (unit * gain).astype(BF)
        gg_ref[0:1, lanes] += jnp.sum(gm * unit, axis=0, keepdims=True)
        g_gated = inv * (gm * gain) - gated * pull
        gy_ref[:, lanes] = (g_gated * silu).astype(BF)
        gz_ref[:, lanes] = (g_gated * y * (sig + silu * (1.0 - sig))).astype(BF)


def full(shape):
    return pl.BlockSpec(shape, lambda i: (0,) * len(shape))


def onehots(inner):
    heads = inner // WIDTH
    owner = np.arange(inner) // WIDTH
    spread = np.zeros((LANES, inner), np.float32)
    spread[owner, np.arange(inner)] = 1
    spread[32 + owner, np.arange(inner)] = 1
    collect = np.zeros((inner, LANES), np.float32)
    collect[np.arange(inner), owner] = 1
    return jnp.asarray(spread, BF), jnp.asarray(collect, BF)


PARAMS = pltpu.CompilerParams(dimension_semantics=("arbitrary",), vmem_limit_bytes=52 * 2**20)


def common_scratch(inner):
    return [
        pltpu.VMEM((LANES, SPAN), F32),
        pltpu.VMEM((SPAN, inner), F32),
        pltpu.VMEM((SPAN, inner), F32),
        pltpu.VMEM((SPAN, inner), F32),
        pltpu.VMEM((8, inner), F32),
        pltpu.VMEM((SPAN, 2 * SPAN), F32),
    ]


def scan_forward(xbc, col, row, cw, hp, skip):
    length, mixed, inner = xbc.shape[0], cw.shape[1], skip.shape[1]
    spread, _ = onehots(inner)
    blocks = length // SPAN
    return pl.pallas_call(
        partial(fwd_kernel, inner),
        grid=(blocks,),
        in_specs=[
            pl.BlockSpec((SPAN, mixed + LANES), lambda i: (i, 0)),
            pl.BlockSpec((SPAN, 16), lambda i: (i, 0)),
            pl.BlockSpec((8, SPAN), lambda i: (0, i)),
            full((8, mixed)), full((8, LANES)), full((8, inner)), full((LANES, inner)),
        ],
        out_specs=[
            pl.BlockSpec((SPAN, inner), lambda i: (i, 0)),
            pl.BlockSpec((SPAN, mixed), lambda i: (i, 0)),
            pl.BlockSpec((LANES, inner), lambda i: (i, 0)),
        ],
        out_shape=[
            jax.ShapeDtypeStruct((length, inner), F32),
            jax.ShapeDtypeStruct((length, mixed), F32),
            jax.ShapeDtypeStruct((blocks * LANES, inner), BF),
        ],
        scratch_shapes=[pltpu.VMEM((SPAN + 8, mixed), F32), pltpu.VMEM((LANES, inner), F32)] + common_scratch(inner),
        compiler_params=PARAMS,
        cost_estimate=pl.CostEstimate(flops=6 * 10**9, bytes_accessed=3 * 10**7, transcendentals=10**7),
        name="scan_forward",
    )(xbc, col, row, cw, hp, skip, spread)


def scan_backward(xbc, pre, y, gy, sin, col, row, cw, hp, skip):
    length, mixed, inner = xbc.shape[0], cw.shape[1], skip.shape[1]
    spread, collect = onehots(inner)
    blocks = length // SPAN
    rev = lambda i: (blocks - 1 - i, 0)
    return pl.pallas_call(
        partial(bwd_kernel, inner),
        grid=(blocks,),
        in_specs=[
            pl.BlockSpec((SPAN, mixed + LANES), rev),
            pl.BlockSpec((SPAN, mixed), rev),
            pl.BlockSpec((SPAN, inner), rev),
            pl.BlockSpec((SPAN, inner), rev),
            pl.BlockSpec((LANES, inner), rev),
            pl.BlockSpec((SPAN, 16), rev),
            pl.BlockSpec((8, SPAN), lambda i: (0, blocks - 1 - i)),
            full((8, mixed)), full((8, LANES)), full((8, inner)), full((LANES, inner)), full((inner, LANES)),
        ],
        out_specs=[
            pl.BlockSpec((SPAN, mixed + LANES), rev),
            full((8, mixed)), full((8, LANES)), full((8, inner)),
        ],
        out_shape=[
            jax.ShapeDtypeStruct((length, mixed + LANES), BF),
            jax.ShapeDtypeStruct((8, mixed), F32),
            jax.ShapeDtypeStruct((8, LANES), F32),
            jax.ShapeDtypeStruct((8, inner), F32),
        ],
        scratch_shapes=[
            pltpu.VMEM((SPAN + 8, mixed), F32), pltpu.VMEM((8, mixed), F32), pltpu.VMEM((LANES, inner), F32),
        ] + common_scratch(inner) + [
            pltpu.VMEM((SPAN, SPAN), F32), pltpu.VMEM((SPAN, LANES), F32), pltpu.VMEM((SPAN, LANES), F32),
            pltpu.VMEM((3 * SPAN, LANES), F32), pltpu.VMEM((8, inner), F32),
        ],
        compiler_params=PARAMS,
        cost_estimate=pl.CostEstimate(flops=2 * 10**10, bytes_accessed=5 * 10**7, transcendentals=10**7),
        name="scan_backward",
    )(xbc, pre, y, gy, sin, col, row, cw, hp, skip, spread, collect)


def gate(y, normed, dy, zo, gain):
    length, inner = y.shape
    width = normed.shape[1]
    rows = 256
    block = lambda columns: pl.BlockSpec((rows, columns), lambda i: (i, 0))
    return pl.pallas_call(
        gate_kernel,
        grid=(length // rows,),
        in_specs=[
            block(inner), block(width), block(width), full(zo[0].shape), full(zo[1].shape), full((8, inner)),
        ],
        out_specs=[block(inner), block(inner), block(inner), full((8, inner))],
        out_shape=[jax.ShapeDtypeStruct((length, inner), BF)] * 3 + [jax.ShapeDtypeStruct((8, inner), F32)],
        scratch_shapes=[pltpu.VMEM((rows, inner), F32), pltpu.VMEM((rows, inner), F32)],
        compiler_params=PARAMS,
        cost_estimate=pl.CostEstimate(flops=9 * 10**9, bytes_accessed=4 * 10**7, transcendentals=4 * 10**6),
        name="gate",
    )(y, normed, dy, *zo, gain)


def input_kernel(tokens_ref, dy_ref, gz_ref, gp_ref, mixed_ref, zo0_ref, zo1_ref, wx_ref, gain_ref, grad_ref, out_ref):
    width, inner = tokens_ref.shape[1], gz_ref.shape[1]
    g_normed = mm_nt(gp_ref[...], wx_ref[...])
    for k in range(0, inner, width):
        lanes = slice(k, k + width)
        g_normed = g_normed + mm_nt(gz_ref[:, lanes], z_weight((zo0_ref, zo1_ref), lanes))
    inputs = tokens_ref[...].astype(F32)
    inv = lax.rsqrt(jnp.mean(inputs * inputs, axis=1, keepdims=True) + EPS)
    unit = inputs * inv
    scaled = g_normed * gain_ref[0:1, :]
    pull = jnp.mean(scaled * unit, axis=1, keepdims=True)
    grad_ref[...] = (dy_ref[...].astype(F32) + inv * (scaled - unit * pull)).astype(BF)
    total = inputs
    for k in range(0, inner, 2 * LANES):
        lanes = slice(k, k + 2 * LANES)
        total = total + mm(mixed_ref[:, lanes], out_weight_rows((zo0_ref, zo1_ref), lanes))
    out_ref[...] = total.astype(BF)


def input_gradient(tokens, dy, gz, gp, mixed_out, zo, w_x, gain):
    length, width = tokens.shape
    rows = 256
    block = lambda v: pl.BlockSpec((rows, v.shape[1]), lambda i: (i, 0))
    return pl.pallas_call(
        input_kernel,
        grid=(length // rows,),
        in_specs=[block(v) for v in (tokens, dy, gz, gp, mixed_out)] + [full(v.shape) for v in (*zo, w_x, gain)],
        out_specs=[block(tokens)] * 2,
        out_shape=[jax.ShapeDtypeStruct((length, width), BF)] * 2,
        compiler_params=PARAMS,
        cost_estimate=pl.CostEstimate(flops=10**7, bytes_accessed=10**5, transcendentals=0),
        name="input_gradient",
    )(tokens, dy, gz, gp, mixed_out, *zo, w_x, gain)


def document_info(resets):
    length = resets.shape[0]
    segment = jnp.cumsum(resets).astype(jnp.int32)
    back = [jnp.pad(segment, (k, 0), constant_values=-1)[:length] == segment for k in (1, 2, 3)]
    ahead = [jnp.pad(segment, (0, k), constant_values=-1)[k:] == segment for k in (1, 2, 3)]
    last = segment.reshape(-1, SPAN)[:, -1]
    before = jnp.concatenate([jnp.full((1,), -1, jnp.int32), last[:-1]])
    last, before = jnp.repeat(last, SPAN), jnp.repeat(before, SPAN)
    columns = [segment] + back + ahead + [segment == before, segment == last, last == before]
    columns = columns + [jnp.zeros_like(segment)] * (16 - len(columns))
    col = jnp.stack([c.astype(F32) for c in columns], axis=1)
    row = jnp.broadcast_to(segment.astype(F32)[None, :], (8, length))
    return col, row


def rows8(*rows):
    width = rows[0].shape[-1]
    rows = [r.reshape(-1, width).astype(F32) for r in rows]
    have = sum(r.shape[0] for r in rows)
    return jnp.concatenate(rows + [jnp.zeros((8 - have, width), F32)], axis=0)


def pairs(size, flip):
    return [(i, i ^ flip) for i in range(size)]


def other_core(value, reps):
    return lax.ppermute(value, "rep", pairs(reps, 1))


def swap_halves(own, core, reps, axis):
    other = other_core(own, reps)
    first = core == 0
    return jnp.stack([jnp.where(first, own, other), jnp.where(first, other, own)], axis=axis)


def half_of(value, core, axis):
    pick = lambda k: lax.dynamic_index_in_dim(value, k, axis, keepdims=False)
    return pick(core), pick(1 - core)


def sum_cores(value, core, reps):
    mine, theirs = half_of(value, core, 1)
    return (mine.astype(F32) + other_core(theirs, reps).astype(F32)).astype(BF)


def sum_reps(value, reps, flip=2):
    while flip < reps:
        value = add(value, lax.ppermute(value, "rep", pairs(reps, flip)))
        flip *= 2
    return value


def gather_shards(value, small, shards):
    if shards != 8:
        return lax.all_gather(value, "shard", axis=0), lax.all_gather(small, "shard", axis=0), value
    member = lax.axis_index("shard")
    z, y = member // 2, member % 2

    def from_behind(block, k):
        return lax.ppermute(block, "shard", [(i, (i + 2 * k) % 8) for i in range(8)])

    got = [(0, value)] + [(k, from_behind(value, k)) for k in (1, 3, 2)]
    other = lax.ppermute(small, "shard", pairs(8, 1))
    pair = jnp.stack([jnp.where(y == 0, small, other), jnp.where(y == 0, other, small)])
    places = jnp.stack([pair] + [from_behind(pair, k) for k in (1, 2, 3)])
    small_all = jnp.take(places, (z - jnp.arange(4)) % 4, axis=0).reshape((8,) + small.shape)
    blank, arrived = lax.optimization_barrier((jnp.zeros((), value.dtype), got[1][1]))
    got[1] = (1, arrived)
    out = jnp.broadcast_to(blank, (4, 2) + value.shape)
    start = (0,) * value.ndim
    for k, block in got:
        across = lax.ppermute(block, "shard", pairs(8, 1))
        at = (z - k) % 4
        out = lax.dynamic_update_slice(out, block[None, None], (at, y) + start)
        out = lax.dynamic_update_slice(out, across[None, None], (at, 1 - y) + start)
        if k == 3:
            out, small_all = lax.optimization_barrier((out, small_all))
    return out.reshape((8,) + value.shape), small_all, arrived


def along_z(value, z):
    own = lax.dynamic_index_in_dim(value, z, 0, keepdims=False)
    got = []
    for k in (1, 3, 2):
        entry = lax.dynamic_index_in_dim(value, (z + k) % 4, 0, keepdims=False)
        got.append(lax.ppermute(entry, "shard", [(i, (i + 2 * k) % 8) for i in range(8)]))
    return [own] + got


def along_y(value, y, axis):
    mine, theirs = half_of(value, y, axis)
    return [mine, lax.ppermute(theirs, "shard", pairs(8, 1))]


def add(*values):
    return sum(v.astype(F32) for v in values).astype(values[0].dtype)


def scatter_shards(first, second, shards, during):
    if shards != 8:
        first, second = during(0, (first, second))
        return during(1, tuple(lax.psum_scatter(v, "shard", scatter_dimension=0) for v in (first, second)))
    member = lax.axis_index("shard")
    z, y = member // 2, member % 2
    first = along_y(first.reshape((4, 2) + first.shape[1:]), y, 1)
    second = along_z(second.reshape((4, 2) + second.shape[1:]), z)
    first, second = during(0, (first, second))
    first = along_z(add(*first), z)
    second = along_y(add(*second), y, 0)
    first, second = during(1, (first, second))
    return add(*first), add(*second)


def on_device(reps, shards, *args):
    (tokens, resets, norm_gain, in_weight, conv_weight, conv_bias, step_bias, decay_log, skip_gain, gate_gain,
     out_weight, cotangent) = args
    rows = in_weight.shape[0]
    width = tokens.shape[1]
    inner = shards * gate_gain.shape[0]
    mixed = shards * conv_bias.shape[0]
    heads = shards * step_bias.shape[0]
    half = rows // 2
    core = lax.axis_index("rep") % 2
    barrier = lax.optimization_barrier

    small_parts = (norm_gain, conv_weight, conv_bias, step_bias, decay_log, skip_gain, gate_gain)
    small = jnp.concatenate([v.reshape(-1) for v in small_parts])
    small = jnp.pad(small, (0, -small.shape[0] % 1024)).reshape(-1, 1024)
    own_rows = lax.dynamic_slice_in_dim(in_weight, core * half, half, 0)
    x_all, small_all, arrived = gather_shards(jnp.pad(own_rows[:, inner:], ((0, 0), (0, LANES - heads))), small, shards)
    w_x = swap_halves(x_all, core, reps, 1).reshape(width, mixed + LANES)
    small_all = small_all.reshape(shards, -1).astype(F32)
    out_own = lax.dynamic_slice_in_dim(out_weight, core * 2 * half, 2 * half, 0)
    zo_own = jnp.concatenate([own_rows[:, :width], own_rows[:, width:inner], out_own], axis=0)
    zo_own, _ = barrier((zo_own, arrived))
    zo_all = lax.all_gather(zo_own, "shard", axis=0)

    full_small, at = [], 0
    for part in small_parts:
        piece = small_all[:, at : at + part.size]
        at += part.size
        if part.ndim == 2:
            piece = jnp.moveaxis(piece.reshape(shards, part.shape[0], part.shape[1]), 0, 1).reshape(part.shape[0], -1)
        else:
            piece = piece.reshape(-1)
        full_small.append(piece)
    gain, cw, cb, sb, dl, sk, gg = full_small
    repeat = LANES // heads
    cw8 = rows8(cw, cb)
    hp8 = rows8(jnp.tile(sb, repeat), jnp.tile(-jnp.exp(dl), repeat))
    sk8 = rows8(jnp.repeat(sk, WIDTH))
    gg8 = rows8(gg)

    col, row = document_info(resets)
    inputs = tokens.astype(F32)
    inv_rms = lax.rsqrt(jnp.mean(inputs * inputs, axis=-1, keepdims=True) + EPS)
    normed = (inputs * inv_rms * gain[None, :]).astype(BF)
    xbc = mm(normed, w_x)
    y, pre, sin = scan_forward(xbc, col, row, cw8, hp8, sk8)
    zo_all, y = barrier((zo_all, y))
    zo_other = other_core(zo_all, reps)
    zo = (jnp.where(core == 0, zo_all, zo_other), jnp.where(core == 0, zo_other, zo_all))
    mixed_out, gy, gz, gg_grad = gate(y, normed, cotangent, zo, gg8)

    def grad_of(left, right):
        return lax.dot_general(left, right, (((0,), (0,)), ((), ())), preferred_element_type=F32).astype(BF)

    out_grad = sum_cores(grad_of(mixed_out, cotangent).reshape(shards, 2, 2 * half, width), core, reps)
    z_grads = [
        sum_cores(grad_of(normed, gz[:, k : k + width]).reshape(shards, 2, half, width), core, reps)
        for k in (0, width)
    ]
    zo_sum, gy = barrier((jnp.concatenate(z_grads + [out_grad], axis=1), gy))
    zo_own = lax.psum_scatter(zo_sum, "shard", scatter_dimension=0)
    gp, cwg, hpg, skg = scan_backward(xbc, pre, y, gy, sin, col, row, cw8, hp8, sk8)
    cut = (mixed + LANES) // (3 * LANES) * 2 * LANES
    x_grad = grad_of(normed, gp).reshape(shards, 2, half, mixed + LANES)
    x_mine, x_theirs = half_of(x_grad, core, 1)
    x_theirs = other_core(x_theirs, reps)
    x_sums = [add(x_mine[:, :, s], x_theirs[:, :, s]) for s in (slice(0, cut), slice(cut, mixed + LANES))]
    x_sums, gp = barrier((x_sums, gp))
    input_grad, output = input_gradient(tokens, cotangent, gz, gp, mixed_out, zo, w_x, rows8(gain))

    grads = (cwg[:4], cwg[4], hpg[0, :heads], hpg[1, :heads], skg[0].reshape(heads, WIDTH).sum(axis=1), gg_grad[0])
    split = lambda v: jnp.moveaxis(v.reshape(v.shape[:-1] + (shards, -1)), -2, 0).reshape(shards, -1)
    own = jnp.concatenate([split(v) for v in grads], axis=1)
    own = own + other_core(own, reps)
    member = lax.axis_index("shard")
    z_at, y_at = member // 2, member % 2
    staged = shards == 8 and reps > 2
    if staged:
        own = along_y(own.reshape(4, 2, -1), y_at, 1)
    else:
        own = lax.psum_scatter(own, "shard", scatter_dimension=0)

    def during(stage, value):
        nonlocal input_grad, output, zo_own, own
        if stage == 0:
            value, input_grad, output, zo_own, own = barrier((value, input_grad, output, zo_own, own))
            if staged:
                zo_own = [zo_own, lax.ppermute(zo_own, "rep", pairs(reps, 2))]
                own = along_z(add(*own), z_at)
        elif staged:
            value, zo_own, own = barrier((value, zo_own, own))
            zo_own, own = add(*zo_own), add(*own)
        return value

    x_parts = scatter_shards(*x_sums, shards, during)
    zo_own = swap_halves(sum_reps(zo_own, reps, 4 if staged else 2), core, reps, 0).astype(F32)
    own = sum_reps(own, reps)
    x_own = swap_halves(sum_reps(jnp.concatenate(x_parts, axis=1), reps), core, reps, 0).astype(F32)
    small_grads, at = [], 0
    for part in small_parts[1:]:
        small_grads.append(own[at : at + part.size].reshape(part.shape))
        at += part.size

    out_part = zo_own[:, 2 * half :].reshape(out_weight.shape)
    in_grad = jnp.concatenate(
        [
            zo_own[:, :half].reshape(rows, width),
            zo_own[:, half : 2 * half].reshape(rows, width),
            x_own.reshape(rows, -1)[:, : mixed + heads],
        ],
        axis=1,
    )
    gain_grad = jnp.sum(in_weight.astype(F32) * in_grad, axis=1) / norm_gain.astype(F32)
    return (output, input_grad, gain_grad, in_grad, *small_grads, out_part)


def solution(mesh):
    by_token, by_shard = P(("rep", "shard"), None), P("shard")
    in_specs = (
        by_token, P(("rep", "shard")), by_shard, P("shard", None), P(None, "shard"), by_shard, by_shard, by_shard,
        by_shard, by_shard, P("shard", None), by_token,
    )
    out_specs = (
        by_token, by_token, by_shard, P("shard", None), P(None, "shard"), by_shard, by_shard, by_shard, by_shard,
        by_shard, P("shard", None),
    )
    return jax.shard_map(
        partial(on_device, mesh.shape["rep"], mesh.shape["shard"]),
        mesh=mesh,
        in_specs=in_specs,
        out_specs=out_specs,
        check_vma=False,
    )
```

```python
from functools import partial

import jax
import jax.numpy as jnp
import numpy as np
from jax import lax
from jax.experimental import pallas as pl
from jax.experimental.pallas import tpu as pltpu
from jax.sharding import PartitionSpec as P

EPS = 1e-05
SPAN = 128
LANES = 128
WIDTH = 64
BF = jnp.bfloat16
F32 = jnp.float32
HIGH = lax.Precision.HIGHEST


def mm(a, b):
    return jnp.dot(a, b, preferred_element_type=F32)


def mm_nt(a, b):
    return lax.dot_general(a, b, (((1,), (1,)), ((), ())), preferred_element_type=F32)


def split_lanes(v):
    lane = lax.broadcasted_iota(jnp.int32, v.shape, 1)
    high = v.astype(BF).astype(F32)
    return jnp.where(lane < 32, high, v - high).astype(BF)


def halves(v):
    high = v.astype(BF)
    return high, (v - high.astype(F32)).astype(BF)


def block_diag(v):
    lane = lax.broadcasted_iota(jnp.int32, v.shape, 1)
    zero = jnp.zeros_like(v)
    return jnp.concatenate([jnp.where(lane < WIDTH, v, zero), jnp.where(lane >= WIDTH, v, zero)], axis=0)


def softplus(v):
    return jnp.maximum(v, 0.0) + jnp.log1p(jnp.exp(-jnp.abs(v)))


def sigmoid(v):
    return 0.5 * jnp.tanh(0.5 * v) + 0.5


def repeat_heads(raw):
    lane = lax.broadcasted_iota(jnp.int32, raw.shape, 1)
    once = jnp.where(lane < 32, raw, 0.0)
    twice = once + pltpu.roll(once, 32, 1)
    return twice + pltpu.roll(twice, 64, 1)


def head_values(raw, col, hp_ref, ee_ref, at_ref, dtx_ref, esx_ref, tex_ref, keepx_ref):
    span = raw.shape[0]
    shifted = repeat_heads(raw) + hp_ref[0:1, :]
    dt = softplus(shifted)
    rates = hp_ref[1:2, :] * dt
    row = lax.broadcasted_iota(jnp.int32, (span, span), 0)
    column = lax.broadcasted_iota(jnp.int32, (span, span), 1)
    tri = jnp.where(row >= column, 1.0, 0.0).astype(F32)
    total = jnp.dot(tri, rates, precision=HIGH, preferred_element_type=F32)
    at_ref[...] = total.T
    last = total[span - 1 : span, :]
    ee = ee_ref[...]
    dtx_ref[...] = mm(split_lanes(dt), ee)
    esx_ref[...] = mm(split_lanes(jnp.exp(total) * col[:, 7:8]), ee)
    tex_ref[...] = mm(split_lanes(jnp.exp(last - total) * col[:, 8:9]), ee)
    keepx_ref[...] = mm(split_lanes(jnp.broadcast_to(jnp.exp(last) * col[0:1, 9:10], (8, LANES))), ee)
    return shifted, rates, total


def pair_decay(pair, total, at_ref):
    span = total.shape[0]
    heads = (2 * pair, 2 * pair + 1)
    column = jnp.concatenate([jnp.broadcast_to(total[:, h : h + 1], (span, span)) for h in heads], axis=1)
    row = jnp.concatenate([at_ref[h : h + 1, :] for h in heads], axis=1)
    return column, row


def fwd_kernel(
    inner,
    xbc_ref, col_ref, row_ref, cw_ref, hp_ref, skip_ref, ee_ref,
    y_ref, pre_ref, sin_ref,
    buf, state, at_ref, dtx_ref, esx_ref, tex_ref, keepx_ref, g2_ref,
):
    span = y_ref.shape[0]
    mixed = pre_ref.shape[1]
    step = pl.program_id(0)

    @pl.when(step == 0)
    def _():
        buf[0:8, :] = jnp.zeros((8, mixed), F32)
        state[...] = jnp.zeros_like(state)

    @pl.when(step > 0)
    def _():
        buf[0:8, :] = buf[span : span + 8, :]

    buf[8 : 8 + span, :] = xbc_ref[:, :mixed]
    col = col_ref[...]
    _, _, total = head_values(
        xbc_ref[:, mixed : mixed + LANES], col, hp_ref, ee_ref, at_ref, dtx_ref, esx_ref, tex_ref, keepx_ref
    )
    same = [None] + [jnp.broadcast_to(col[:, k : k + 1], (span, LANES)) for k in (1, 2, 3)]

    def conv(lanes):
        pre = cw_ref[4:5, lanes] + cw_ref[3:4, lanes] * buf[8 : 8 + span, lanes]
        for k in (1, 2, 3):
            pre = pre + cw_ref[3 - k : 4 - k, lanes] * (buf[8 - k : 8 - k + span, lanes] * same[k])
        pre_ref[:, lanes] = pre
        return pre * sigmoid(pre)

    b_f = conv(slice(inner, inner + LANES))
    c_b = conv(slice(inner + LANES, inner + 2 * LANES)).astype(BF)
    b_b = b_f.astype(BF)
    b_t = b_f.T.astype(BF)
    t_index = lax.broadcasted_iota(jnp.int32, (span, span), 0)
    s_index = lax.broadcasted_iota(jnp.int32, (span, span), 1)
    linked = (t_index >= s_index) & (col[:, 0:1] == row_ref[0:1, :])
    inter = jnp.where(linked, mm_nt(c_b, b_b), 0.0)
    g2_ref[...] = jnp.concatenate([inter, inter], axis=1)

    def pair_step(pair):
        lanes = slice(pair * LANES, (pair + 1) * LANES)
        x = conv(lanes)
        xd = x * dtx_ref[:, lanes]
        column, row = pair_decay(pair, total, at_ref)
        decay = jnp.exp(jnp.minimum(column - row, 0.0))
        inside = mm((g2_ref[...] * decay).astype(BF), block_diag(xd.astype(BF)))
        held = state[:, lanes]
        held_b = held.astype(BF)
        sin_ref[:, lanes] = held_b
        y_ref[:, lanes] = inside + mm(c_b, held_b) * esx_ref[:, lanes] + skip_ref[0:1, lanes] * x
        state[:, lanes] = held * keepx_ref[0:1, lanes] + mm(b_t, (xd * tex_ref[:, lanes]).astype(BF))

    for pair in range(inner // LANES):
        pair_step(pair)


def bwd_kernel(
    inner,
    xbc_ref, pre_ref, y_ref, gy_ref, sin_ref, col_ref, row_ref, cw_ref, hp_ref, skip_ref, ee_ref, rt_ref,
    gp_ref, cwg_ref, hpg_ref, skg_ref,
    grad, halo, gstate, at_ref, dtx_ref, esx_ref, tex_ref, keepx_ref, gt2_ref, ggt_ref, gb_ref, gc_ref, acc_ref, kv_ref,
):
    span = y_ref.shape[0]
    mixed = pre_ref.shape[1]
    step = pl.program_id(0)

    @pl.when(step == 0)
    def _():
        halo[...] = jnp.zeros_like(halo)
        gstate[...] = jnp.zeros_like(gstate)
        cwg_ref[...] = jnp.zeros_like(cwg_ref)
        hpg_ref[...] = jnp.zeros_like(hpg_ref)
        skg_ref[...] = jnp.zeros_like(skg_ref)

    col = col_ref[...]
    shifted, rates, total = head_values(
        xbc_ref[:, mixed : mixed + LANES], col, hp_ref, ee_ref, at_ref, dtx_ref, esx_ref, tex_ref, keepx_ref
    )
    ahead = [None] + [jnp.broadcast_to(col[:, 3 + k : 4 + k], (span, LANES)) for k in (1, 2, 3)]

    def conv_back(lanes, g):
        grad[0:span, lanes] = g
        grad[span : span + 8, lanes] = halo[:, lanes]
        halo[:, lanes] = g[0:8, :]
        xin = xbc_ref[:, lanes]
        back = cw_ref[3:4, lanes] * g
        cwg_ref[3:4, lanes] += jnp.sum(xin * g, axis=0, keepdims=True)
        cwg_ref[4:5, lanes] += jnp.sum(g, axis=0, keepdims=True)
        for k in (1, 2, 3):
            moved = grad[k : k + span, lanes] * ahead[k]
            back = back + cw_ref[3 - k : 4 - k, lanes] * moved
            cwg_ref[3 - k : 4 - k, lanes] += jnp.sum(xin * moved, axis=0, keepdims=True)
        gp_ref[:, lanes] = back.astype(BF)

    def act(lanes):
        pre = pre_ref[:, lanes]
        sig = sigmoid(pre)
        return pre * sig, sig * (1.0 + pre * (1.0 - sig))

    b_lanes, c_lanes = slice(inner, inner + LANES), slice(inner + LANES, inner + 2 * LANES)
    b_f, b_slope = act(b_lanes)
    c_f, c_slope = act(c_lanes)
    b_b, c_b = b_f.astype(BF), c_f.astype(BF)
    c_t = c_f.T.astype(BF)
    s_index = lax.broadcasted_iota(jnp.int32, (span, span), 0)
    t_index = lax.broadcasted_iota(jnp.int32, (span, span), 1)
    linked = (t_index >= s_index) & (col[:, 0:1] == row_ref[0:1, :])
    inter = jnp.where(linked, mm_nt(b_b, c_b), 0.0)
    gt2_ref[...] = jnp.concatenate([inter, inter], axis=1)
    ggt_ref[...] = jnp.zeros_like(ggt_ref)
    gb_ref[...] = jnp.zeros_like(gb_ref)
    gc_ref[...] = jnp.zeros_like(gc_ref)
    acc_ref[...] = jnp.zeros_like(acc_ref)

    def pair_step(pair):
        lanes = slice(pair * LANES, (pair + 1) * LANES)
        x, slope = act(lanes)
        dtx, tex = dtx_ref[:, lanes], tex_ref[:, lanes]
        xd = x * dtx
        xd_b = xd.astype(BF)
        gy_b = gy_ref[:, lanes]
        gy = gy_b.astype(F32)
        diag = block_diag(gy_b)
        column, row = pair_decay(pair, total, at_ref)
        decay = jnp.exp(jnp.minimum(row - column, 0.0))
        linked_g = mm_nt(xd_b, diag) * decay
        ggt_ref[...] += linked_g[:, :span] + linked_g[:, span:]
        gx_in = mm((gt2_ref[...] * decay).astype(BF), diag)
        gs = gstate[:, lanes]
        gs_b = gs.astype(BF)
        gx_state = tex * mm(b_b, gs_b)
        gxd = gx_in + gx_state
        from_state = xd * gx_state
        skip = skip_ref[0:1, lanes]
        drift = gy * (y_ref[:, lanes] - skip * x) - xd_b.astype(F32) * gx_in - from_state
        parts = [halves(v) for v in (drift, from_state, x * gxd)]
        stacked = jnp.concatenate([jnp.concatenate(part, axis=1) for part in parts], axis=0)
        rt = rt_ref[lanes, :]
        acc_ref[...] += mm(stacked, jnp.concatenate([rt, rt], axis=0))
        skg_ref[0:1, lanes] += jnp.sum(gy * x, axis=0, keepdims=True)
        held_b = sin_ref[:, lanes]
        keepx = keepx_ref[0:1, lanes]
        kv_ref[0:1, lanes] = keepx * jnp.sum(held_b.astype(F32) * gs, axis=0, keepdims=True)
        scaled = (esx_ref[:, lanes] * gy).astype(BF)
        gc_ref[...] += mm_nt(scaled, held_b)
        gb_ref[...] += mm_nt((xd * tex).astype(BF), gs_b)
        gstate[:, lanes] = keepx * gs + mm(c_t, scaled)
        conv_back(lanes, (dtx * gxd + skip * gy) * slope)

    kv_ref[...] = jnp.zeros_like(kv_ref)
    for pair in range(inner // LANES):
        pair_step(pair)
    g_inter = jnp.where(linked, ggt_ref[...], 0.0)
    conv_back(b_lanes, (gb_ref[...] + mm(g_inter.astype(BF), c_b)) * b_slope)
    conv_back(c_lanes, (gc_ref[...] + mm(g_inter.T.astype(BF), b_b)) * c_slope)
    kv_high, kv_low = halves(kv_ref[...])
    rt = rt_ref[...]
    kept = mm(kv_high, rt) + mm(kv_low, rt)
    at_end = jnp.sum(acc_ref[span : 2 * span, :], axis=0, keepdims=True) + kept[0:1, :]
    tri = jnp.where(t_index >= s_index, 1.0, 0.0).astype(F32)
    g_rate = jnp.dot(tri, acc_ref[0:span, :], precision=HIGH, preferred_element_type=F32) + at_end
    g_raw = (acc_ref[2 * span : 3 * span, :] + hp_ref[1:2, :] * g_rate) * sigmoid(shifted)
    gp_ref[:, mixed : mixed + LANES] = g_raw.astype(BF)
    hpg_ref[0:1, :] += jnp.sum(g_raw, axis=0, keepdims=True)
    hpg_ref[1:2, :] += jnp.sum(rates * g_rate, axis=0, keepdims=True)


def z_weight(zo_refs, lanes):
    shards, rows, width = zo_refs[0].shape
    half, side = rows // 4, lanes.start // width
    columns = slice(lanes.start - side * width, lanes.stop - side * width)
    parts = [ref[:, side * half : (side + 1) * half, columns] for ref in zo_refs]
    return jnp.stack(parts, axis=1).reshape(2 * shards * half, columns.stop - columns.start)


def out_weight_rows(zo_refs, lanes):
    shards, rows, width = zo_refs[0].shape
    parts = [ref[lanes.start // rows : lanes.stop // rows, rows // 2 :, :] for ref in zo_refs]
    return jnp.stack(parts, axis=1).reshape(lanes.stop - lanes.start, width)


def in_core_order(core_ref, mine_ref, other_ref, body):
    @pl.when(core_ref[0] == 0)
    def _():
        body((mine_ref, other_ref))

    @pl.when(core_ref[0] != 0)
    def _():
        body((other_ref, mine_ref))


def gate_kernel(core_ref, y_ref, normed_ref, dy_ref, mine_ref, other_ref, *refs):
    @pl.when(pl.program_id(0) == 0)
    def _():
        refs[4][...] = jnp.zeros_like(refs[4])

    in_core_order(
        core_ref, mine_ref, other_ref, lambda zo: gate_body(y_ref, normed_ref, dy_ref, zo, *refs)
    )


def gate_body(y_ref, normed_ref, dy_ref, zo, gain_ref, out_ref, gy_ref, gz_ref, gg_ref, z_ref, gm_ref):
    rows, inner = y_ref.shape

    pieces = [slice(k, k + 2 * LANES) for k in range(0, inner, 2 * LANES)]
    square = jnp.zeros((rows, 2 * LANES), F32)
    cross = jnp.zeros((rows, 2 * LANES), F32)
    normed, dy = normed_ref[...], dy_ref[...]
    for lanes in pieces:
        z = mm(normed, z_weight(zo, lanes))
        gm = mm_nt(dy, out_weight_rows(zo, lanes))
        z_ref[:, lanes] = z
        gm_ref[:, lanes] = gm
        gated = y_ref[:, lanes] * (z * sigmoid(z))
        square = square + gated * gated
        cross = cross + gated * (gm * gain_ref[0:1, lanes])
    inv = lax.rsqrt(jnp.sum(square, axis=1, keepdims=True) / inner + EPS)
    pull = inv * inv * inv * (jnp.sum(cross, axis=1, keepdims=True) / inner)
    for lanes in pieces:
        z, y, gm = z_ref[:, lanes], y_ref[:, lanes], gm_ref[:, lanes]
        sig = sigmoid(z)
        silu = z * sig
        gated = y * silu
        gain = gain_ref[0:1, lanes]
        unit = gated * inv
        out_ref[:, lanes] = (unit * gain).astype(BF)
        gg_ref[0:1, lanes] += jnp.sum(gm * unit, axis=0, keepdims=True)
        g_gated = inv * (gm * gain) - gated * pull
        gy_ref[:, lanes] = (g_gated * silu).astype(BF)
        gz_ref[:, lanes] = (g_gated * y * (sig + silu * (1.0 - sig))).astype(BF)


def full(shape):
    return pl.BlockSpec(shape, lambda i: (0,) * len(shape))


def onehots(inner):
    heads = inner // WIDTH
    owner = np.arange(inner) // WIDTH
    spread = np.zeros((LANES, inner), np.float32)
    spread[owner, np.arange(inner)] = 1
    spread[32 + owner, np.arange(inner)] = 1
    collect = np.zeros((inner, LANES), np.float32)
    collect[np.arange(inner), owner] = 1
    return jnp.asarray(spread, BF), jnp.asarray(collect, BF)


PARAMS = pltpu.CompilerParams(dimension_semantics=("arbitrary",), vmem_limit_bytes=52 * 2**20)


def common_scratch(inner):
    return [
        pltpu.VMEM((LANES, SPAN), F32),
        pltpu.VMEM((SPAN, inner), F32),
        pltpu.VMEM((SPAN, inner), F32),
        pltpu.VMEM((SPAN, inner), F32),
        pltpu.VMEM((8, inner), F32),
        pltpu.VMEM((SPAN, 2 * SPAN), F32),
    ]


def scan_forward(xbc, col, row, cw, hp, skip):
    length, mixed, inner = xbc.shape[0], cw.shape[1], skip.shape[1]
    spread, _ = onehots(inner)
    blocks = length // SPAN
    return pl.pallas_call(
        partial(fwd_kernel, inner),
        grid=(blocks,),
        in_specs=[
            pl.BlockSpec((SPAN, mixed + LANES), lambda i: (i, 0)),
            pl.BlockSpec((SPAN, 16), lambda i: (i, 0)),
            pl.BlockSpec((8, SPAN), lambda i: (0, i)),
            full((8, mixed)), full((8, LANES)), full((8, inner)), full((LANES, inner)),
        ],
        out_specs=[
            pl.BlockSpec((SPAN, inner), lambda i: (i, 0)),
            pl.BlockSpec((SPAN, mixed), lambda i: (i, 0)),
            pl.BlockSpec((LANES, inner), lambda i: (i, 0)),
        ],
        out_shape=[
            jax.ShapeDtypeStruct((length, inner), F32),
            jax.ShapeDtypeStruct((length, mixed), F32),
            jax.ShapeDtypeStruct((blocks * LANES, inner), BF),
        ],
        scratch_shapes=[pltpu.VMEM((SPAN + 8, mixed), F32), pltpu.VMEM((LANES, inner), F32)] + common_scratch(inner),
        compiler_params=PARAMS,
        cost_estimate=pl.CostEstimate(flops=6 * 10**9, bytes_accessed=3 * 10**7, transcendentals=10**7),
        name="scan_forward",
    )(xbc, col, row, cw, hp, skip, spread)


def scan_backward(xbc, pre, y, gy, sin, col, row, cw, hp, skip):
    length, mixed, inner = xbc.shape[0], cw.shape[1], skip.shape[1]
    spread, collect = onehots(inner)
    blocks = length // SPAN
    rev = lambda i: (blocks - 1 - i, 0)
    return pl.pallas_call(
        partial(bwd_kernel, inner),
        grid=(blocks,),
        in_specs=[
            pl.BlockSpec((SPAN, mixed + LANES), rev),
            pl.BlockSpec((SPAN, mixed), rev),
            pl.BlockSpec((SPAN, inner), rev),
            pl.BlockSpec((SPAN, inner), rev),
            pl.BlockSpec((LANES, inner), rev),
            pl.BlockSpec((SPAN, 16), rev),
            pl.BlockSpec((8, SPAN), lambda i: (0, blocks - 1 - i)),
            full((8, mixed)), full((8, LANES)), full((8, inner)), full((LANES, inner)), full((inner, LANES)),
        ],
        out_specs=[
            pl.BlockSpec((SPAN, mixed + LANES), rev),
            full((8, mixed)), full((8, LANES)), full((8, inner)),
        ],
        out_shape=[
            jax.ShapeDtypeStruct((length, mixed + LANES), BF),
            jax.ShapeDtypeStruct((8, mixed), F32),
            jax.ShapeDtypeStruct((8, LANES), F32),
            jax.ShapeDtypeStruct((8, inner), F32),
        ],
        scratch_shapes=[
            pltpu.VMEM((SPAN + 8, mixed), F32), pltpu.VMEM((8, mixed), F32), pltpu.VMEM((LANES, inner), F32),
        ] + common_scratch(inner) + [
            pltpu.VMEM((SPAN, SPAN), F32), pltpu.VMEM((SPAN, LANES), F32), pltpu.VMEM((SPAN, LANES), F32),
            pltpu.VMEM((3 * SPAN, LANES), F32), pltpu.VMEM((8, inner), F32),
        ],
        compiler_params=PARAMS,
        cost_estimate=pl.CostEstimate(flops=2 * 10**10, bytes_accessed=5 * 10**7, transcendentals=10**7),
        name="scan_backward",
    )(xbc, pre, y, gy, sin, col, row, cw, hp, skip, spread, collect)


def gate(core, y, normed, dy, zo, gain):
    length, inner = y.shape
    width = normed.shape[1]
    rows = 256
    block = lambda columns: pl.BlockSpec((rows, columns), lambda i: (i, 0))
    return pl.pallas_call(
        gate_kernel,
        grid=(length // rows,),
        in_specs=[
            pl.BlockSpec(memory_space=pltpu.SMEM),
            block(inner), block(width), block(width), full(zo[0].shape), full(zo[1].shape), full((8, inner)),
        ],
        out_specs=[block(inner), block(inner), block(inner), full((8, inner))],
        out_shape=[jax.ShapeDtypeStruct((length, inner), BF)] * 3 + [jax.ShapeDtypeStruct((8, inner), F32)],
        scratch_shapes=[pltpu.VMEM((rows, inner), F32), pltpu.VMEM((rows, inner), F32)],
        compiler_params=PARAMS,
        cost_estimate=pl.CostEstimate(flops=9 * 10**9, bytes_accessed=4 * 10**7, transcendentals=4 * 10**6),
        name="gate",
    )(core, y, normed, dy, *zo, gain)


def input_kernel(core_ref, tokens_ref, dy_ref, gz_ref, gp_ref, mixed_ref, mine_ref, other_ref, *refs):
    in_core_order(
        core_ref,
        mine_ref,
        other_ref,
        lambda zo: input_body(tokens_ref, dy_ref, gz_ref, gp_ref, mixed_ref, zo, *refs),
    )


def input_body(tokens_ref, dy_ref, gz_ref, gp_ref, mixed_ref, zo, wx_ref, gain_ref, grad_ref, out_ref):
    width, inner = tokens_ref.shape[1], gz_ref.shape[1]
    g_normed = mm_nt(gp_ref[...], wx_ref[...])
    for k in range(0, inner, width):
        lanes = slice(k, k + width)
        g_normed = g_normed + mm_nt(gz_ref[:, lanes], z_weight(zo, lanes))
    inputs = tokens_ref[...].astype(F32)
    inv = lax.rsqrt(jnp.mean(inputs * inputs, axis=1, keepdims=True) + EPS)
    unit = inputs * inv
    scaled = g_normed * gain_ref[0:1, :]
    pull = jnp.mean(scaled * unit, axis=1, keepdims=True)
    grad_ref[...] = (dy_ref[...].astype(F32) + inv * (scaled - unit * pull)).astype(BF)
    total = inputs
    for k in range(0, inner, 2 * LANES):
        lanes = slice(k, k + 2 * LANES)
        total = total + mm(mixed_ref[:, lanes], out_weight_rows(zo, lanes))
    out_ref[...] = total.astype(BF)


def input_gradient(core, tokens, dy, gz, gp, mixed_out, zo, w_x, gain):
    length, width = tokens.shape
    rows = 256
    block = lambda v: pl.BlockSpec((rows, v.shape[1]), lambda i: (i, 0))
    return pl.pallas_call(
        input_kernel,
        grid=(length // rows,),
        in_specs=[pl.BlockSpec(memory_space=pltpu.SMEM)]
        + [block(v) for v in (tokens, dy, gz, gp, mixed_out)] + [full(v.shape) for v in (*zo, w_x, gain)],
        out_specs=[block(tokens)] * 2,
        out_shape=[jax.ShapeDtypeStruct((length, width), BF)] * 2,
        compiler_params=PARAMS,
        cost_estimate=pl.CostEstimate(flops=10**7, bytes_accessed=10**5, transcendentals=0),
        name="input_gradient",
    )(core, tokens, dy, gz, gp, mixed_out, *zo, w_x, gain)


def document_info(resets):
    length = resets.shape[0]
    segment = jnp.cumsum(resets).astype(jnp.int32)
    back = [jnp.pad(segment, (k, 0), constant_values=-1)[:length] == segment for k in (1, 2, 3)]
    ahead = [jnp.pad(segment, (0, k), constant_values=-1)[k:] == segment for k in (1, 2, 3)]
    last = segment.reshape(-1, SPAN)[:, -1]
    before = jnp.concatenate([jnp.full((1,), -1, jnp.int32), last[:-1]])
    last, before = jnp.repeat(last, SPAN), jnp.repeat(before, SPAN)
    columns = [segment] + back + ahead + [segment == before, segment == last, last == before]
    columns = columns + [jnp.zeros_like(segment)] * (16 - len(columns))
    col = jnp.stack([c.astype(F32) for c in columns], axis=1)
    row = jnp.broadcast_to(segment.astype(F32)[None, :], (8, length))
    return col, row


def rows8(*rows):
    width = rows[0].shape[-1]
    rows = [r.reshape(-1, width).astype(F32) for r in rows]
    have = sum(r.shape[0] for r in rows)
    return jnp.concatenate(rows + [jnp.zeros((8 - have, width), F32)], axis=0)


def pairs(size, flip):
    return [(i, i ^ flip) for i in range(size)]


def other_core(value, reps):
    return lax.ppermute(value, "rep", pairs(reps, 1))


def swap_halves(own, core, reps, axis):
    other = other_core(own, reps)
    first = core == 0
    return jnp.stack([jnp.where(first, own, other), jnp.where(first, other, own)], axis=axis)


def half_of(value, core, axis):
    pick = lambda k: lax.dynamic_index_in_dim(value, k, axis, keepdims=False)
    return pick(core), pick(1 - core)


def sum_cores(value, core, reps):
    mine, theirs = half_of(value, core, 1)
    return (mine.astype(F32) + other_core(theirs, reps).astype(F32)).astype(BF)


def sum_reps(value, reps, flip=2):
    while flip < reps:
        value = add(value, lax.ppermute(value, "rep", pairs(reps, flip)))
        flip *= 2
    return value


def gather_shards(value, small, shards):
    if shards != 8:
        return lax.all_gather(value, "shard", axis=0), lax.all_gather(small, "shard", axis=0), value
    member = lax.axis_index("shard")
    z, y = member // 2, member % 2

    def from_behind(block, k):
        return lax.ppermute(block, "shard", [(i, (i + 2 * k) % 8) for i in range(8)])

    got = [(0, value)] + [(k, from_behind(value, k)) for k in (1, 3, 2)]
    other = lax.ppermute(small, "shard", pairs(8, 1))
    pair = jnp.stack([jnp.where(y == 0, small, other), jnp.where(y == 0, other, small)])
    places = jnp.stack([pair] + [from_behind(pair, k) for k in (1, 2, 3)])
    small_all = jnp.take(places, (z - jnp.arange(4)) % 4, axis=0).reshape((8,) + small.shape)
    blank, arrived = lax.optimization_barrier((jnp.zeros((), value.dtype), got[1][1]))
    got[1] = (1, arrived)
    out = jnp.broadcast_to(blank, (4, 2) + value.shape)
    start = (0,) * value.ndim
    for k, block in got:
        across = lax.ppermute(block, "shard", pairs(8, 1))
        at = (z - k) % 4
        out = lax.dynamic_update_slice(out, block[None, None], (at, y) + start)
        out = lax.dynamic_update_slice(out, across[None, None], (at, 1 - y) + start)
        if k == 3:
            out, small_all = lax.optimization_barrier((out, small_all))
    return out.reshape((8,) + value.shape), small_all, arrived


def along_z(value, z):
    own = lax.dynamic_index_in_dim(value, z, 0, keepdims=False)
    got = []
    for k in (1, 3, 2):
        entry = lax.dynamic_index_in_dim(value, (z + k) % 4, 0, keepdims=False)
        got.append(lax.ppermute(entry, "shard", [(i, (i + 2 * k) % 8) for i in range(8)]))
    return [own] + got


def along_y(value, y, axis):
    mine, theirs = half_of(value, y, axis)
    return [mine, lax.ppermute(theirs, "shard", pairs(8, 1))]


def add(*values):
    return sum(v.astype(F32) for v in values).astype(values[0].dtype)


def scatter_shards(first, second, shards, during):
    if shards != 8:
        first, second = during(0, (first, second))
        return during(1, tuple(lax.psum_scatter(v, "shard", scatter_dimension=0) for v in (first, second)))
    member = lax.axis_index("shard")
    z, y = member // 2, member % 2
    first = along_y(first.reshape((4, 2) + first.shape[1:]), y, 1)
    second = along_z(second.reshape((4, 2) + second.shape[1:]), z)
    first, second = during(0, (first, second))
    first = along_z(add(*first), z)
    second = along_y(add(*second), y, 0)
    first, second = during(1, (first, second))
    return add(*first), add(*second)


def on_device(reps, shards, *args):
    (tokens, resets, norm_gain, in_weight, conv_weight, conv_bias, step_bias, decay_log, skip_gain, gate_gain,
     out_weight, cotangent) = args
    rows = in_weight.shape[0]
    width = tokens.shape[1]
    inner = shards * gate_gain.shape[0]
    mixed = shards * conv_bias.shape[0]
    heads = shards * step_bias.shape[0]
    half = rows // 2
    core = lax.axis_index("rep") % 2
    barrier = lax.optimization_barrier

    small_parts = (norm_gain, conv_weight, conv_bias, step_bias, decay_log, skip_gain, gate_gain)
    small = jnp.concatenate([v.reshape(-1) for v in small_parts])
    small = jnp.pad(small, (0, -small.shape[0] % 1024)).reshape(-1, 1024)
    own_rows = lax.dynamic_slice_in_dim(in_weight, core * half, half, 0)
    x_all, small_all, arrived = gather_shards(jnp.pad(own_rows[:, inner:], ((0, 0), (0, LANES - heads))), small, shards)
    w_x = swap_halves(x_all, core, reps, 1).reshape(width, mixed + LANES)
    small_all = small_all.reshape(shards, -1).astype(F32)
    out_own = lax.dynamic_slice_in_dim(out_weight, core * 2 * half, 2 * half, 0)
    zo_own = jnp.concatenate([own_rows[:, :width], own_rows[:, width:inner], out_own], axis=0)
    zo_own, _ = barrier((zo_own, arrived))
    zo_all = lax.all_gather(zo_own, "shard", axis=0)

    full_small, at = [], 0
    for part in small_parts:
        piece = small_all[:, at : at + part.size]
        at += part.size
        if part.ndim == 2:
            piece = jnp.moveaxis(piece.reshape(shards, part.shape[0], part.shape[1]), 0, 1).reshape(part.shape[0], -1)
        else:
            piece = piece.reshape(-1)
        full_small.append(piece)
    gain, cw, cb, sb, dl, sk, gg = full_small
    repeat = LANES // heads
    cw8 = rows8(cw, cb)
    hp8 = rows8(jnp.tile(sb, repeat), jnp.tile(-jnp.exp(dl), repeat))
    sk8 = rows8(jnp.repeat(sk, WIDTH))
    gg8 = rows8(gg)

    col, row = document_info(resets)
    inputs = tokens.astype(F32)
    inv_rms = lax.rsqrt(jnp.mean(inputs * inputs, axis=-1, keepdims=True) + EPS)
    normed = (inputs * inv_rms * gain[None, :]).astype(BF)
    xbc = mm(normed, w_x)
    y, pre, sin = scan_forward(xbc, col, row, cw8, hp8, sk8)
    zo_all, y = barrier((zo_all, y))
    zo = (zo_all, other_core(zo_all, reps))
    core_at = jnp.reshape(core, (1,))
    mixed_out, gy, gz, gg_grad = gate(core_at, y, normed, cotangent, zo, gg8)

    def grad_of(left, right):
        return lax.dot_general(left, right, (((0,), (0,)), ((), ())), preferred_element_type=F32).astype(BF)

    out_grad = sum_cores(grad_of(mixed_out, cotangent).reshape(shards, 2, 2 * half, width), core, reps)
    z_grad = sum_cores(grad_of(normed, gz).reshape(shards, 2, half, inner), core, reps)
    zo_sum = jnp.concatenate([z_grad[:, :, :width], z_grad[:, :, width:], out_grad], axis=1)
    zo_sum, gy = barrier((zo_sum, gy))
    zo_own = lax.psum_scatter(zo_sum, "shard", scatter_dimension=0)
    gp, cwg, hpg, skg = scan_backward(xbc, pre, y, gy, sin, col, row, cw8, hp8, sk8)
    cut = (mixed + LANES) // (3 * LANES) * 2 * LANES
    x_grad = grad_of(normed, gp).reshape(shards, 2, half, mixed + LANES)
    x_mine, x_theirs = half_of(x_grad, core, 1)
    x_theirs = other_core(x_theirs, reps)
    x_sums = [add(x_mine[:, :, s], x_theirs[:, :, s]) for s in (slice(0, cut), slice(cut, mixed + LANES))]
    x_sums, gp = barrier((x_sums, gp))
    input_grad, output = input_gradient(core_at, tokens, cotangent, gz, gp, mixed_out, zo, w_x, rows8(gain))

    grads = (cwg[:4], cwg[4], hpg[0, :heads], hpg[1, :heads], skg[0].reshape(heads, WIDTH).sum(axis=1), gg_grad[0])
    split = lambda v: jnp.moveaxis(v.reshape(v.shape[:-1] + (shards, -1)), -2, 0).reshape(shards, -1)
    own = jnp.concatenate([split(v) for v in grads], axis=1)
    own = own + other_core(own, reps)
    member = lax.axis_index("shard")
    z_at, y_at = member // 2, member % 2
    staged = shards == 8 and reps > 2
    if staged:
        own = along_y(own.reshape(4, 2, -1), y_at, 1)
    else:
        own = lax.psum_scatter(own, "shard", scatter_dimension=0)

    def during(stage, value):
        nonlocal input_grad, output, zo_own, own
        if stage == 0:
            value, input_grad, output, zo_own, own = barrier((value, input_grad, output, zo_own, own))
            if staged:
                zo_own = [zo_own, lax.ppermute(zo_own, "rep", pairs(reps, 2))]
                own = along_z(add(*own), z_at)
        elif staged:
            value, zo_own, own = barrier((value, zo_own, own))
            zo_own, own = add(*zo_own), add(*own)
        return value

    x_parts = scatter_shards(*x_sums, shards, during)
    zo_own = swap_halves(sum_reps(zo_own, reps, 4 if staged else 2), core, reps, 0).astype(F32)
    own = sum_reps(own, reps)
    x_own = swap_halves(sum_reps(jnp.concatenate(x_parts, axis=1), reps), core, reps, 0).astype(F32)
    small_grads, at = [], 0
    for part in small_parts[1:]:
        small_grads.append(own[at : at + part.size].reshape(part.shape))
        at += part.size

    out_part = zo_own[:, 2 * half :].reshape(out_weight.shape)
    in_grad = jnp.concatenate(
        [
            zo_own[:, :half].reshape(rows, width),
            zo_own[:, half : 2 * half].reshape(rows, width),
            x_own.reshape(rows, -1)[:, : mixed + heads],
        ],
        axis=1,
    )
    gain_grad = jnp.sum(in_weight.astype(F32) * in_grad, axis=1) / norm_gain.astype(F32)
    return (output, input_grad, gain_grad, in_grad, *small_grads, out_part)


def solution(mesh):
    by_token, by_shard = P(("rep", "shard"), None), P("shard")
    in_specs = (
        by_token, P(("rep", "shard")), by_shard, P("shard", None), P(None, "shard"), by_shard, by_shard, by_shard,
        by_shard, by_shard, P("shard", None), by_token,
    )
    out_specs = (
        by_token, by_token, by_shard, P("shard", None), P(None, "shard"), by_shard, by_shard, by_shard, by_shard,
        by_shard, P("shard", None),
    )
    return jax.shard_map(
        partial(on_device, mesh.shape["rep"], mesh.shape["shard"]),
        mesh=mesh,
        in_specs=in_specs,
        out_specs=out_specs,
        check_vma=False,
    )
```

```python
from functools import partial

import jax
import jax.numpy as jnp
import numpy as np
from jax import lax
from jax.experimental import pallas as pl
from jax.experimental.pallas import tpu as pltpu
from jax.sharding import PartitionSpec as P

EPS = 1e-05
SPAN = 128
LANES = 128
WIDTH = 64
BF = jnp.bfloat16
F32 = jnp.float32
HIGH = lax.Precision.HIGHEST


def mm(a, b):
    return jnp.dot(a, b, preferred_element_type=F32)


def mm_nt(a, b):
    return lax.dot_general(a, b, (((1,), (1,)), ((), ())), preferred_element_type=F32)


def split_lanes(v):
    lane = lax.broadcasted_iota(jnp.int32, v.shape, 1)
    high = v.astype(BF).astype(F32)
    return jnp.where(lane < 32, high, v - high).astype(BF)


def halves(v):
    high = v.astype(BF)
    return high, (v - high.astype(F32)).astype(BF)


def block_diag(v):
    lane = lax.broadcasted_iota(jnp.int32, v.shape, 1)
    zero = jnp.zeros_like(v)
    return jnp.concatenate([jnp.where(lane < WIDTH, v, zero), jnp.where(lane >= WIDTH, v, zero)], axis=0)


def softplus(v):
    return jnp.maximum(v, 0.0) + jnp.log1p(jnp.exp(-jnp.abs(v)))


def sigmoid(v):
    return 0.5 * jnp.tanh(0.5 * v) + 0.5


def repeat_heads(raw):
    lane = lax.broadcasted_iota(jnp.int32, raw.shape, 1)
    once = jnp.where(lane < 32, raw, 0.0)
    twice = once + pltpu.roll(once, 32, 1)
    return twice + pltpu.roll(twice, 64, 1)


def head_values(raw, col, hp_ref, ee_ref, at_ref, dtx_ref, esx_ref, tex_ref, keepx_ref):
    span = raw.shape[0]
    shifted = repeat_heads(raw) + hp_ref[0:1, :]
    dt = softplus(shifted)
    rates = hp_ref[1:2, :] * dt
    row = lax.broadcasted_iota(jnp.int32, (span, span), 0)
    column = lax.broadcasted_iota(jnp.int32, (span, span), 1)
    tri = jnp.where(row >= column, 1.0, 0.0).astype(F32)
    total = jnp.dot(tri, rates, precision=HIGH, preferred_element_type=F32)
    at_ref[...] = total.T
    last = total[span - 1 : span, :]
    ee = ee_ref[...]
    dtx_ref[...] = mm(split_lanes(dt), ee)
    esx_ref[...] = mm(split_lanes(jnp.exp(total) * col[:, 7:8]), ee)
    tex_ref[...] = mm(split_lanes(jnp.exp(last - total) * col[:, 8:9]), ee)
    keepx_ref[...] = mm(split_lanes(jnp.broadcast_to(jnp.exp(last) * col[0:1, 9:10], (8, LANES))), ee)
    return shifted, rates, total


def pair_decay(pair, total, at_ref):
    span = total.shape[0]
    heads = (2 * pair, 2 * pair + 1)
    column = jnp.concatenate([jnp.broadcast_to(total[:, h : h + 1], (span, span)) for h in heads], axis=1)
    row = jnp.concatenate([at_ref[h : h + 1, :] for h in heads], axis=1)
    return column, row


def fwd_kernel(
    inner,
    xbc_ref, col_ref, row_ref, cw_ref, hp_ref, skip_ref, ee_ref,
    y_ref, pre_ref, sin_ref,
    buf, state, at_ref, dtx_ref, esx_ref, tex_ref, keepx_ref, g2_ref,
):
    span = y_ref.shape[0]
    mixed = pre_ref.shape[1]
    step = pl.program_id(0)

    @pl.when(step == 0)
    def _():
        buf[0:8, :] = jnp.zeros((8, mixed), F32)
        state[...] = jnp.zeros_like(state)

    @pl.when(step > 0)
    def _():
        buf[0:8, :] = buf[span : span + 8, :]

    buf[8 : 8 + span, :] = xbc_ref[:, :mixed]
    col = col_ref[...]
    _, _, total = head_values(
        xbc_ref[:, mixed : mixed + LANES], col, hp_ref, ee_ref, at_ref, dtx_ref, esx_ref, tex_ref, keepx_ref
    )
    same = [None] + [jnp.broadcast_to(col[:, k : k + 1], (span, LANES)) for k in (1, 2, 3)]

    def conv(lanes):
        pre = cw_ref[4:5, lanes] + cw_ref[3:4, lanes] * buf[8 : 8 + span, lanes]
        for k in (1, 2, 3):
            pre = pre + cw_ref[3 - k : 4 - k, lanes] * (buf[8 - k : 8 - k + span, lanes] * same[k])
        pre_ref[:, lanes] = pre
        return pre * sigmoid(pre)

    b_f = conv(slice(inner, inner + LANES))
    c_b = conv(slice(inner + LANES, inner + 2 * LANES)).astype(BF)
    b_b = b_f.astype(BF)
    b_t = b_f.T.astype(BF)
    t_index = lax.broadcasted_iota(jnp.int32, (span, span), 0)
    s_index = lax.broadcasted_iota(jnp.int32, (span, span), 1)
    linked = (t_index >= s_index) & (col[:, 0:1] == row_ref[0:1, :])
    inter = jnp.where(linked, mm_nt(c_b, b_b), 0.0)
    g2_ref[...] = jnp.concatenate([inter, inter], axis=1)

    def pair_step(pair):
        lanes = slice(pair * LANES, (pair + 1) * LANES)
        x = conv(lanes)
        xd = x * dtx_ref[:, lanes]
        column, row = pair_decay(pair, total, at_ref)
        decay = jnp.exp(jnp.minimum(column - row, 0.0))
        inside = mm((g2_ref[...] * decay).astype(BF), block_diag(xd.astype(BF)))
        held = state[:, lanes]
        held_b = held.astype(BF)
        sin_ref[:, lanes] = held_b
        y_ref[:, lanes] = inside + mm(c_b, held_b) * esx_ref[:, lanes] + skip_ref[0:1, lanes] * x
        state[:, lanes] = held * keepx_ref[0:1, lanes] + mm(b_t, (xd * tex_ref[:, lanes]).astype(BF))

    for pair in range(inner // LANES):
        pair_step(pair)


def bwd_kernel(
    inner,
    xbc_ref, pre_ref, y_ref, gy_ref, sin_ref, col_ref, row_ref, cw_ref, hp_ref, skip_ref, ee_ref, rt_ref,
    gp_ref, cwg_ref, hpg_ref, skg_ref,
    grad, halo, gstate, at_ref, dtx_ref, esx_ref, tex_ref, keepx_ref, gt2_ref, ggt_ref, gb_ref, gc_ref, acc_ref, kv_ref,
):
    span = y_ref.shape[0]
    mixed = pre_ref.shape[1]
    step = pl.program_id(0)

    @pl.when(step == 0)
    def _():
        halo[...] = jnp.zeros_like(halo)
        gstate[...] = jnp.zeros_like(gstate)
        cwg_ref[...] = jnp.zeros_like(cwg_ref)
        hpg_ref[...] = jnp.zeros_like(hpg_ref)
        skg_ref[...] = jnp.zeros_like(skg_ref)

    col = col_ref[...]
    shifted, rates, total = head_values(
        xbc_ref[:, mixed : mixed + LANES], col, hp_ref, ee_ref, at_ref, dtx_ref, esx_ref, tex_ref, keepx_ref
    )
    ahead = [None] + [jnp.broadcast_to(col[:, 3 + k : 4 + k], (span, LANES)) for k in (1, 2, 3)]

    def conv_back(lanes, g):
        grad[0:span, lanes] = g
        grad[span : span + 8, lanes] = halo[:, lanes]
        halo[:, lanes] = g[0:8, :]
        xin = xbc_ref[:, lanes]
        back = cw_ref[3:4, lanes] * g
        cwg_ref[3:4, lanes] += jnp.sum(xin * g, axis=0, keepdims=True)
        cwg_ref[4:5, lanes] += jnp.sum(g, axis=0, keepdims=True)
        for k in (1, 2, 3):
            moved = grad[k : k + span, lanes] * ahead[k]
            back = back + cw_ref[3 - k : 4 - k, lanes] * moved
            cwg_ref[3 - k : 4 - k, lanes] += jnp.sum(xin * moved, axis=0, keepdims=True)
        gp_ref[:, lanes] = back.astype(BF)

    def act(lanes):
        pre = pre_ref[:, lanes]
        sig = sigmoid(pre)
        return pre * sig, sig * (1.0 + pre * (1.0 - sig))

    b_lanes, c_lanes = slice(inner, inner + LANES), slice(inner + LANES, inner + 2 * LANES)
    b_f, b_slope = act(b_lanes)
    c_f, c_slope = act(c_lanes)
    b_b, c_b = b_f.astype(BF), c_f.astype(BF)
    c_t = c_f.T.astype(BF)
    s_index = lax.broadcasted_iota(jnp.int32, (span, span), 0)
    t_index = lax.broadcasted_iota(jnp.int32, (span, span), 1)
    linked = (t_index >= s_index) & (col[:, 0:1] == row_ref[0:1, :])
    inter = jnp.where(linked, mm_nt(b_b, c_b), 0.0)
    gt2_ref[...] = jnp.concatenate([inter, inter], axis=1)
    ggt_ref[...] = jnp.zeros_like(ggt_ref)
    gb_ref[...] = jnp.zeros_like(gb_ref)
    gc_ref[...] = jnp.zeros_like(gc_ref)
    acc_ref[...] = jnp.zeros_like(acc_ref)

    def pair_step(pair):
        lanes = slice(pair * LANES, (pair + 1) * LANES)
        x, slope = act(lanes)
        dtx, tex = dtx_ref[:, lanes], tex_ref[:, lanes]
        xd = x * dtx
        xd_b = xd.astype(BF)
        gy_b = gy_ref[:, lanes]
        gy = gy_b.astype(F32)
        diag = block_diag(gy_b)
        column, row = pair_decay(pair, total, at_ref)
        decay = jnp.exp(jnp.minimum(row - column, 0.0))
        linked_g = mm_nt(xd_b, diag) * decay
        ggt_ref[...] += linked_g[:, :span] + linked_g[:, span:]
        gx_in = mm((gt2_ref[...] * decay).astype(BF), diag)
        gs = gstate[:, lanes]
        gs_b = gs.astype(BF)
        gx_state = tex * mm(b_b, gs_b)
        gxd = gx_in + gx_state
        from_state = xd * gx_state
        skip = skip_ref[0:1, lanes]
        drift = gy * (y_ref[:, lanes] - skip * x) - xd_b.astype(F32) * gx_in - from_state
        parts = [halves(v) for v in (drift, from_state, x * gxd)]
        stacked = jnp.concatenate([jnp.concatenate(part, axis=1) for part in parts], axis=0)
        rt = rt_ref[lanes, :]
        acc_ref[...] += mm(stacked, jnp.concatenate([rt, rt], axis=0))
        skg_ref[0:1, lanes] += jnp.sum(gy * x, axis=0, keepdims=True)
        held_b = sin_ref[:, lanes]
        keepx = keepx_ref[0:1, lanes]
        kv_ref[0:1, lanes] = keepx * jnp.sum(held_b.astype(F32) * gs, axis=0, keepdims=True)
        scaled = (esx_ref[:, lanes] * gy).astype(BF)
        gc_ref[...] += mm_nt(scaled, held_b)
        gb_ref[...] += mm_nt((xd * tex).astype(BF), gs_b)
        gstate[:, lanes] = keepx * gs + mm(c_t, scaled)
        conv_back(lanes, (dtx * gxd + skip * gy) * slope)

    kv_ref[...] = jnp.zeros_like(kv_ref)
    for pair in range(inner // LANES):
        pair_step(pair)
    g_inter = jnp.where(linked, ggt_ref[...], 0.0)
    conv_back(b_lanes, (gb_ref[...] + mm(g_inter.astype(BF), c_b)) * b_slope)
    conv_back(c_lanes, (gc_ref[...] + mm(g_inter.T.astype(BF), b_b)) * c_slope)
    kv_high, kv_low = halves(kv_ref[...])
    rt = rt_ref[...]
    kept = mm(kv_high, rt) + mm(kv_low, rt)
    at_end = jnp.sum(acc_ref[span : 2 * span, :], axis=0, keepdims=True) + kept[0:1, :]
    tri = jnp.where(t_index >= s_index, 1.0, 0.0).astype(F32)
    g_rate = jnp.dot(tri, acc_ref[0:span, :], precision=HIGH, preferred_element_type=F32) + at_end
    g_raw = (acc_ref[2 * span : 3 * span, :] + hp_ref[1:2, :] * g_rate) * sigmoid(shifted)
    gp_ref[:, mixed : mixed + LANES] = g_raw.astype(BF)
    hpg_ref[0:1, :] += jnp.sum(g_raw, axis=0, keepdims=True)
    hpg_ref[1:2, :] += jnp.sum(rates * g_rate, axis=0, keepdims=True)


def z_weight(zo_refs, lanes):
    shards, rows, width = zo_refs[0].shape
    half, side = rows // 4, lanes.start // width
    columns = slice(lanes.start - side * width, lanes.stop - side * width)
    parts = [ref[:, side * half : (side + 1) * half, columns] for ref in zo_refs]
    return jnp.stack(parts, axis=1).reshape(2 * shards * half, columns.stop - columns.start)


def out_weight_rows(zo_refs, lanes):
    shards, rows, width = zo_refs[0].shape
    parts = [ref[lanes.start // rows : lanes.stop // rows, rows // 2 :, :] for ref in zo_refs]
    return jnp.stack(parts, axis=1).reshape(lanes.stop - lanes.start, width)


def in_core_order(core_ref, mine_ref, other_ref, body):
    @pl.when(core_ref[0] == 0)
    def _():
        body((mine_ref, other_ref))

    @pl.when(core_ref[0] != 0)
    def _():
        body((other_ref, mine_ref))


def gate_kernel(core_ref, y_ref, normed_ref, dy_ref, mine_ref, other_ref, *refs):
    @pl.when(pl.program_id(0) == 0)
    def _():
        refs[4][...] = jnp.zeros_like(refs[4])

    in_core_order(
        core_ref, mine_ref, other_ref, lambda zo: gate_body(y_ref, normed_ref, dy_ref, zo, *refs)
    )


def gate_body(y_ref, normed_ref, dy_ref, zo, gain_ref, out_ref, gy_ref, gz_ref, gg_ref, z_ref, gm_ref):
    rows, inner = y_ref.shape

    pieces = [slice(k, k + 2 * LANES) for k in range(0, inner, 2 * LANES)]
    square = jnp.zeros((rows, 2 * LANES), F32)
    cross = jnp.zeros((rows, 2 * LANES), F32)
    normed, dy = normed_ref[...], dy_ref[...]
    for lanes in pieces:
        z = mm(normed, z_weight(zo, lanes))
        gm = mm_nt(dy, out_weight_rows(zo, lanes))
        z_ref[:, lanes] = z
        gm_ref[:, lanes] = gm
        gated = y_ref[:, lanes] * (z * sigmoid(z))
        square = square + gated * gated
        cross = cross + gated * (gm * gain_ref[0:1, lanes])
    inv = lax.rsqrt(jnp.sum(square, axis=1, keepdims=True) / inner + EPS)
    pull = inv * inv * inv * (jnp.sum(cross, axis=1, keepdims=True) / inner)
    for lanes in pieces:
        z, y, gm = z_ref[:, lanes], y_ref[:, lanes], gm_ref[:, lanes]
        sig = sigmoid(z)
        silu = z * sig
        gated = y * silu
        gain = gain_ref[0:1, lanes]
        unit = gated * inv
        out_ref[:, lanes] = (unit * gain).astype(BF)
        gg_ref[0:1, lanes] += jnp.sum(gm * unit, axis=0, keepdims=True)
        g_gated = inv * (gm * gain) - gated * pull
        gy_ref[:, lanes] = (g_gated * silu).astype(BF)
        gz_ref[:, lanes] = (g_gated * y * (sig + silu * (1.0 - sig))).astype(BF)


def full(shape):
    return pl.BlockSpec(shape, lambda i: (0,) * len(shape))


def onehots(inner):
    heads = inner // WIDTH
    owner = np.arange(inner) // WIDTH
    spread = np.zeros((LANES, inner), np.float32)
    spread[owner, np.arange(inner)] = 1
    spread[32 + owner, np.arange(inner)] = 1
    collect = np.zeros((inner, LANES), np.float32)
    collect[np.arange(inner), owner] = 1
    return jnp.asarray(spread, BF), jnp.asarray(collect, BF)


PARAMS = pltpu.CompilerParams(dimension_semantics=("arbitrary",), vmem_limit_bytes=52 * 2**20)


def common_scratch(inner):
    return [
        pltpu.VMEM((LANES, SPAN), F32),
        pltpu.VMEM((SPAN, inner), F32),
        pltpu.VMEM((SPAN, inner), F32),
        pltpu.VMEM((SPAN, inner), F32),
        pltpu.VMEM((8, inner), F32),
        pltpu.VMEM((SPAN, 2 * SPAN), F32),
    ]


def scan_forward(xbc, col, row, cw, hp, skip):
    length, mixed, inner = xbc.shape[0], cw.shape[1], skip.shape[1]
    spread, _ = onehots(inner)
    blocks = length // SPAN
    return pl.pallas_call(
        partial(fwd_kernel, inner),
        grid=(blocks,),
        in_specs=[
            pl.BlockSpec((SPAN, mixed + LANES), lambda i: (i, 0)),
            pl.BlockSpec((SPAN, 16), lambda i: (i, 0)),
            pl.BlockSpec((8, SPAN), lambda i: (0, i)),
            full((8, mixed)), full((8, LANES)), full((8, inner)), full((LANES, inner)),
        ],
        out_specs=[
            pl.BlockSpec((SPAN, inner), lambda i: (i, 0)),
            pl.BlockSpec((SPAN, mixed), lambda i: (i, 0)),
            pl.BlockSpec((LANES, inner), lambda i: (i, 0)),
        ],
        out_shape=[
            jax.ShapeDtypeStruct((length, inner), F32),
            jax.ShapeDtypeStruct((length, mixed), F32),
            jax.ShapeDtypeStruct((blocks * LANES, inner), BF),
        ],
        scratch_shapes=[pltpu.VMEM((SPAN + 8, mixed), F32), pltpu.VMEM((LANES, inner), F32)] + common_scratch(inner),
        compiler_params=PARAMS,
        cost_estimate=pl.CostEstimate(flops=6 * 10**9, bytes_accessed=3 * 10**7, transcendentals=10**7),
        name="scan_forward",
    )(xbc, col, row, cw, hp, skip, spread)


def scan_backward(xbc, pre, y, gy, sin, col, row, cw, hp, skip):
    length, mixed, inner = xbc.shape[0], cw.shape[1], skip.shape[1]
    spread, collect = onehots(inner)
    blocks = length // SPAN
    rev = lambda i: (blocks - 1 - i, 0)
    return pl.pallas_call(
        partial(bwd_kernel, inner),
        grid=(blocks,),
        in_specs=[
            pl.BlockSpec((SPAN, mixed + LANES), rev),
            pl.BlockSpec((SPAN, mixed), rev),
            pl.BlockSpec((SPAN, inner), rev),
            pl.BlockSpec((SPAN, inner), rev),
            pl.BlockSpec((LANES, inner), rev),
            pl.BlockSpec((SPAN, 16), rev),
            pl.BlockSpec((8, SPAN), lambda i: (0, blocks - 1 - i)),
            full((8, mixed)), full((8, LANES)), full((8, inner)), full((LANES, inner)), full((inner, LANES)),
        ],
        out_specs=[
            pl.BlockSpec((SPAN, mixed + LANES), rev),
            full((8, mixed)), full((8, LANES)), full((8, inner)),
        ],
        out_shape=[
            jax.ShapeDtypeStruct((length, mixed + LANES), BF),
            jax.ShapeDtypeStruct((8, mixed), F32),
            jax.ShapeDtypeStruct((8, LANES), F32),
            jax.ShapeDtypeStruct((8, inner), F32),
        ],
        scratch_shapes=[
            pltpu.VMEM((SPAN + 8, mixed), F32), pltpu.VMEM((8, mixed), F32), pltpu.VMEM((LANES, inner), F32),
        ] + common_scratch(inner) + [
            pltpu.VMEM((SPAN, SPAN), F32), pltpu.VMEM((SPAN, LANES), F32), pltpu.VMEM((SPAN, LANES), F32),
            pltpu.VMEM((3 * SPAN, LANES), F32), pltpu.VMEM((8, inner), F32),
        ],
        compiler_params=PARAMS,
        cost_estimate=pl.CostEstimate(flops=2 * 10**10, bytes_accessed=5 * 10**7, transcendentals=10**7),
        name="scan_backward",
    )(xbc, pre, y, gy, sin, col, row, cw, hp, skip, spread, collect)


def gate(core, y, normed, dy, zo, gain):
    length, inner = y.shape
    width = normed.shape[1]
    rows = 256
    block = lambda columns: pl.BlockSpec((rows, columns), lambda i: (i, 0))
    return pl.pallas_call(
        gate_kernel,
        grid=(length // rows,),
        in_specs=[
            pl.BlockSpec(memory_space=pltpu.SMEM),
            block(inner), block(width), block(width), full(zo[0].shape), full(zo[1].shape), full((8, inner)),
        ],
        out_specs=[block(inner), block(inner), block(inner), full((8, inner))],
        out_shape=[jax.ShapeDtypeStruct((length, inner), BF)] * 3 + [jax.ShapeDtypeStruct((8, inner), F32)],
        scratch_shapes=[pltpu.VMEM((rows, inner), F32), pltpu.VMEM((rows, inner), F32)],
        compiler_params=PARAMS,
        cost_estimate=pl.CostEstimate(flops=9 * 10**9, bytes_accessed=4 * 10**7, transcendentals=4 * 10**6),
        name="gate",
    )(core, y, normed, dy, *zo, gain)


def input_kernel(core_ref, tokens_ref, dy_ref, gz_ref, gp_ref, mixed_ref, mine_ref, other_ref, *refs):
    in_core_order(
        core_ref,
        mine_ref,
        other_ref,
        lambda zo: input_body(tokens_ref, dy_ref, gz_ref, gp_ref, mixed_ref, zo, *refs),
    )


def input_body(tokens_ref, dy_ref, gz_ref, gp_ref, mixed_ref, zo, wx_ref, gain_ref, grad_ref, out_ref):
    width, inner = tokens_ref.shape[1], gz_ref.shape[1]
    g_normed = mm_nt(gp_ref[...], wx_ref[...])
    for k in range(0, inner, width):
        lanes = slice(k, k + width)
        g_normed = g_normed + mm_nt(gz_ref[:, lanes], z_weight(zo, lanes))
    inputs = tokens_ref[...].astype(F32)
    inv = lax.rsqrt(jnp.mean(inputs * inputs, axis=1, keepdims=True) + EPS)
    unit = inputs * inv
    scaled = g_normed * gain_ref[0:1, :]
    pull = jnp.mean(scaled * unit, axis=1, keepdims=True)
    grad_ref[...] = (dy_ref[...].astype(F32) + inv * (scaled - unit * pull)).astype(BF)
    total = inputs
    for k in range(0, inner, 2 * LANES):
        lanes = slice(k, k + 2 * LANES)
        total = total + mm(mixed_ref[:, lanes], out_weight_rows(zo, lanes))
    out_ref[...] = total.astype(BF)


def input_gradient(core, tokens, dy, gz, gp, mixed_out, zo, w_x, gain):
    length, width = tokens.shape
    rows = 256
    block = lambda v: pl.BlockSpec((rows, v.shape[1]), lambda i: (i, 0))
    return pl.pallas_call(
        input_kernel,
        grid=(length // rows,),
        in_specs=[pl.BlockSpec(memory_space=pltpu.SMEM)]
        + [block(v) for v in (tokens, dy, gz, gp, mixed_out)] + [full(v.shape) for v in (*zo, w_x, gain)],
        out_specs=[block(tokens)] * 2,
        out_shape=[jax.ShapeDtypeStruct((length, width), BF)] * 2,
        compiler_params=PARAMS,
        cost_estimate=pl.CostEstimate(flops=10**7, bytes_accessed=10**5, transcendentals=0),
        name="input_gradient",
    )(core, tokens, dy, gz, gp, mixed_out, *zo, w_x, gain)


def document_info(resets):
    length = resets.shape[0]
    segment = jnp.cumsum(resets).astype(jnp.int32)
    back = [jnp.pad(segment, (k, 0), constant_values=-1)[:length] == segment for k in (1, 2, 3)]
    ahead = [jnp.pad(segment, (0, k), constant_values=-1)[k:] == segment for k in (1, 2, 3)]
    last = segment.reshape(-1, SPAN)[:, -1]
    before = jnp.concatenate([jnp.full((1,), -1, jnp.int32), last[:-1]])
    last, before = jnp.repeat(last, SPAN), jnp.repeat(before, SPAN)
    columns = [segment] + back + ahead + [segment == before, segment == last, last == before]
    columns = columns + [jnp.zeros_like(segment)] * (16 - len(columns))
    col = jnp.stack([c.astype(F32) for c in columns], axis=1)
    row = jnp.broadcast_to(segment.astype(F32)[None, :], (8, length))
    return col, row


def rows8(*rows):
    width = rows[0].shape[-1]
    rows = [r.reshape(-1, width).astype(F32) for r in rows]
    have = sum(r.shape[0] for r in rows)
    return jnp.concatenate(rows + [jnp.zeros((8 - have, width), F32)], axis=0)


def pairs(size, flip):
    return [(i, i ^ flip) for i in range(size)]


def other_core(value, reps):
    return lax.ppermute(value, "rep", pairs(reps, 1))


def swap_halves(own, core, reps, axis):
    other = other_core(own, reps)
    first = core == 0
    return jnp.stack([jnp.where(first, own, other), jnp.where(first, other, own)], axis=axis)


def half_of(value, core, axis):
    pick = lambda k: lax.dynamic_index_in_dim(value, k, axis, keepdims=False)
    return pick(core), pick(1 - core)


def sum_cores(value, core, reps):
    mine, theirs = half_of(value, core, 1)
    return (mine.astype(F32) + other_core(theirs, reps).astype(F32)).astype(BF)


def sum_reps(value, reps, flip=2):
    while flip < reps:
        value = add(value, lax.ppermute(value, "rep", pairs(reps, flip)))
        flip *= 2
    return value


def gather_shards(value, small, shards):
    if shards != 8:
        return lax.all_gather(value, "shard", axis=0), lax.all_gather(small, "shard", axis=0), value
    member = lax.axis_index("shard")
    z, y = member // 2, member % 2

    def from_behind(block, k):
        return lax.ppermute(block, "shard", [(i, (i + 2 * k) % 8) for i in range(8)])

    got = [(0, value)] + [(k, from_behind(value, k)) for k in (1, 3, 2)]
    other = lax.ppermute(small, "shard", pairs(8, 1))
    pair = jnp.stack([jnp.where(y == 0, small, other), jnp.where(y == 0, other, small)])
    places = jnp.stack([pair] + [from_behind(pair, k) for k in (1, 2, 3)])
    small_all = jnp.take(places, (z - jnp.arange(4)) % 4, axis=0).reshape((8,) + small.shape)
    blank, arrived = lax.optimization_barrier((jnp.zeros((), value.dtype), got[1][1]))
    got[1] = (1, arrived)
    out = jnp.broadcast_to(blank, (4, 2) + value.shape)
    start = (0,) * value.ndim
    for k, block in got:
        across = lax.ppermute(block, "shard", pairs(8, 1))
        at = (z - k) % 4
        out = lax.dynamic_update_slice(out, block[None, None], (at, y) + start)
        out = lax.dynamic_update_slice(out, across[None, None], (at, 1 - y) + start)
        if k == 3:
            out, small_all = lax.optimization_barrier((out, small_all))
    return out.reshape((8,) + value.shape), small_all, arrived


def along_z(value, z):
    own = lax.dynamic_index_in_dim(value, z, 0, keepdims=False)
    got = []
    for k in (1, 3, 2):
        entry = lax.dynamic_index_in_dim(value, (z + k) % 4, 0, keepdims=False)
        got.append(lax.ppermute(entry, "shard", [(i, (i + 2 * k) % 8) for i in range(8)]))
    return [own] + got


def along_y(value, y, axis):
    mine, theirs = half_of(value, y, axis)
    return [mine, lax.ppermute(theirs, "shard", pairs(8, 1))]


def add(*values):
    return sum(v.astype(F32) for v in values).astype(values[0].dtype)


def scatter_shards(first, second, shards, during):
    if shards != 8:
        first, second = during(0, (first, second))
        return during(1, tuple(lax.psum_scatter(v, "shard", scatter_dimension=0) for v in (first, second)))
    member = lax.axis_index("shard")
    z, y = member // 2, member % 2
    first = along_y(first.reshape((4, 2) + first.shape[1:]), y, 1)
    second = along_z(second.reshape((4, 2) + second.shape[1:]), z)
    first, second = during(0, (first, second))
    first = along_z(add(*first), z)
    second = along_y(add(*second), y, 0)
    first, second = during(1, (first, second))
    return add(*first), add(*second)


def on_device(reps, shards, *args):
    (tokens, resets, norm_gain, in_weight, conv_weight, conv_bias, step_bias, decay_log, skip_gain, gate_gain,
     out_weight, cotangent) = args
    rows = in_weight.shape[0]
    width = tokens.shape[1]
    inner = shards * gate_gain.shape[0]
    mixed = shards * conv_bias.shape[0]
    heads = shards * step_bias.shape[0]
    half = rows // 2
    core = lax.axis_index("rep") % 2
    barrier = lax.optimization_barrier

    small_parts = (norm_gain, conv_weight, conv_bias, step_bias, decay_log, skip_gain, gate_gain)
    small = jnp.concatenate([v.reshape(-1) for v in small_parts])
    small = jnp.pad(small, (0, -small.shape[0] % 1024)).reshape(-1, 1024)
    own_rows = lax.dynamic_slice_in_dim(in_weight, core * half, half, 0)
    x_all, small_all, arrived = gather_shards(jnp.pad(own_rows[:, inner:], ((0, 0), (0, LANES - heads))), small, shards)
    w_x = swap_halves(x_all, core, reps, 1).reshape(width, mixed + LANES)
    small_all = small_all.reshape(shards, -1).astype(F32)
    out_own = lax.dynamic_slice_in_dim(out_weight, core * 2 * half, 2 * half, 0)
    zo_own = jnp.concatenate([own_rows[:, :width], own_rows[:, width:inner], out_own], axis=0)
    zo_own, _ = barrier((zo_own, arrived))
    zo_all = lax.all_gather(zo_own, "shard", axis=0)

    full_small, at = [], 0
    for part in small_parts:
        piece = small_all[:, at : at + part.size]
        at += part.size
        if part.ndim == 2:
            piece = jnp.moveaxis(piece.reshape(shards, part.shape[0], part.shape[1]), 0, 1).reshape(part.shape[0], -1)
        else:
            piece = piece.reshape(-1)
        full_small.append(piece)
    gain, cw, cb, sb, dl, sk, gg = full_small
    repeat = LANES // heads
    cw8 = rows8(cw, cb)
    hp8 = rows8(jnp.tile(sb, repeat), jnp.tile(-jnp.exp(dl), repeat))
    sk8 = rows8(jnp.repeat(sk, WIDTH))
    gg8 = rows8(gg)

    col, row = document_info(resets)
    inputs = tokens.astype(F32)
    inv_rms = lax.rsqrt(jnp.mean(inputs * inputs, axis=-1, keepdims=True) + EPS)
    normed = (inputs * inv_rms * gain[None, :]).astype(BF)
    xbc = mm(normed, w_x)
    y, pre, sin = scan_forward(xbc, col, row, cw8, hp8, sk8)
    zo_all, y = barrier((zo_all, y))
    zo = (zo_all, other_core(zo_all, reps))
    core_at = jnp.reshape(core, (1,))
    mixed_out, gy, gz, gg_grad = gate(core_at, y, normed, cotangent, zo, gg8)

    def grad_of(left, right):
        return lax.dot_general(left, right, (((0,), (0,)), ((), ())), preferred_element_type=F32).astype(BF)

    out_grad = sum_cores(grad_of(mixed_out, cotangent).reshape(shards, 2, 2 * half, width), core, reps)
    z_grad = sum_cores(grad_of(normed, gz).reshape(shards, 2, half, inner), core, reps)
    zo_sum = jnp.concatenate([z_grad[:, :, :width], z_grad[:, :, width:], out_grad], axis=1)
    zo_sum, gy = barrier((zo_sum, gy))
    zo_own = lax.psum_scatter(zo_sum, "shard", scatter_dimension=0)
    gp, cwg, hpg, skg = scan_backward(xbc, pre, y, gy, sin, col, row, cw8, hp8, sk8)
    cut = (mixed + 2 * LANES) // (2 * LANES) * LANES
    x_grad = grad_of(normed, gp).reshape(shards, 2, half, mixed + LANES)
    x_mine, x_theirs = half_of(x_grad, core, 1)
    x_theirs = other_core(x_theirs, reps)
    x_sums = [add(x_mine[:, :, s], x_theirs[:, :, s]) for s in (slice(0, cut), slice(cut, mixed + LANES))]
    x_sums, gp = barrier((x_sums, gp))
    input_grad, output = input_gradient(core_at, tokens, cotangent, gz, gp, mixed_out, zo, w_x, rows8(gain))

    grads = (cwg[:4], cwg[4], hpg[0, :heads], hpg[1, :heads], skg[0].reshape(heads, WIDTH).sum(axis=1), gg_grad[0])
    split = lambda v: jnp.moveaxis(v.reshape(v.shape[:-1] + (shards, -1)), -2, 0).reshape(shards, -1)
    own = jnp.concatenate([split(v) for v in grads], axis=1)
    own = own + other_core(own, reps)
    member = lax.axis_index("shard")
    z_at, y_at = member // 2, member % 2
    staged = shards == 8 and reps > 2
    if staged:
        own = along_y(own.reshape(4, 2, -1), y_at, 1)
    else:
        own = lax.psum_scatter(own, "shard", scatter_dimension=0)

    def during(stage, value):
        nonlocal input_grad, output, zo_own, own
        if stage == 0:
            value, input_grad, output, zo_own, own = barrier((value, input_grad, output, zo_own, own))
            if staged:
                zo_own = [zo_own, lax.ppermute(zo_own, "rep", pairs(reps, 2))]
                own = along_z(add(*own), z_at)
        elif staged:
            value, zo_own, own = barrier((value, zo_own, own))
            zo_own, own = add(*zo_own), add(*own)
        return value

    x_parts = scatter_shards(*x_sums, shards, during)
    zo_own = swap_halves(sum_reps(zo_own, reps, 4 if staged else 2), core, reps, 0).astype(F32)
    own = sum_reps(own, reps)
    x_own = swap_halves(sum_reps(jnp.concatenate(x_parts, axis=1), reps), core, reps, 0).astype(F32)
    small_grads, at = [], 0
    for part in small_parts[1:]:
        small_grads.append(own[at : at + part.size].reshape(part.shape))
        at += part.size

    out_part = zo_own[:, 2 * half :].reshape(out_weight.shape)
    in_grad = jnp.concatenate(
        [
            zo_own[:, :half].reshape(rows, width),
            zo_own[:, half : 2 * half].reshape(rows, width),
            x_own.reshape(rows, -1)[:, : mixed + heads],
        ],
        axis=1,
    )
    gain_grad = jnp.sum(in_weight.astype(F32) * in_grad, axis=1) / norm_gain.astype(F32)
    return (output, input_grad, gain_grad, in_grad, *small_grads, out_part)


def solution(mesh):
    by_token, by_shard = P(("rep", "shard"), None), P("shard")
    in_specs = (
        by_token, P(("rep", "shard")), by_shard, P("shard", None), P(None, "shard"), by_shard, by_shard, by_shard,
        by_shard, by_shard, P("shard", None), by_token,
    )
    out_specs = (
        by_token, by_token, by_shard, P("shard", None), P(None, "shard"), by_shard, by_shard, by_shard, by_shard,
        by_shard, P("shard", None),
    )
    return jax.shard_map(
        partial(on_device, mesh.shape["rep"], mesh.shape["shard"]),
        mesh=mesh,
        in_specs=in_specs,
        out_specs=out_specs,
        check_vma=False,
    )
```
